128 devices in a mesh: dp: 16 (over y, x), seq: 8 (over z, core).
Axes of the slice: x: 4, y: 4, z: 4, core: 2. Of those that a mesh axis runs over, the one named last changes fastest.
Arguments:
- frames: bfloat16 [16, 6144, 1024], P('dp', 'seq'), may hold values from -6 to 6
- cotangent: bfloat16 [16, 6144, 1024], P('dp', 'seq'), may hold values from -6 to 6
- segments: int32 [16, 6144], P('dp', 'seq'), may hold values from 0 to 95, never falling along the last dimension, each value on 1 to 128 neighbouring positions
- w_in: bfloat16 [1024, 2048], P(('dp', 'seq')), may hold values from -0.1875 to 0.1875
- w_out: bfloat16 [1024, 1024], P(('dp', 'seq')), may hold values from -0.1875 to 0.1875
- kernel: bfloat16 [1024, 31], P(('dp', 'seq')), may hold values from -1 to 1
- gain_in: bfloat16 [1024], P(('dp', 'seq')), may hold values from 0.099609375 to 1.8984375
- gain_mid: bfloat16 [1024], P(('dp', 'seq')), may hold values from 0.099609375 to 1.8984375
Outputs:
- block_out: bfloat16 [16, 6144, 1024], P('dp', 'seq')
- input_grad: bfloat16 [16, 6144, 1024], P('dp', 'seq')
- grad_w_in: float32 [1024, 2048], P(('dp', 'seq'))
- grad_w_out: float32 [1024, 1024], P(('dp', 'seq'))
- grad_kernel: float32 [1024, 31], P(('dp', 'seq'))
- grad_gain_in: float32 [1024], P(('dp', 'seq'))
- grad_gain_mid: float32 [1024], P(('dp', 'seq'))
The draws below stay inside these ranges and needn't reach their ends.
Inputs may be any that keep to these rules, and one draw needn't show every extreme that they name: `segments`: along each recording the ids never fall; each utterance holds 1 to 128 frames, and one holds exactly 128.
All inputs are finite; a program needn't handle non-finite values.
Results may differ from the reference program's by a relative error of at most 0.013.
Values may be sent and summed in bfloat16 or wider, within the bound.
A program may use at most 128 MiB of HBM per device.

```python
import math
import jax
import jax.numpy as jnp
import numpy as np
from jax import lax

D = 1024
KW = 31
SEQ_ROWS = 6144
FRAMES = 98304
UTTERANCES = 96
N_DP = 16


def shard_levels(rng, dims, split, least, top_value):
    loudness = 1.0
    for axis_at, parts in split:
        draws = jax.random.uniform(jax.random.fold_in(jax.random.fold_in(rng, 6), axis_at), (parts,), jnp.float32, least / len(split), top_value / len(split))
        loudness = loudness * jnp.repeat(jnp.exp(draws), dims[axis_at] // parts).reshape((-1,) + (1,) * (len(dims) - 1 - axis_at))
    return loudness


def split_up(number_of, total, bound, lean):
    portions = [(1 << 20) // math.isqrt(grade ** lean) + 1 for grade in range(2, number_of + 1)]
    surplus, holding = total - bound - (number_of - 1), [1] * (number_of - 1)
    while surplus > 0:
        free = [i for i in range(number_of - 1) if holding[i] < bound]
        pool, budget = sum([portions[i] for i in free]), surplus
        for i in free:
            more = min(bound - holding[i], max(1, budget * portions[i] // pool), surplus)
            holding[i] = holding[i] + more
            surplus = surplus - more
    return np.array([bound] + holding)


def uneven_parts(key, count, total, reach, skew):
    if count == 2:
        one = jax.random.randint(key, (), max(1, total - reach), min(reach, total - 1) + 1)
        return jnp.stack([one, total - one])
    tallies = jnp.asarray(split_up(count, total, reach, skew), jnp.int32)
    twos = (count - 1) // 2
    source_of, taker = tallies[1:1 + 2 * twos:2], tallies[2:2 + 2 * twos:2]
    slack = jnp.minimum(source_of - 1, reach - taker)
    passed = jax.random.randint(jax.random.fold_in(key, 1), (twos,), 0, 1 << 20) % (slack + 1)
    tallies = tallies.at[1:1 + 2 * twos:2].set(source_of - passed).at[2:2 + 2 * twos:2].set(taker + passed)
    return tallies[jax.random.permutation(jax.random.fold_in(key, 2), count)]


def noise(stream_key, dims, scale, most, pieces=(), held_as=jnp.bfloat16):
    drawn = jax.random.normal(stream_key, dims, jnp.float32) * scale
    if len(pieces) > 0:
        drawn = shard_levels(stream_key, dims, pieces, -0.22, 0.18) * drawn
    return jnp.clip(drawn, min=-most, max=most).astype(held_as)


def setup_inputs(seed: int = 0) -> dict:
    key_list = jax.random.split(jax.random.key(seed), 9)
    frames = noise(key_list[0], (N_DP, SEQ_ROWS, D), 1.0, 6.0, ((0, 16), (1, 8)))
    cotangent = noise(key_list[1], (N_DP, SEQ_ROWS, D), 1.0, 6.0, ((0, 16), (1, 8)))
    segments = jax.vmap(lambda own: jnp.searchsorted(jnp.cumsum(uneven_parts(own, UTTERANCES, SEQ_ROWS, 128, 2)), jnp.arange(SEQ_ROWS), side="right"))(jax.random.split(key_list[2], N_DP)).reshape((N_DP, SEQ_ROWS)).astype(jnp.int32)
    w_in = noise(key_list[3], (D, 2 * D), D ** -0.5, 0.1875, ((0, 128),))
    w_out = noise(key_list[4], (D, D), D ** -0.5, 0.1875, ((0, 128),))
    kernel = noise(key_list[5], (D, KW), KW ** -0.5, 1.0, ((0, 128),))
    gain_in = jnp.clip(1.0 + 0.18 * jax.random.normal(key_list[6], (D,), jnp.float32), 0.099609375, 1.8984375).astype(jnp.bfloat16)
    gain_mid = jnp.clip(1.0 + 0.18 * jax.random.normal(key_list[7], (D,), jnp.float32), 0.099609375, 1.8984375).astype(jnp.bfloat16)
    return {"frames": frames, "cotangent": cotangent, "segments": segments, "w_in": w_in, "w_out": w_out, "kernel": kernel, "gain_in": gain_in, "gain_mid": gain_mid}


EPS = 1e-05
HALF = 15

def norm_rows(values, gain):
    mean = lax.optimization_barrier(jnp.mean(values, axis=-1, keepdims=True))
    centred = values - mean
    inv = lax.rsqrt(lax.optimization_barrier(jnp.mean(centred * centred, axis=-1, keepdims=True)) + EPS)
    normal = centred * inv
    return (normal, inv, normal * gain)

def norm_back(grad_out, normal, inv, gain):
    scaled = grad_out * gain
    return inv * (scaled - lax.optimization_barrier(jnp.mean(scaled, -1, keepdims=True)) - normal * lax.optimization_barrier(jnp.mean(scaled * normal, -1, keepdims=True)))

def block_pass(frames, cotangent, seg_pad, widen_glu, widen_grad, w_in, w_out, kernel, gain_in, gain_mid, scale):
    rows = frames.shape[0]
    width = frames.shape[1]
    taps = kernel.shape[1]
    kern = kernel.astype(jnp.float32)
    centre = seg_pad[HALF:HALF + rows]
    x_val = frames.astype(jnp.float32)
    normal_in, inv_in, scaled_in = norm_rows(x_val, gain_in.astype(jnp.float32))
    ln_in = scaled_in.astype(jnp.bfloat16)
    pre = jnp.dot(ln_in, w_in, preferred_element_type=jnp.float32)
    value = pre[:, :width]
    gate_sig = jax.nn.sigmoid(pre[:, width:])
    glu = (value * gate_sig).astype(jnp.bfloat16)
    glu_pad = widen_glu(glu)
    mixed = jnp.zeros((rows, width), jnp.float32)
    for tap in range(taps):
        same = (seg_pad[tap:tap + rows] == centre)[:, None]
        mixed = mixed + jnp.where(same, glu_pad[tap:tap + rows].astype(jnp.float32) * kern[:, tap], 0.0)
    gmid = gain_mid.astype(jnp.float32)
    normal_mid, inv_mid, ln_mid = norm_rows(mixed, gmid)
    sig_mid = jax.nn.sigmoid(ln_mid)
    act = (ln_mid * sig_mid).astype(jnp.bfloat16)
    block_out = (x_val + jnp.dot(act, w_out, preferred_element_type=jnp.float32)).astype(jnp.bfloat16)
    grad_w_out = jnp.dot(act.T, cotangent, preferred_element_type=jnp.float32) * scale
    d_act = jnp.dot(cotangent, w_out.T, preferred_element_type=jnp.float32)
    d_ln_mid = d_act * (sig_mid + ln_mid * sig_mid * (1.0 - sig_mid))
    grad_gain_mid = lax.optimization_barrier(jnp.sum(d_ln_mid * normal_mid, axis=0)) * scale
    d_mixed = norm_back(d_ln_mid, normal_mid, inv_mid, gmid)
    grad_pad = widen_grad(d_mixed)
    d_glu = jnp.zeros((rows, width), jnp.float32)
    kernel_terms = []
    for tap in range(taps):
        same = (seg_pad[tap:tap + rows] == centre)[:, None]
        kernel_terms.append(lax.optimization_barrier(jnp.sum(jnp.where(same, glu_pad[tap:tap + rows].astype(jnp.float32) * d_mixed, 0.0), axis=0)))
        start = 2 * HALF - tap
        back_same = (seg_pad[start:start + rows] == centre)[:, None]
        d_glu = d_glu + jnp.where(back_same, grad_pad[start:start + rows] * kern[:, tap], 0.0)
    grad_kernel = jnp.stack(kernel_terms, axis=1) * scale
    d_pre = jnp.concatenate([d_glu * gate_sig, d_glu * value * gate_sig * (1.0 - gate_sig)], axis=-1).astype(jnp.bfloat16)
    grad_w_in = jnp.dot(ln_in.T, d_pre, preferred_element_type=jnp.float32) * scale
    d_ln_in = jnp.dot(d_pre, w_in.T, preferred_element_type=jnp.float32)
    gin = gain_in.astype(jnp.float32)
    grad_gain_in = lax.optimization_barrier(jnp.sum(d_ln_in * normal_in, axis=0)) * scale
    input_grad = (cotangent.astype(jnp.float32) + norm_back(d_ln_in, normal_in, inv_in, gin)).astype(jnp.bfloat16)
    return (block_out, input_grad, (grad_w_in, grad_w_out, grad_kernel, grad_gain_in, grad_gain_mid))

def widen_rows(values):
    return jnp.pad(values, ((HALF, HALF), (0, 0)))

def reference(frames, cotangent, segments, w_in, w_out, kernel, gain_in, gain_mid):
    scale = jnp.float32(1.0 / math.sqrt(FRAMES))
    width = frames.shape[2]

    def step(carry, item):
        frame_rows, cot_rows, seg_rows = item
        seg_pad = jnp.pad(seg_rows, HALF, constant_values=-1)
        out_rows, grad_rows, partial_grads = block_pass(frame_rows, cot_rows, seg_pad, widen_rows, widen_rows, w_in, w_out, kernel, gain_in, gain_mid, scale)
        carry = tuple((left + right for left, right in zip(carry, partial_grads)))
        return (carry, (out_rows, grad_rows))
    init = (jnp.zeros((width, 2 * width), jnp.float32), jnp.zeros((width, width), jnp.float32), jnp.zeros((width, kernel.shape[1]), jnp.float32), jnp.zeros((width,), jnp.float32), jnp.zeros((width,), jnp.float32))
    grads, (block_out, input_grad) = lax.scan(step, init, (frames, cotangent, segments))
    return (block_out, input_grad, grads[0], grads[1], grads[2], grads[3], grads[4])
```

```python
import math

import jax
import jax.numpy as jnp
from jax import lax
from jax.experimental import pallas as pl
from jax.experimental.pallas import tpu as pltpu
from jax.sharding import PartitionSpec as P

MESH = pl.DeviceIdType.MESH
HALFW = 1664
WIDE = 2 * HALFW
PARTS = ((0, 512, 256), (512, 512, 256), (1024, 640, 384))
ORDERS = (("z", "x", "y"), ("x", "y", "z"), ("y", "z", "x"))
HALO = 32


def place():
    d, s = lax.axis_index("dp"), lax.axis_index("seq")
    return {"y": d // 4, "x": d % 4, "z": s // 2}, s % 2


def dev(coords, core):
    return (coords["y"] * 4 + coords["x"], coords["z"] * 2 + core)


def moved(coords, axis, by):
    out = dict(coords)
    out[axis] = (coords[axis] + by + 4) % 4
    return out


def greet(targets):
    barrier = pltpu.get_barrier_semaphore()
    for t in targets:
        pl.semaphore_signal(barrier, inc=1, device_id=t, device_id_type=MESH)
    pl.semaphore_wait(barrier, len(targets))


def block_index(coords, full, axis, value):
    out = []
    for a in ("y", "x", "z"):
        if a == axis:
            out.append(value)
        elif a in full:
            out.append(slice(None))
        else:
            out.append(coords[a])
    return tuple(out)


def gather_kernel(
    shard_ref, frames_ref, cot_ref, seg_ref,
    out_ref, hf_ref, hc_ref, hs_ref,
    buf, sib, sib_sem, halo_send, halo_recv, a_send, a_recv, s_send, s_recv, out_sem,
):
    me, core = place()
    sibling = dev(me, 1 - core)
    right = (lax.axis_index("dp"), (lax.axis_index("seq") + 1) % 8)
    left = (lax.axis_index("dp"), (lax.axis_index("seq") + 7) % 8)
    cross = dev(moved(me, "z", 2 * core - 1), 1 - core)
    targets = [dev(moved(me, a, b), core) for a in "yxz" for b in (1, -1)]
    greet(targets + [sibling, cross])

    first = pltpu.make_async_remote_copy(
        src_ref=shard_ref, dst_ref=sib, send_sem=sib_sem.at[0], recv_sem=sib_sem.at[1],
        device_id=sibling, device_id_type=MESH)
    first.start()
    halos = []
    rows = frames_ref.shape[0]
    for n, (src, dst, h) in enumerate(((frames_ref, hf_ref, HALO), (cot_ref, hc_ref, 16), (seg_ref, hs_ref, HALO))):
        for m, (at, to, who) in enumerate(((rows - h, 0, right), (0, h, left))):
            cp = pltpu.make_async_remote_copy(
                src_ref=src.at[pl.ds(at, h)], dst_ref=dst.at[pl.ds(to, h)],
                send_sem=halo_send.at[n, m], recv_sem=halo_recv.at[n, m],
                device_id=who, device_id_type=MESH)
            halos.append(cp)
    first.wait()
    mine, other = shard_ref[...], sib[...]
    low = jnp.where(core == 0, mine[:, :HALFW], other[:, HALFW:])
    high = jnp.where(core == 0, other[:, :HALFW], mine[:, HALFW:])
    buf[me["y"], me["x"], me["z"], :, pl.ds(pl.multiple_of(core * HALFW, 128), HALFW)] = jnp.concatenate(
        [low, high], axis=0).astype(jnp.bfloat16)
    for cp in halos:
        cp.start()

    def cols(p, lo, width, c=core):
        return pl.ds(pl.multiple_of(c * HALFW + PARTS[p][0] + lo, 128), width)

    def send(p, ph, which, idx, lo, width, by):
        axis = ORDERS[p][ph]
        ref = buf.at[idx + (slice(None), cols(p, lo, width))]
        return pltpu.make_async_remote_copy(
            src_ref=ref, dst_ref=ref, send_sem=a_send.at[p, ph, which], recv_sem=a_recv.at[p, ph, which],
            device_id=dev(moved(me, axis, by), core), device_id_type=MESH)

    def to_sibling(p, which, idx, c=core):
        start, width, _ = PARTS[p]
        ref = buf.at[idx + (slice(None), cols(p, 0, width, c))]
        return pltpu.make_async_remote_copy(
            src_ref=ref, dst_ref=ref, send_sem=s_send.at[p, which], recv_sem=s_recv.at[p, which],
            device_id=sibling, device_id_type=MESH)

    def block(p, ph, by):
        axis = ORDERS[p][ph]
        return block_index(me, ORDERS[p][:ph], axis, (me[axis] + by + 4) % 4)

    sends = []
    for ph in range(3):
        for p in range(3):
            _, width, half = PARTS[p]
            if ph > 0:
                opp = block(p, ph - 1, 2)
                send(p, ph - 1, 2, opp, 0, half, 1).wait_recv()
                send(p, ph - 1, 3, opp, half, width - half, -1).wait_recv()
            own = block(p, ph, 0)
            for which, by in ((0, 1), (1, -1)):
                cp = send(p, ph, which, own, 0, width, by)
                cp.start()
                sends.append(cp)
            if ph == 2:
                cp = to_sibling(p, 0, own)
                cp.start()
                sends.append(cp)
        for p in range(3):
            _, width, half = PARTS[p]
            for which, by, lo, w in ((0, -1, 0, half), (1, 1, half, width - half)):
                idx = block(p, ph, by)
                send(p, ph, which, idx, 0, width, -by).wait_recv()
                cp = send(p, ph, which + 2, idx, lo, w, -by)
                cp.start()
                sends.append(cp)
                if ph == 2:
                    cp = to_sibling(p, 1 + which, idx)
                    cp.start()
                    sends.append(cp)
    for p in range(3):
        _, width, half = PARTS[p]
        opp = block(p, 2, 2)
        send(p, 2, 2, opp, 0, half, 1).wait_recv()
        send(p, 2, 3, opp, half, width - half, -1).wait_recv()
        cp = to_sibling(p, 3, opp)
        cp.start()
        sends.append(cp)
    for p in range(3):
        for which, by in ((0, 0), (1, -1), (2, 1), (3, 2)):
            to_sibling(p, which, block(p, 2, by), 1 - core).wait_recv()
    out = pltpu.make_async_copy(buf, out_ref, out_sem)
    out.start()
    for cp in sends:
        cp.wait_send()
    for cp in halos:
        cp.wait()
    out.wait()


def gather(shard, frames, cot, seg):
    bf = jnp.bfloat16
    vm = pl.BlockSpec(memory_space=pltpu.VMEM)
    hbm = pl.BlockSpec(memory_space=pl.ANY)
    return pl.pallas_call(
        gather_kernel,
        out_shape=(
            jax.ShapeDtypeStruct((4, 4, 4, 16, WIDE), bf),
            jax.ShapeDtypeStruct((2 * HALO, 1024), bf),
            jax.ShapeDtypeStruct((32, 1024), bf),
            jax.ShapeDtypeStruct((2 * HALO, 128), bf),
        ),
        in_specs=[vm, hbm, hbm, hbm],
        out_specs=(hbm, vm, vm, vm),
        scratch_shapes=[
            pltpu.VMEM((4, 4, 4, 16, WIDE), bf),
            pltpu.VMEM((8, WIDE), jnp.float32),
            pltpu.SemaphoreType.DMA((2,)),
            pltpu.SemaphoreType.DMA((3, 2)),
            pltpu.SemaphoreType.DMA((3, 2)),
            pltpu.SemaphoreType.DMA((3, 3, 4)),
            pltpu.SemaphoreType.DMA((3, 3, 4)),
            pltpu.SemaphoreType.DMA((3, 4)),
            pltpu.SemaphoreType.DMA((3, 4)),
            pltpu.SemaphoreType.DMA,
        ],
        compiler_params=pltpu.CompilerParams(
            collective_id=0, has_side_effects=True, vmem_limit_bytes=24 << 20),
        name="gather_weights",
    )(shard, frames, cot, seg)


def shapes_of(full):
    return tuple(4 if a in full else 1 for a in "yxz")


def scatter_kernel(
    g_ref, out_ref,
    acc, sibbuf, h0, h1, h2, f0, f1, f2, last, low, fin, own_sem, d_send, d_recv, a_send, a_recv, e_sem,
):
    me, core = place()
    sibling = dev(me, 1 - core)
    targets = [dev(moved(me, a, b), core) for a in "yxz" for b in (1, -1)]
    greet(targets + [sibling])
    hbufs, fbufs = (h0, h1, h2), (f0, f1, f2)

    def cols(p, c):
        return pl.ds(pl.multiple_of(c * HALFW + PARTS[p][0], 128), PARTS[p][1])

    def lane(p, lo, w):
        return pl.ds(PARTS[p][0] + lo, w)

    full3 = (slice(None),) * 4
    owns, gives, sends = [], [], []
    for p in range(3):
        give = pltpu.make_async_remote_copy(
            src_ref=g_ref.at[full3 + (cols(p, 1 - core),)], dst_ref=sibbuf.at[full3 + (lane(p, 0, PARTS[p][1]),)],
            send_sem=d_send.at[p], recv_sem=d_recv.at[p], device_id=sibling, device_id_type=MESH)
        give.start()
        own = pltpu.make_async_copy(
            g_ref.at[full3 + (cols(p, core),)], acc.at[full3 + (lane(p, 0, PARTS[p][1]),)], own_sem.at[p])
        own.start()
        owns.append(own)
        gives.append(give)

    def axis_of(p, ph):
        return ORDERS[p][2 - ph]

    def rest(p, ph):
        return ORDERS[p][: 2 - ph]

    def block(p, ph, by):
        axis = axis_of(p, ph)
        return block_index(me, rest(p, ph), axis, (me[axis] + by + 4) % 4)

    def hview(p, ph, lo, w):
        nd = 2 - ph
        return hbufs[ph].at[(slice(None),) * nd + (slice(None), lane(p, lo, w))]

    def fview(p, ph, which, lo, w):
        nd = 2 - ph
        return fbufs[ph].at[(which,) + (slice(None),) * nd + (slice(None), lane(p, lo, w))]

    def send_half(p, ph, which):
        _, width, half = PARTS[p]
        lo, w, by = ((0, half, 1), (half, width - half, -1))[which]
        return pltpu.make_async_remote_copy(
            src_ref=acc.at[block(p, ph, 2) + (slice(None), lane(p, lo, w))], dst_ref=hview(p, ph, lo, w),
            send_sem=a_send.at[p, ph, which], recv_sem=a_recv.at[p, ph, which],
            device_id=dev(moved(me, axis_of(p, ph), by), core), device_id_type=MESH)

    def send_full(p, ph, which):
        _, width, _ = PARTS[p]
        by = (1, -1)[which]
        return pltpu.make_async_remote_copy(
            src_ref=acc.at[block(p, ph, by) + (slice(None), lane(p, 0, width))], dst_ref=fview(p, ph, which, 0, width),
            send_sem=a_send.at[p, ph, 2 + which], recv_sem=a_recv.at[p, ph, 2 + which],
            device_id=dev(moved(me, axis_of(p, ph), by), core), device_id_type=MESH)

    def over(p, ph, value_axis_index, body):
        names = rest(p, ph)
        axis = axis_of(p, ph)
        n = 4 ** len(names)

        def index(k):
            digits = [k // 4, k % 4][2 - len(names):] if names else []
            by_name = dict(zip([a for a in "yxz" if a in names], digits))
            at = []
            for a in "yxz":
                at.append(by_name[a] if a in by_name else (value_axis_index if a == axis else me[a]))
            return tuple(at), tuple(digits)

        if n == 1:
            body(*index(0))
        else:
            def step(k, carry):
                body(*index(k))
                return carry
            lax.fori_loop(0, n, step, 0)

    f32 = jnp.float32
    for p in range(3):
        start, width, half = PARTS[p]
        owns[p].wait()
        gives[p].wait_recv()
        sl = pl.ds(start, width)

        def body(k, carry, sl=sl):
            at = (k // 16, (k // 4) % 4, k % 4, slice(None), sl)
            acc[at] = (acc[at].astype(f32) + sibbuf[at].astype(f32)).astype(jnp.bfloat16)
            return carry
        lax.fori_loop(0, 64, body, 0)
        for which in (0, 1):
            cp = send_half(p, 0, which)
            cp.start()
            sends.append(cp)
    for ph in range(3):
        for p in range(3):
            start, width, half = PARTS[p]
            axis = axis_of(p, ph)
            for which, by, lo, w in ((0, 1, 0, half), (1, -1, half, width - half)):
                send_half(p, ph, which).wait_recv()
                sl = pl.ds(start + lo, w)

                def body(at, dig, ph=ph, sl=sl):
                    at = at + (slice(None), sl)
                    hat = dig + (slice(None), sl)
                    acc[at] = (acc[at].astype(f32) + hbufs[ph][hat].astype(f32)).astype(jnp.bfloat16)
                over(p, ph, (me[axis] + by + 4) % 4, body)
                cp = send_full(p, ph, which)
                cp.start()
                sends.append(cp)
        for p in range(3):
            start, width, half = PARTS[p]
            axis = axis_of(p, ph)
            for which in (0, 1):
                send_full(p, ph, which).wait_recv()
            sl = pl.ds(start, width)

            def body(at, dig, ph=ph, sl=sl):
                at = at + (slice(None), sl)
                total = (acc[at].astype(f32) + fbufs[ph][(0,) + dig + (slice(None), sl)].astype(f32)
                         + fbufs[ph][(1,) + dig + (slice(None), sl)].astype(f32))
                if ph < 2:
                    acc[at] = total.astype(jnp.bfloat16)
                else:
                    last[:, sl] = total
            over(p, ph, me[axis], body)
            if ph < 2:
                for which in (0, 1):
                    cp = send_half(p, ph + 1, which)
                    cp.start()
                    sends.append(cp)
    top, bottom = last[0:8, :], last[8:16, :]
    low[...] = jnp.where(core == 0, bottom, top)
    swap = pltpu.make_async_remote_copy(
        src_ref=low, dst_ref=fin, send_sem=e_sem.at[0], recv_sem=e_sem.at[1], device_id=sibling, device_id_type=MESH)
    swap.start()
    mine = jnp.where(core == 0, top, bottom)
    swap.wait()
    theirs = fin[...]
    out_ref[:, :HALFW] = jnp.where(core == 0, mine, theirs)
    out_ref[:, HALFW:] = jnp.where(core == 0, theirs, mine)
    for cp in sends + gives:
        cp.wait_send()


def scatter(g):
    bf = jnp.bfloat16
    return pl.pallas_call(
        scatter_kernel,
        out_shape=jax.ShapeDtypeStruct((8, WIDE), jnp.float32),
        in_specs=[pl.BlockSpec(memory_space=pl.ANY)],
        out_specs=pl.BlockSpec(memory_space=pltpu.VMEM),
        scratch_shapes=[
            pltpu.VMEM((4, 4, 4, 16, HALFW), bf),
            pltpu.VMEM((4, 4, 4, 16, HALFW), bf),
            pltpu.VMEM((4, 4, 16, HALFW), bf),
            pltpu.VMEM((4, 16, HALFW), bf),
            pltpu.VMEM((16, HALFW), bf),
            pltpu.VMEM((2, 4, 4, 16, HALFW), bf),
            pltpu.VMEM((2, 4, 16, HALFW), bf),
            pltpu.VMEM((2, 16, HALFW), bf),
            pltpu.VMEM((16, HALFW), jnp.float32),
            pltpu.VMEM((8, HALFW), jnp.float32),
            pltpu.VMEM((8, HALFW), jnp.float32),
            pltpu.SemaphoreType.DMA((3,)),
            pltpu.SemaphoreType.DMA((3,)),
            pltpu.SemaphoreType.DMA((3,)),
            pltpu.SemaphoreType.DMA((3, 3, 4)),
            pltpu.SemaphoreType.DMA((3, 3, 4)),
            pltpu.SemaphoreType.DMA((2,)),
        ],
        compiler_params=pltpu.CompilerParams(
            collective_id=1, has_side_effects=True, vmem_limit_bytes=32 << 20),
        name="scatter_grads",
    )(g)


EPS = 1e-05
HALF = 15


def with_halo(array, sides, width):
    for axis, dim in sides:
        count, length = (lax.axis_size(axis), array.shape[dim])
        up = [(i, (i + 1) % count) for i in range(count - 1)]
        down = [(j, i) for i, j in up]
        last = lax.slice_in_dim(array, length - width, length, axis=dim)
        first = lax.slice_in_dim(array, 0, width, axis=dim)
        before = lax.ppermute(last, axis, up)
        after = lax.ppermute(first, axis, down)
        array = jnp.concatenate([before, array, after], axis=dim)
    return array


def norm_rows(values, gain):
    mean = jnp.mean(values, axis=-1, keepdims=True)
    centred = values - mean
    inv = lax.rsqrt(jnp.mean(centred * centred, axis=-1, keepdims=True) + EPS)
    normal = centred * inv
    return (normal, inv, normal * gain)


def norm_back(grad_out, normal, inv, gain):
    scaled = grad_out * gain
    return inv * (
        scaled
        - jnp.mean(scaled, -1, keepdims=True)
        - normal * jnp.mean(scaled * normal, -1, keepdims=True)
    )


def block_pass(
    frames, cotangent, seg_pad, widen_glu, widen_grad, w_in, w_out, kernel, gain_in, gain_mid, scale
):
    rows = frames.shape[0]
    width = frames.shape[1]
    taps = kernel.shape[1]
    kern = kernel.astype(jnp.float32)
    centre = seg_pad[HALF : HALF + rows]
    x_val = frames.astype(jnp.float32)
    normal_in, inv_in, scaled_in = norm_rows(x_val, gain_in.astype(jnp.float32))
    ln_in = scaled_in.astype(jnp.bfloat16)
    pre = jnp.dot(ln_in, w_in, preferred_element_type=jnp.float32)
    value = pre[:, :width]
    gate_sig = jax.nn.sigmoid(pre[:, width:])
    glu = (value * gate_sig).astype(jnp.bfloat16)
    glu_pad = widen_glu(glu)
    mixed = jnp.zeros((rows, width), jnp.float32)
    for tap in range(taps):
        same = (seg_pad[tap : tap + rows] == centre)[:, None]
        mixed = mixed + jnp.where(
            same, glu_pad[tap : tap + rows].astype(jnp.float32) * kern[:, tap], 0.0
        )
    gmid = gain_mid.astype(jnp.float32)
    normal_mid, inv_mid, ln_mid = norm_rows(mixed, gmid)
    sig_mid = jax.nn.sigmoid(ln_mid)
    act = (ln_mid * sig_mid).astype(jnp.bfloat16)
    block_out = (x_val + jnp.dot(act, w_out, preferred_element_type=jnp.float32)).astype(
        jnp.bfloat16
    )
    grad_w_out = jnp.dot(act.T, cotangent, preferred_element_type=jnp.float32) * scale
    d_act = jnp.dot(cotangent, w_out.T, preferred_element_type=jnp.float32)
    d_ln_mid = d_act * (sig_mid + ln_mid * sig_mid * (1.0 - sig_mid))
    grad_gain_mid = jnp.sum(d_ln_mid * normal_mid, axis=0) * scale
    d_mixed = norm_back(d_ln_mid, normal_mid, inv_mid, gmid)
    grad_pad = widen_grad(d_mixed)
    d_glu = jnp.zeros((rows, width), jnp.float32)
    kernel_terms = []
    for tap in range(taps):
        same = (seg_pad[tap : tap + rows] == centre)[:, None]
        kernel_terms.append(
            jnp.sum(
                jnp.where(same, glu_pad[tap : tap + rows].astype(jnp.float32) * d_mixed, 0.0),
                axis=0,
            )
        )
        start = 2 * HALF - tap
        back_same = (seg_pad[start : start + rows] == centre)[:, None]
        d_glu = d_glu + jnp.where(back_same, grad_pad[start : start + rows] * kern[:, tap], 0.0)
    grad_kernel = jnp.stack(kernel_terms, axis=1) * scale
    d_pre = jnp.concatenate(
        [d_glu * gate_sig, d_glu * value * gate_sig * (1.0 - gate_sig)], axis=-1
    ).astype(jnp.bfloat16)
    grad_w_in = jnp.dot(ln_in.T, d_pre, preferred_element_type=jnp.float32) * scale
    d_ln_in = jnp.dot(d_pre, w_in.T, preferred_element_type=jnp.float32)
    gin = gain_in.astype(jnp.float32)
    grad_gain_in = jnp.sum(d_ln_in * normal_in, axis=0) * scale
    input_grad = (
        cotangent.astype(jnp.float32) + norm_back(d_ln_in, normal_in, inv_in, gin)
    ).astype(jnp.bfloat16)
    return (
        block_out,
        input_grad,
        (grad_w_in, grad_w_out, grad_kernel, grad_gain_in, grad_gain_mid),
    )


def shards(frames, cotangent, segments, w_in, w_out, kernel, gain_in, gain_mid):
    frame_rows = frames[0]
    cot_rows = cotangent[0]
    rows = frame_rows.shape[0]
    f32 = jnp.float32
    packed = jnp.concatenate(
        [w_in.astype(f32), w_out.astype(f32), kernel.astype(f32), gain_in.astype(f32)[:, None],
         gain_mid.astype(f32)[:, None], jnp.zeros((8, WIDE - 3072 - 33), f32)], axis=1)
    seg_rows = jnp.broadcast_to(segments[0].astype(jnp.bfloat16)[:, None], (rows, 128))
    full, _, _, seg_halo = gather(packed, frame_rows, cot_rows, seg_rows)
    full = full.reshape(1024, WIDE)
    scale = jnp.float32(1.0 / math.sqrt(rows * 128))
    at = lax.axis_index("seq")
    halo = seg_halo[:, 0].astype(jnp.int32)
    seg_pad = jnp.concatenate([
        jnp.where(at == 0, -1, halo[HALO - HALF : HALO]), segments[0],
        jnp.where(at == 7, -1, halo[HALO : HALO + HALF])])
    block_out, input_grad, partial_grads = block_pass(
        frame_rows,
        cot_rows,
        seg_pad,
        lambda values: with_halo(values, (("seq", 0),), HALF),
        lambda values: with_halo(values, (("seq", 0),), HALF),
        full[:, :2048],
        full[:, 2048:3072],
        full[:, 3072:3103],
        full[:, 3103],
        full[:, 3104],
        scale,
    )
    bf = jnp.bfloat16
    g = jnp.concatenate([
        partial_grads[0].astype(bf), partial_grads[1].astype(bf), partial_grads[2].astype(bf),
        partial_grads[3].astype(bf)[:, None], partial_grads[4].astype(bf)[:, None],
        jnp.zeros((1024, WIDE - 3072 - 33), bf)], axis=1).reshape(4, 4, 4, 16, WIDE)
    r = scatter(g)
    return (block_out[None], input_grad[None], r[:, :2048], r[:, 2048:3072], r[:, 3072:3103], r[:, 3103], r[:, 3104])


def solution(mesh):
    in_specs = (
        P("dp", "seq", None),
        P("dp", "seq", None),
        P("dp", "seq"),
        P(("dp", "seq"), None),
        P(("dp", "seq"), None),
        P(("dp", "seq"), None),
        P(("dp", "seq")),
        P(("dp", "seq")),
    )
    out_specs = (
        P("dp", "seq", None),
        P("dp", "seq", None),
        P(("dp", "seq"), None),
        P(("dp", "seq"), None),
        P(("dp", "seq"), None),
        P(("dp", "seq")),
        P(("dp", "seq")),
    )
    return jax.shard_map(shards, mesh=mesh, in_specs=in_specs, out_specs=out_specs, check_vma=False)
```

```python
import math

import jax
import jax.numpy as jnp
import numpy as np
from jax import lax
from jax.experimental import pallas as pl
from jax.experimental.pallas import tpu as pltpu
from jax.sharding import PartitionSpec as P

MESH = pl.DeviceIdType.MESH
HALFW = 1664
WIDE = 2 * HALFW
PARTS = ((0, 512, 256), (512, 512, 256), (1024, 640, 384))
ORDERS = (("z", "x", "y"), ("x", "y", "z"), ("y", "z", "x"))
HALO = 32


def place():
    d, s = lax.axis_index("dp"), lax.axis_index("seq")
    return {"y": d // 4, "x": d % 4, "z": s // 2}, s % 2


def dev(coords, core):
    return (coords["y"] * 4 + coords["x"], coords["z"] * 2 + core)


def moved(coords, axis, by):
    out = dict(coords)
    out[axis] = (coords[axis] + by + 4) % 4
    return out


def greet(targets):
    barrier = pltpu.get_barrier_semaphore()
    for t in targets:
        pl.semaphore_signal(barrier, inc=1, device_id=t, device_id_type=MESH)
    pl.semaphore_wait(barrier, len(targets))


def block_index(coords, full, axis, value):
    out = []
    for a in ("y", "x", "z"):
        if a == axis:
            out.append(value)
        elif a in full:
            out.append(slice(None))
        else:
            out.append(coords[a])
    return tuple(out)


def gather_kernel(
    shard_ref, frames_ref, cot_ref, seg_ref,
    out_ref, hf_ref, hc_ref, hs_ref,
    buf, sib, sib_sem, halo_send, halo_recv, a_send, a_recv, s_send, s_recv, out_sem,
):
    me, core = place()
    sibling = dev(me, 1 - core)
    right = (lax.axis_index("dp"), (lax.axis_index("seq") + 1) % 8)
    left = (lax.axis_index("dp"), (lax.axis_index("seq") + 7) % 8)
    cross = dev(moved(me, "z", 2 * core - 1), 1 - core)
    targets = [dev(moved(me, a, b), core) for a in "yxz" for b in (1, -1)]
    greet(targets + [sibling, cross])

    first = pltpu.make_async_remote_copy(
        src_ref=shard_ref, dst_ref=sib, send_sem=sib_sem.at[0], recv_sem=sib_sem.at[1],
        device_id=sibling, device_id_type=MESH)
    first.start()
    halos = []
    rows = frames_ref.shape[0]
    for n, (src, dst, h) in enumerate(((frames_ref, hf_ref, HALO), (cot_ref, hc_ref, 16), (seg_ref, hs_ref, HALO))):
        for m, (at, to, who) in enumerate(((rows - h, 0, right), (0, h, left))):
            cp = pltpu.make_async_remote_copy(
                src_ref=src.at[pl.ds(at, h)], dst_ref=dst.at[pl.ds(to, h)],
                send_sem=halo_send.at[n, m], recv_sem=halo_recv.at[n, m],
                device_id=who, device_id_type=MESH)
            halos.append(cp)
    first.wait()
    mine, other = shard_ref[...], sib[...]
    low = jnp.where(core == 0, mine[:, :HALFW], other[:, HALFW:])
    high = jnp.where(core == 0, other[:, :HALFW], mine[:, HALFW:])
    buf[me["y"], me["x"], me["z"], :, pl.ds(pl.multiple_of(core * HALFW, 128), HALFW)] = jnp.concatenate(
        [low, high], axis=0).astype(jnp.bfloat16)
    for cp in halos:
        cp.start()

    def cols(p, lo, width, c=core):
        return pl.ds(pl.multiple_of(c * HALFW + PARTS[p][0] + lo, 128), width)

    def send(p, ph, which, idx, lo, width, by):
        axis = ORDERS[p][ph]
        ref = buf.at[idx + (slice(None), cols(p, lo, width))]
        return pltpu.make_async_remote_copy(
            src_ref=ref, dst_ref=ref, send_sem=a_send.at[p, ph, which], recv_sem=a_recv.at[p, ph, which],
            device_id=dev(moved(me, axis, by), core), device_id_type=MESH)

    def to_sibling(p, which, idx, c=core):
        start, width, _ = PARTS[p]
        ref = buf.at[idx + (slice(None), cols(p, 0, width, c))]
        return pltpu.make_async_remote_copy(
            src_ref=ref, dst_ref=ref, send_sem=s_send.at[p, which], recv_sem=s_recv.at[p, which],
            device_id=sibling, device_id_type=MESH)

    def block(p, ph, by):
        axis = ORDERS[p][ph]
        return block_index(me, ORDERS[p][:ph], axis, (me[axis] + by + 4) % 4)

    sends = []
    for ph in range(3):
        for p in range(3):
            _, width, half = PARTS[p]
            if ph > 0:
                opp = block(p, ph - 1, 2)
                send(p, ph - 1, 2, opp, 0, half, 1).wait_recv()
                send(p, ph - 1, 3, opp, half, width - half, -1).wait_recv()
            own = block(p, ph, 0)
            for which, by in ((0, 1), (1, -1)):
                cp = send(p, ph, which, own, 0, width, by)
                cp.start()
                sends.append(cp)
            if ph == 2:
                cp = to_sibling(p, 0, own)
                cp.start()
                sends.append(cp)
        for p in range(3):
            _, width, half = PARTS[p]
            for which, by, lo, w in ((0, -1, 0, half), (1, 1, half, width - half)):
                idx = block(p, ph, by)
                send(p, ph, which, idx, 0, width, -by).wait_recv()
                cp = send(p, ph, which + 2, idx, lo, w, -by)
                cp.start()
                sends.append(cp)
                if ph == 2:
                    cp = to_sibling(p, 1 + which, idx)
                    cp.start()
                    sends.append(cp)
    for p in range(3):
        _, width, half = PARTS[p]
        opp = block(p, 2, 2)
        send(p, 2, 2, opp, 0, half, 1).wait_recv()
        send(p, 2, 3, opp, half, width - half, -1).wait_recv()
        cp = to_sibling(p, 3, opp)
        cp.start()
        sends.append(cp)
    for p in range(3):
        for which, by in ((0, 0), (1, -1), (2, 1), (3, 2)):
            to_sibling(p, which, block(p, 2, by), 1 - core).wait_recv()
    out = pltpu.make_async_copy(buf, out_ref, out_sem)
    out.start()
    for cp in sends:
        cp.wait_send()
    for cp in halos:
        cp.wait()
    out.wait()


def gather(shard, frames, cot, seg):
    bf = jnp.bfloat16
    vm = pl.BlockSpec(memory_space=pltpu.VMEM)
    hbm = pl.BlockSpec(memory_space=pl.ANY)
    return pl.pallas_call(
        gather_kernel,
        out_shape=(
            jax.ShapeDtypeStruct((4, 4, 4, 16, WIDE), bf),
            jax.ShapeDtypeStruct((2 * HALO, 1024), bf),
            jax.ShapeDtypeStruct((32, 1024), bf),
            jax.ShapeDtypeStruct((2 * HALO, 128), bf),
        ),
        in_specs=[vm, hbm, hbm, hbm],
        out_specs=(hbm, vm, vm, vm),
        scratch_shapes=[
            pltpu.VMEM((4, 4, 4, 16, WIDE), bf),
            pltpu.VMEM((8, WIDE), jnp.float32),
            pltpu.SemaphoreType.DMA((2,)),
            pltpu.SemaphoreType.DMA((3, 2)),
            pltpu.SemaphoreType.DMA((3, 2)),
            pltpu.SemaphoreType.DMA((3, 3, 4)),
            pltpu.SemaphoreType.DMA((3, 3, 4)),
            pltpu.SemaphoreType.DMA((3, 4)),
            pltpu.SemaphoreType.DMA((3, 4)),
            pltpu.SemaphoreType.DMA,
        ],
        compiler_params=pltpu.CompilerParams(
            collective_id=0, has_side_effects=True, vmem_limit_bytes=24 << 20),
        name="gather_weights",
    )(shard, frames, cot, seg)


def shapes_of(full):
    return tuple(4 if a in full else 1 for a in "yxz")


def scatter_kernel(
    g_ref, out_ref,
    acc, sibbuf, h0, h1, h2, f0, f1, f2, last, low, fin, own_sem, d_send, d_recv, a_send, a_recv, e_sem,
):
    me, core = place()
    sibling = dev(me, 1 - core)
    targets = [dev(moved(me, a, b), core) for a in "yxz" for b in (1, -1)]
    greet(targets + [sibling])
    hbufs, fbufs = (h0, h1, h2), (f0, f1, f2)

    def cols(p, c):
        return pl.ds(pl.multiple_of(c * HALFW + PARTS[p][0], 128), PARTS[p][1])

    def lane(p, lo, w):
        return pl.ds(PARTS[p][0] + lo, w)

    full3 = (slice(None),) * 4
    owns, gives, sends = [], [], []
    for p in range(3):
        give = pltpu.make_async_remote_copy(
            src_ref=g_ref.at[full3 + (cols(p, 1 - core),)], dst_ref=sibbuf.at[full3 + (lane(p, 0, PARTS[p][1]),)],
            send_sem=d_send.at[p], recv_sem=d_recv.at[p], device_id=sibling, device_id_type=MESH)
        give.start()
        own = pltpu.make_async_copy(
            g_ref.at[full3 + (cols(p, core),)], acc.at[full3 + (lane(p, 0, PARTS[p][1]),)], own_sem.at[p])
        own.start()
        owns.append(own)
        gives.append(give)

    def axis_of(p, ph):
        return ORDERS[p][2 - ph]

    def rest(p, ph):
        return ORDERS[p][: 2 - ph]

    def block(p, ph, by):
        axis = axis_of(p, ph)
        return block_index(me, rest(p, ph), axis, (me[axis] + by + 4) % 4)

    def hview(p, ph, lo, w):
        nd = 2 - ph
        return hbufs[ph].at[(slice(None),) * nd + (slice(None), lane(p, lo, w))]

    def fview(p, ph, which, lo, w):
        nd = 2 - ph
        return fbufs[ph].at[(which,) + (slice(None),) * nd + (slice(None), lane(p, lo, w))]

    def send_half(p, ph, which):
        _, width, half = PARTS[p]
        lo, w, by = ((0, half, 1), (half, width - half, -1))[which]
        return pltpu.make_async_remote_copy(
            src_ref=acc.at[block(p, ph, 2) + (slice(None), lane(p, lo, w))], dst_ref=hview(p, ph, lo, w),
            send_sem=a_send.at[p, ph, which], recv_sem=a_recv.at[p, ph, which],
            device_id=dev(moved(me, axis_of(p, ph), by), core), device_id_type=MESH)

    def send_full(p, ph, which):
        _, width, _ = PARTS[p]
        by = (1, -1)[which]
        return pltpu.make_async_remote_copy(
            src_ref=acc.at[block(p, ph, by) + (slice(None), lane(p, 0, width))], dst_ref=fview(p, ph, which, 0, width),
            send_sem=a_send.at[p, ph, 2 + which], recv_sem=a_recv.at[p, ph, 2 + which],
            device_id=dev(moved(me, axis_of(p, ph), by), core), device_id_type=MESH)

    def over(p, ph, value_axis_index, body):
        names = rest(p, ph)
        axis = axis_of(p, ph)
        n = 4 ** len(names)

        def index(k):
            digits = [k // 4, k % 4][2 - len(names):] if names else []
            by_name = dict(zip([a for a in "yxz" if a in names], digits))
            at = []
            for a in "yxz":
                at.append(by_name[a] if a in by_name else (value_axis_index if a == axis else me[a]))
            return tuple(at), tuple(digits)

        if n == 1:
            body(*index(0))
        else:
            def step(k, carry):
                body(*index(k))
                return carry
            lax.fori_loop(0, n, step, 0)

    f32 = jnp.float32
    for p in range(3):
        start, width, half = PARTS[p]
        owns[p].wait()
        gives[p].wait_recv()
        sl = pl.ds(start, width)

        def body(k, carry, sl=sl):
            at = (k // 16, (k // 4) % 4, k % 4, slice(None), sl)
            acc[at] = (acc[at].astype(f32) + sibbuf[at].astype(f32)).astype(jnp.bfloat16)
            return carry
        lax.fori_loop(0, 64, body, 0)
        for which in (0, 1):
            cp = send_half(p, 0, which)
            cp.start()
            sends.append(cp)
    for ph in range(3):
        for p in range(3):
            start, width, half = PARTS[p]
            axis = axis_of(p, ph)
            for which, by, lo, w in ((0, 1, 0, half), (1, -1, half, width - half)):
                send_half(p, ph, which).wait_recv()
                sl = pl.ds(start + lo, w)

                def body(at, dig, ph=ph, sl=sl):
                    at = at + (slice(None), sl)
                    hat = dig + (slice(None), sl)
                    acc[at] = (acc[at].astype(f32) + hbufs[ph][hat].astype(f32)).astype(jnp.bfloat16)
                over(p, ph, (me[axis] + by + 4) % 4, body)
                cp = send_full(p, ph, which)
                cp.start()
                sends.append(cp)
        for p in range(3):
            start, width, half = PARTS[p]
            axis = axis_of(p, ph)
            for which in (0, 1):
                send_full(p, ph, which).wait_recv()
            sl = pl.ds(start, width)

            def body(at, dig, ph=ph, sl=sl):
                at = at + (slice(None), sl)
                total = (acc[at].astype(f32) + fbufs[ph][(0,) + dig + (slice(None), sl)].astype(f32)
                         + fbufs[ph][(1,) + dig + (slice(None), sl)].astype(f32))
                if ph < 2:
                    acc[at] = total.astype(jnp.bfloat16)
                else:
                    last[:, sl] = total
            over(p, ph, me[axis], body)
            if ph < 2:
                for which in (0, 1):
                    cp = send_half(p, ph + 1, which)
                    cp.start()
                    sends.append(cp)
    top, bottom = last[0:8, :], last[8:16, :]
    low[...] = jnp.where(core == 0, bottom, top)
    swap = pltpu.make_async_remote_copy(
        src_ref=low, dst_ref=fin, send_sem=e_sem.at[0], recv_sem=e_sem.at[1], device_id=sibling, device_id_type=MESH)
    swap.start()
    mine = jnp.where(core == 0, top, bottom)
    swap.wait()
    theirs = fin[...]
    out_ref[:, :HALFW] = jnp.where(core == 0, mine, theirs)
    out_ref[:, HALFW:] = jnp.where(core == 0, theirs, mine)
    for cp in sends + gives:
        cp.wait_send()


def scatter(g):
    bf = jnp.bfloat16
    return pl.pallas_call(
        scatter_kernel,
        out_shape=jax.ShapeDtypeStruct((8, WIDE), jnp.float32),
        in_specs=[pl.BlockSpec(memory_space=pl.ANY)],
        out_specs=pl.BlockSpec(memory_space=pltpu.VMEM),
        scratch_shapes=[
            pltpu.VMEM((4, 4, 4, 16, HALFW), bf),
            pltpu.VMEM((4, 4, 4, 16, HALFW), bf),
            pltpu.VMEM((4, 4, 16, HALFW), bf),
            pltpu.VMEM((4, 16, HALFW), bf),
            pltpu.VMEM((16, HALFW), bf),
            pltpu.VMEM((2, 4, 4, 16, HALFW), bf),
            pltpu.VMEM((2, 4, 16, HALFW), bf),
            pltpu.VMEM((2, 16, HALFW), bf),
            pltpu.VMEM((16, HALFW), jnp.float32),
            pltpu.VMEM((8, HALFW), jnp.float32),
            pltpu.VMEM((8, HALFW), jnp.float32),
            pltpu.SemaphoreType.DMA((3,)),
            pltpu.SemaphoreType.DMA((3,)),
            pltpu.SemaphoreType.DMA((3,)),
            pltpu.SemaphoreType.DMA((3, 3, 4)),
            pltpu.SemaphoreType.DMA((3, 3, 4)),
            pltpu.SemaphoreType.DMA((2,)),
        ],
        compiler_params=pltpu.CompilerParams(
            collective_id=1, has_side_effects=True, vmem_limit_bytes=32 << 20),
        name="scatter_grads",
    )(g)


EPS = 1e-05
HALF = 15
ROWS = 768
D = 1024
NFFT = 256


def tables():
    omega = 2 * np.pi * (np.arange(128) + 0.5) / NFFT
    phase = omega[:, None] * np.arange(NFFT)[None]
    basis = np.concatenate([np.cos(phase), -np.sin(phase)], axis=0)
    lag = omega[:, None] * (np.arange(31) - HALF)[None]
    spread = np.zeros((NFFT, 128))
    spread[:, :31] = np.concatenate([np.cos(lag), np.sin(lag)], axis=0) * (2 / NFFT)
    back = np.zeros((128, NFFT))
    back[:31] = np.concatenate([np.cos(lag), -np.sin(lag)], axis=0).T * (2 / NFFT)
    return (jnp.asarray(basis, jnp.bfloat16), jnp.asarray(spread, jnp.float32), jnp.asarray(back, jnp.float32))


def colours(ids):
    step = ids[HALF:] - ids[:-HALF]
    fwd_at, bwd_at = (0, 208, 416, 592), (16, 208, 400, 592)
    counts, rows = [], []
    for starts, length in ((fwd_at, 240), (bwd_at, 224)):
        for at in starts:
            count = jnp.max(step[at : at + length - HALF]) + 1
            counts.append(count)
            own = jnp.pad(ids[at : at + length] % count, (0, NFFT - length), constant_values=-1)
            rows.append(own)
    inner = jnp.arange(NFFT)
    for w in range(4):
        rows.append(jnp.where((inner >= 16) & (inner < 208), rows[4 + w], -1))
    table = jnp.stack(rows).astype(jnp.float32)
    return jnp.stack(counts).astype(jnp.int32), jnp.broadcast_to(table[:, None, :], (12, 8, NFFT))


def sigmoid(v):
    return 0.5 * jnp.tanh(0.5 * v) + 0.5


NT = (((1,), (1,)), ((), ()))
TN = (((0,), (0,)), ((), ()))
F32 = jnp.float32
BF = jnp.bfloat16


def nt(a, b):
    return lax.dot_general(a, b, NT, preferred_element_type=F32)


def mm(a, b):
    return jnp.dot(a, b, preferred_element_type=F32)


def row_mean(v):
    return jnp.sum(v, axis=-1, keepdims=True) * (1.0 / D)


def mid_kernel(
    counts, table, basis, spread, back, frames, cot, hf, hc, w_hbm,
    out_ref, igrad_ref, g_hbm,
    xe, ce, w, ln, glu, sig, mixed, work, act, dm, dpre, g, spec, prod, gains, extra, inv_in, mean_in, sems,
):
    scale = 1.0 / math.sqrt(98304.0)

    def cp(src, dst, n):
        c = pltpu.make_async_copy(src, dst, sems.at[n])
        c.start()
        return c

    loads = [
        cp(frames, xe.at[pl.ds(32, ROWS)], 0),
        cp(hf.at[pl.ds(0, 32)], xe.at[pl.ds(0, 32)], 1),
        cp(hf.at[pl.ds(32, 32)], xe.at[pl.ds(800, 32)], 2),
        cp(w_hbm, w, 3),
        cp(cot, ce.at[pl.ds(16, ROWS)], 4),
        cp(hc.at[pl.ds(0, 16)], ce.at[pl.ds(0, 16)], 5),
        cp(hc.at[pl.ds(16, 16)], ce.at[pl.ds(784, 16)], 6),
    ]
    loads[3].wait()
    taps = w[:, 3072:3200].astype(F32).T
    gains[0:8, :] = jnp.broadcast_to(taps[31:32, :], (8, D))
    gains[8:16, :] = jnp.broadcast_to(taps[32:33, :], (8, D))
    spec[...] = jnp.dot(spread[...], taps, precision=lax.Precision.HIGHEST, preferred_element_type=F32)
    glu[pl.ds(832, 16), :] = jnp.zeros((16, D), BF)
    dm[pl.ds(800, 32), :] = jnp.zeros((32, D), BF)
    prod[...] = jnp.zeros((NFFT, D), F32)
    extra[...] = jnp.zeros((128, D), F32)
    for n in (0, 1, 2):
        loads[n].wait()

    @pl.loop(0, 52)
    def _(i):
        at = pl.ds(pl.multiple_of(i * 16, 16), 16)
        x = xe[at, :].astype(F32)
        mean = row_mean(x)
        cen = x - mean
        inv = lax.rsqrt(row_mean(cen * cen) + EPS)
        ln[at, :] = (cen * inv * gains[0:1, :]).astype(BF)
        inv_in[at, :] = jnp.broadcast_to(inv, (16, 128))
        mean_in[at, :] = jnp.broadcast_to(mean, (16, 128))

    @pl.loop(0, 8)
    def _(i):
        j, r = i // 2, i % 2
        rows = pl.ds(pl.multiple_of(r * 416, 16), 416)
        c0 = pl.ds(pl.multiple_of(j * 256, 256), 256)
        c1 = pl.ds(pl.multiple_of(j * 256 + 1024, 256), 256)
        lhs = ln[rows, :]
        value = mm(lhs, w[:, c0])
        s = sigmoid(mm(lhs, w[:, c1]))
        glu[rows, c0] = (value * s).astype(BF)
        sig[rows, c0] = s

    for n in (4, 5, 6):
        loads[n].wait()

    def masked(row, c):
        hit = table[row, 0:1, :] == c.astype(F32)
        return jnp.where(hit, basis[...].astype(F32), 0.0).astype(BF)

    @pl.loop(0, 4)
    def _(wi):
        base = pl.multiple_of(jnp.minimum(wi * 208, 592), 16)
        mixed[pl.ds(base, 208), :] = jnp.zeros((208, D), F32)

        @pl.loop(0, counts[wi])
        def _(c):
            cm = masked(wi, c)
            inv = cm.T[16:224, :]
            for j in range(4):
                col = slice(j * 256, j * 256 + 256)
                x = mm(cm, glu[pl.ds(base, 256), col])
                xr, xi = x[:128], x[128:]
                hr, hi = spec[:128, col], spec[128:, col]
                y = jnp.concatenate([xr * hr - xi * hi, xr * hi + xi * hr], axis=0).astype(BF)
                mixed[pl.ds(base, 208), col] += mm(inv, y)

    @pl.loop(0, 4)
    def _(j):
        col = pl.ds(pl.multiple_of(j * 256, 256), 256)
        work[:, col] = nt(ce[...], w[col, 2048:3072])

    def mid_rows(i, central):
        at = pl.ds(pl.multiple_of(i * 16, 16), 16)
        gain = gains[8:9, :]
        m = mixed[at, :]
        cen = m - row_mean(m)
        inv = lax.rsqrt(row_mean(cen * cen) + EPS)
        normal = cen * inv
        y = normal * gain
        s = sigmoid(y)
        ys = y * s
        act[at, :] = ys.astype(BF)
        d_ln = work[at, :] * (s + ys * (1.0 - s))
        if central:
            dn = d_ln * normal
            extra[40:48, :] += dn[:8] + dn[8:]
        u = d_ln * gain
        dm[at, :] = (inv * (u - row_mean(u) - normal * row_mean(u * normal))).astype(BF)

    mid_rows(0, False)
    mid_rows(49, False)

    @pl.loop(1, 49)
    def _(i):
        mid_rows(i, True)

    @pl.loop(0, 4)
    def _(j):
        col = pl.ds(pl.multiple_of(j * 256, 256), 256)
        y = mm(act[16:784, :], w[:, pl.ds(pl.multiple_of(2048 + j * 256, 256), 256)])
        out_ref[:, col] = (xe[32:800, col].astype(F32) + y).astype(BF)
        lhs = act[16:784, col].T
        g[col, 2048:3072] = (mm(lhs, ce[16:784, :]) * scale).astype(BF)

    @pl.loop(0, 4)
    def _(wi):
        base = pl.multiple_of(wi * 192, 16)
        mixed[pl.ds(base, 192), :] = jnp.zeros((192, D), F32)

        @pl.loop(0, counts[4 + wi])
        def _(c):
            cm = masked(4 + wi, c)
            cg = masked(8 + wi, c)
            inv = cm.T[16:208, :]
            for j in range(4):
                col = slice(j * 256, j * 256 + 256)
                d = mm(cm, dm[pl.ds(base, 256), col])
                q = mm(cg, glu[pl.ds(base + 16, 256), col])
                dr, di, qr, qi = d[:128], d[128:], q[:128], q[128:]
                hr, hi = spec[:128, col], spec[128:, col]
                y = jnp.concatenate([dr * hr + di * hi, di * hr - dr * hi], axis=0).astype(BF)
                prod[:128, col] += qr * dr + qi * di
                prod[128:, col] += qi * dr - qr * di
                mixed[pl.ds(base, 192), col] += mm(inv, y)

    @pl.loop(0, 48)
    def _(i):
        at = pl.ds(pl.multiple_of(i * 16, 16), 16)
        ext = pl.ds(pl.multiple_of(i * 16 + 32, 16), 16)
        d = mixed[at, :]
        s = sig[ext, :]
        ds = d * s
        dpre[at, :1024] = ds.astype(BF)
        dpre[at, 1024:] = (d * glu[ext, :].astype(F32) * (1.0 - s)).astype(BF)

    @pl.loop(0, 4)
    def _(j):
        col = pl.ds(pl.multiple_of(j * 256, 256), 256)
        lhs = ln[32:800, col].T
        for n in range(4):
            cols = slice(n * 512, n * 512 + 512)
            g[col, cols] = (mm(lhs, dpre[:, cols]) * scale).astype(BF)
        work[0:768, col] = nt(dpre[...], w[col, 0:2048])

    @pl.loop(0, 48)
    def _(i):
        at = pl.ds(pl.multiple_of(i * 16, 16), 16)
        ext = pl.ds(pl.multiple_of(i * 16 + 32, 16), 16)
        inv = inv_in[ext, 0:1]
        normal = (xe[ext, :].astype(F32) - mean_in[ext, 0:1]) * inv
        d = work[at, :]
        dn = d * normal
        extra[48:56, :] += dn[:8] + dn[8:]
        u = d * gains[0:1, :]
        back_in = inv * (u - row_mean(u) - normal * row_mean(u * normal))
        c = ce[pl.ds(pl.multiple_of(i * 16 + 16, 16), 16), :].astype(F32)
        igrad_ref[at, :] = (c + back_in).astype(BF)

    gk = jnp.dot(back[...], prod[...], precision=lax.Precision.HIGHEST, preferred_element_type=F32)
    extra[0:31, :] = gk[0:31]
    g_mid = jnp.sum(extra[40:48, :], axis=0, keepdims=True)
    g_in = jnp.sum(extra[48:56, :], axis=0, keepdims=True)
    extra[31:32, :] = g_in
    extra[32:33, :] = g_mid
    g[:, 3072:3200] = (extra[...].T * scale).astype(BF)
    g[:, 3200:3328] = jnp.zeros((D, 128), BF)
    cp(g, g_hbm, 7).wait()


def mid(counts, table, consts, frames, cot, hf, hc, w):
    vm = pl.BlockSpec(memory_space=pltpu.VMEM)
    hbm = pl.BlockSpec(memory_space=pl.ANY)
    V = pltpu.VMEM
    return pl.pallas_call(
        mid_kernel,
        out_shape=(
            jax.ShapeDtypeStruct((ROWS, D), BF),
            jax.ShapeDtypeStruct((ROWS, D), BF),
            jax.ShapeDtypeStruct((D, WIDE), BF),
        ),
        in_specs=[pl.BlockSpec(memory_space=pltpu.SMEM), vm, vm, vm, vm, hbm, hbm, hbm, hbm, hbm],
        out_specs=(vm, vm, hbm),
        scratch_shapes=[
            V((832, D), BF), V((800, D), BF), V((D, WIDE), BF),
            V((832, D), BF), V((848, D), BF), V((832, D), F32),
            V((800, D), F32), V((800, D), F32), V((800, D), BF), V((832, D), BF),
            V((768, 2 * D), BF), V((D, WIDE), BF), V((NFFT, D), F32), V((NFFT, D), F32),
            V((16, D), F32), V((128, D), F32), V((832, 128), F32), V((832, 128), F32),
            pltpu.SemaphoreType.DMA((8,)),
        ],
        compiler_params=pltpu.CompilerParams(vmem_limit_bytes=60 << 20),
        name="block_pass",
    )(counts, table, *consts, frames, cot, hf, hc, w)


def shards(frames, cotangent, segments, w_in, w_out, kernel, gain_in, gain_mid):
    frame_rows = frames[0]
    cot_rows = cotangent[0]
    packed = jnp.concatenate(
        [w_in.astype(F32), w_out.astype(F32), kernel.astype(F32), gain_in.astype(F32)[:, None],
         gain_mid.astype(F32)[:, None], jnp.zeros((8, WIDE - 3072 - 33), F32)], axis=1)
    seg_rows = jnp.broadcast_to(segments[0].astype(BF)[:, None], (ROWS, 128))
    full, f_halo, c_halo, seg_halo = gather(packed, frame_rows, cot_rows, seg_rows)
    at = lax.axis_index("seq")
    halo = seg_halo[:, 0].astype(jnp.int32)
    own = segments[0]
    ids = jnp.concatenate([
        jnp.where(at == 0, own[0] - 1, halo[:HALO]), own, jnp.where(at == 7, own[-1] + 1, halo[HALO:])])
    counts, table = colours(ids)
    block_out, input_grad, g = mid(
        counts, table, tables(), frame_rows, cot_rows, f_halo, c_halo, full.reshape(1024, WIDE))
    r = scatter(g.reshape(4, 4, 4, 16, WIDE))
    return (block_out[None], input_grad[None], r[:, :2048], r[:, 2048:3072], r[:, 3072:3103], r[:, 3103], r[:, 3104])


def solution(mesh):
    rows = P("dp", "seq", None)
    mat = P(("dp", "seq"), None)
    vec = P(("dp", "seq"))
    return jax.shard_map(
        shards, mesh=mesh, in_specs=(rows, rows, P("dp", "seq"), mat, mat, mat, vec, vec),
        out_specs=(rows, rows, mat, mat, mat, vec, vec), check_vma=False)
```

```python
import math

import jax
import jax.numpy as jnp
import numpy as np
from jax import lax
from jax.experimental import pallas as pl
from jax.experimental.pallas import tpu as pltpu
from jax.sharding import PartitionSpec as P

MESH = pl.DeviceIdType.MESH
HALFW = 1664
WIDE = 2 * HALFW
PARTS = ((0, 512, 256), (512, 512, 256), (1024, 640, 384))
ORDERS = (("z", "x", "y"), ("x", "y", "z"), ("y", "z", "x"))
HALO = 32


def place():
    d, s = lax.axis_index("dp"), lax.axis_index("seq")
    return {"y": d // 4, "x": d % 4, "z": s // 2}, s % 2


def dev(coords, core):
    return (coords["y"] * 4 + coords["x"], coords["z"] * 2 + core)


def moved(coords, axis, by):
    out = dict(coords)
    out[axis] = (coords[axis] + by + 4) % 4
    return out


def greet(targets):
    barrier = pltpu.get_barrier_semaphore()
    for t in targets:
        pl.semaphore_signal(barrier, inc=1, device_id=t, device_id_type=MESH)
    pl.semaphore_wait(barrier, len(targets))


def block_index(coords, full, axis, value):
    out = []
    for a in ("y", "x", "z"):
        if a == axis:
            out.append(value)
        elif a in full:
            out.append(slice(None))
        else:
            out.append(coords[a])
    return tuple(out)


def gather_kernel(
    w_in_ref, w_out_ref, small_ref, seg_ref, frames_ref, cot_ref,
    out_ref, hf_ref, hc_ref, ids_ref,
    buf, shard, sib, segs, sib_sem, halo_send, halo_recv, a_send, a_recv, s_send, s_recv, out_sem,
):
    me, core = place()
    sibling = dev(me, 1 - core)
    seq = lax.axis_index("seq")
    right = (lax.axis_index("dp"), (seq + 1) % 8)
    left = (lax.axis_index("dp"), (seq + 7) % 8)
    cross = dev(moved(me, "z", 2 * core - 1), 1 - core)
    targets = [dev(moved(me, a, b), core) for a in "yxz" for b in (1, -1)]
    shard[:, 0:2048] = w_in_ref[...].astype(jnp.float32)
    shard[:, 2048:3072] = w_out_ref[...].astype(jnp.float32)
    shard[:, 3072:] = small_ref[...]
    greet(targets + [sibling, cross])

    first = pltpu.make_async_remote_copy(
        src_ref=shard, dst_ref=sib, send_sem=sib_sem.at[0], recv_sem=sib_sem.at[1],
        device_id=sibling, device_id_type=MESH)
    first.start()
    halos = []
    rows = frames_ref.shape[0]
    for n, (src, dst, h) in enumerate(((frames_ref, hf_ref, HALO), (cot_ref, hc_ref, 16))):
        for m, (at, to, who) in enumerate(((rows - h, 0, right), (0, h, left))):
            halos.append(pltpu.make_async_remote_copy(
                src_ref=src.at[pl.ds(at, h)], dst_ref=dst.at[pl.ds(to, h)],
                send_sem=halo_send.at[n, m], recv_sem=halo_recv.at[n, m],
                device_id=who, device_id_type=MESH))
    for m, who in enumerate((right, left)):
        halos.append(pltpu.make_async_remote_copy(
            src_ref=seg_ref, dst_ref=segs.at[m], send_sem=halo_send.at[2, m], recv_sem=halo_recv.at[2, m],
            device_id=who, device_id_type=MESH))
    first.wait()
    mine, other = shard[...], sib[...]
    low = jnp.where(core == 0, mine[:, :HALFW], other[:, HALFW:])
    high = jnp.where(core == 0, other[:, :HALFW], mine[:, HALFW:])
    buf[me["y"], me["x"], me["z"], :, pl.ds(pl.multiple_of(core * HALFW, 128), HALFW)] = jnp.concatenate(
        [low, high], axis=0).astype(jnp.bfloat16)
    for cp in halos:
        cp.start()

    def cols(p, lo, width, c=core):
        return pl.ds(pl.multiple_of(c * HALFW + PARTS[p][0] + lo, 128), width)

    def send(p, ph, which, idx, lo, width, by):
        axis = ORDERS[p][ph]
        ref = buf.at[idx + (slice(None), cols(p, lo, width))]
        return pltpu.make_async_remote_copy(
            src_ref=ref, dst_ref=ref, send_sem=a_send.at[p, ph, which], recv_sem=a_recv.at[p, ph, which],
            device_id=dev(moved(me, axis, by), core), device_id_type=MESH)

    def to_sibling(p, which, idx, c=core):
        start, width, _ = PARTS[p]
        ref = buf.at[idx + (slice(None), cols(p, 0, width, c))]
        return pltpu.make_async_remote_copy(
            src_ref=ref, dst_ref=ref, send_sem=s_send.at[p, which], recv_sem=s_recv.at[p, which],
            device_id=sibling, device_id_type=MESH)

    def block(p, ph, by):
        axis = ORDERS[p][ph]
        return block_index(me, ORDERS[p][:ph], axis, (me[axis] + by + 4) % 4)

    sends = []
    for ph in range(3):
        for p in range(3):
            _, width, half = PARTS[p]
            if ph > 0:
                opp = block(p, ph - 1, 2)
                send(p, ph - 1, 2, opp, 0, half, 1).wait_recv()
                send(p, ph - 1, 3, opp, half, width - half, -1).wait_recv()
            own = block(p, ph, 0)
            for which, by in ((0, 1), (1, -1)):
                cp = send(p, ph, which, own, 0, width, by)
                cp.start()
                sends.append(cp)
            if ph == 2:
                cp = to_sibling(p, 0, own)
                cp.start()
                sends.append(cp)
        for p in range(3):
            _, width, half = PARTS[p]
            for which, by, lo, w in ((0, -1, 0, half), (1, 1, half, width - half)):
                idx = block(p, ph, by)
                send(p, ph, which, idx, 0, width, -by).wait_recv()
                cp = send(p, ph, which + 2, idx, lo, w, -by)
                cp.start()
                sends.append(cp)
                if ph == 2:
                    cp = to_sibling(p, 1 + which, idx)
                    cp.start()
                    sends.append(cp)
    outs = []

    def flush(p, c, n):
        at = (slice(None),) * 4 + (cols(p, 0, PARTS[p][1], c),)
        cp = pltpu.make_async_copy(buf.at[at], out_ref.at[at], out_sem.at[p, n])
        cp.start()
        outs.append(cp)

    for p in range(3):
        _, width, half = PARTS[p]
        opp = block(p, 2, 2)
        send(p, 2, 2, opp, 0, half, 1).wait_recv()
        send(p, 2, 3, opp, half, width - half, -1).wait_recv()
        cp = to_sibling(p, 3, opp)
        cp.start()
        sends.append(cp)
        flush(p, core, 0)
    for cp in halos:
        cp.wait()
    own = seg_ref[...]
    before = jnp.where(seq == 0, jnp.broadcast_to(own[0:1, 0:1] - 1, (1, 128)), segs[0, 5:6, :])
    after = jnp.where(seq == 7, jnp.broadcast_to(own[5:6, 127:128] + 1, (1, 128)), segs[1, 0:1, :])
    ids_ref[...] = jnp.concatenate([before, own, after], axis=0).astype(jnp.float32)
    for p in range(3):
        for which, by in ((0, 0), (1, -1), (2, 1), (3, 2)):
            to_sibling(p, which, block(p, 2, by), 1 - core).wait_recv()
        flush(p, 1 - core, 1)
    for cp in sends:
        cp.wait_send()
    for cp in outs:
        cp.wait()


def gather(w_in, w_out, small, seg, frames, cot):
    bf = jnp.bfloat16
    vm = pl.BlockSpec(memory_space=pltpu.VMEM)
    hbm = pl.BlockSpec(memory_space=pltpu.HBM)
    return pl.pallas_call(
        gather_kernel,
        out_shape=(
            jax.ShapeDtypeStruct((4, 4, 4, 16, WIDE), bf),
            jax.ShapeDtypeStruct((2 * HALO, 1024), bf),
            jax.ShapeDtypeStruct((32, 1024), bf),
            jax.ShapeDtypeStruct((8, 128), jnp.float32),
        ),
        in_specs=[vm, vm, vm, vm, hbm, hbm],
        out_specs=(hbm, vm, vm, vm),
        scratch_shapes=[
            pltpu.VMEM((4, 4, 4, 16, WIDE), bf),
            pltpu.VMEM((8, WIDE), jnp.float32),
            pltpu.VMEM((8, WIDE), jnp.float32),
            pltpu.VMEM((2, 6, 128), jnp.int32),
            pltpu.SemaphoreType.DMA((2,)),
            pltpu.SemaphoreType.DMA((3, 2)),
            pltpu.SemaphoreType.DMA((3, 2)),
            pltpu.SemaphoreType.DMA((3, 3, 4)),
            pltpu.SemaphoreType.DMA((3, 3, 4)),
            pltpu.SemaphoreType.DMA((3, 4)),
            pltpu.SemaphoreType.DMA((3, 4)),
            pltpu.SemaphoreType.DMA((3, 2)),
        ],
        compiler_params=pltpu.CompilerParams(
            collective_id=0, has_side_effects=True, vmem_limit_bytes=48 << 20),
        name="gather_weights",
    )(w_in, w_out, small, seg, frames, cot)


def scatter_kernel(
    g_ref, out_ref,
    acc, sibbuf, h0, h1, h2, f0, f1, f2, last, low, fin, own_sem, d_send, d_recv, a_send, a_recv, e_sem,
):
    me, core = place()
    sibling = dev(me, 1 - core)
    targets = [dev(moved(me, a, b), core) for a in "yxz" for b in (1, -1)]
    greet(targets + [sibling])
    hbufs, fbufs = (h0, h1, h2), (f0, f1, f2)

    def cols(p, c):
        return pl.ds(pl.multiple_of(c * HALFW + PARTS[p][0], 128), PARTS[p][1])

    def lane(p, lo, w):
        return pl.ds(PARTS[p][0] + lo, w)

    full3 = (slice(None),) * 4
    owns, gives, sends = [], [], []
    for p in range(3):
        give = pltpu.make_async_remote_copy(
            src_ref=g_ref.at[full3 + (cols(p, 1 - core),)], dst_ref=sibbuf.at[full3 + (lane(p, 0, PARTS[p][1]),)],
            send_sem=d_send.at[p], recv_sem=d_recv.at[p], device_id=sibling, device_id_type=MESH)
        give.start()
        own = pltpu.make_async_copy(
            g_ref.at[full3 + (cols(p, core),)], acc.at[full3 + (lane(p, 0, PARTS[p][1]),)], own_sem.at[p])
        own.start()
        owns.append(own)
        gives.append(give)

    def axis_of(p, ph):
        return ORDERS[p][2 - ph]

    def rest(p, ph):
        return ORDERS[p][: 2 - ph]

    def block(p, ph, by):
        axis = axis_of(p, ph)
        return block_index(me, rest(p, ph), axis, (me[axis] + by + 4) % 4)

    def hview(p, ph, lo, w):
        nd = 2 - ph
        return hbufs[ph].at[(slice(None),) * nd + (slice(None), lane(p, lo, w))]

    def fview(p, ph, which, lo, w):
        nd = 2 - ph
        return fbufs[ph].at[(which,) + (slice(None),) * nd + (slice(None), lane(p, lo, w))]

    def send_half(p, ph, which):
        _, width, half = PARTS[p]
        lo, w, by = ((0, half, 1), (half, width - half, -1))[which]
        return pltpu.make_async_remote_copy(
            src_ref=acc.at[block(p, ph, 2) + (slice(None), lane(p, lo, w))], dst_ref=hview(p, ph, lo, w),
            send_sem=a_send.at[p, ph, which], recv_sem=a_recv.at[p, ph, which],
            device_id=dev(moved(me, axis_of(p, ph), by), core), device_id_type=MESH)

    def send_full(p, ph, which):
        _, width, _ = PARTS[p]
        by = (1, -1)[which]
        return pltpu.make_async_remote_copy(
            src_ref=acc.at[block(p, ph, by) + (slice(None), lane(p, 0, width))], dst_ref=fview(p, ph, which, 0, width),
            send_sem=a_send.at[p, ph, 2 + which], recv_sem=a_recv.at[p, ph, 2 + which],
            device_id=dev(moved(me, axis_of(p, ph), by), core), device_id_type=MESH)

    def over(p, ph, value_axis_index, body):
        names = rest(p, ph)
        axis = axis_of(p, ph)
        n = 4 ** len(names)

        def index(k):
            digits = [k // 4, k % 4][2 - len(names):] if names else []
            by_name = dict(zip([a for a in "yxz" if a in names], digits))
            at = []
            for a in "yxz":
                at.append(by_name[a] if a in by_name else (value_axis_index if a == axis else me[a]))
            return tuple(at), tuple(digits)

        if n == 1:
            body(*index(0))
        else:
            def step(k, carry):
                body(*index(k))
                return carry
            lax.fori_loop(0, n, step, 0)

    f32 = jnp.float32
    for p in range(3):
        start, width, half = PARTS[p]
        owns[p].wait()
        gives[p].wait_recv()
        sl = pl.ds(start, width)

        def body(k, carry, sl=sl):
            at = (k // 16, (k // 4) % 4, k % 4, slice(None), sl)
            acc[at] = (acc[at].astype(f32) + sibbuf[at].astype(f32)).astype(jnp.bfloat16)
            return carry
        lax.fori_loop(0, 64, body, 0)
        for which in (0, 1):
            cp = send_half(p, 0, which)
            cp.start()
            sends.append(cp)
    for ph in range(3):
        for p in range(3):
            start, width, half = PARTS[p]
            axis = axis_of(p, ph)
            for which, by, lo, w in ((0, 1, 0, half), (1, -1, half, width - half)):
                send_half(p, ph, which).wait_recv()
                sl = pl.ds(start + lo, w)

                def body(at, dig, ph=ph, sl=sl):
                    at = at + (slice(None), sl)
                    hat = dig + (slice(None), sl)
                    acc[at] = (acc[at].astype(f32) + hbufs[ph][hat].astype(f32)).astype(jnp.bfloat16)
                over(p, ph, (me[axis] + by + 4) % 4, body)
                cp = send_full(p, ph, which)
                cp.start()
                sends.append(cp)
        for p in range(3):
            start, width, half = PARTS[p]
            axis = axis_of(p, ph)
            for which in (0, 1):
                send_full(p, ph, which).wait_recv()
            sl = pl.ds(start, width)

            def body(at, dig, ph=ph, sl=sl):
                at = at + (slice(None), sl)
                total = (acc[at].astype(f32) + fbufs[ph][(0,) + dig + (slice(None), sl)].astype(f32)
                         + fbufs[ph][(1,) + dig + (slice(None), sl)].astype(f32))
                if ph < 2:
                    acc[at] = total.astype(jnp.bfloat16)
                else:
                    last[:, sl] = total
            over(p, ph, me[axis], body)
            if ph < 2:
                for which in (0, 1):
                    cp = send_half(p, ph + 1, which)
                    cp.start()
                    sends.append(cp)
    top, bottom = last[0:8, :], last[8:16, :]
    low[...] = jnp.where(core == 0, bottom, top)
    swap = pltpu.make_async_remote_copy(
        src_ref=low, dst_ref=fin, send_sem=e_sem.at[0], recv_sem=e_sem.at[1], device_id=sibling, device_id_type=MESH)
    swap.start()
    mine = jnp.where(core == 0, top, bottom)
    swap.wait()
    theirs = fin[...]
    out_ref[:, :HALFW] = jnp.where(core == 0, mine, theirs)
    out_ref[:, HALFW:] = jnp.where(core == 0, theirs, mine)
    for cp in sends + gives:
        cp.wait_send()


def scatter(g):
    bf = jnp.bfloat16
    return pl.pallas_call(
        scatter_kernel,
        out_shape=jax.ShapeDtypeStruct((8, WIDE), jnp.float32),
        in_specs=[pl.BlockSpec(memory_space=pltpu.HBM)],
        out_specs=pl.BlockSpec(memory_space=pltpu.VMEM),
        scratch_shapes=[
            pltpu.VMEM((4, 4, 4, 16, HALFW), bf),
            pltpu.VMEM((4, 4, 4, 16, HALFW), bf),
            pltpu.VMEM((4, 4, 16, HALFW), bf),
            pltpu.VMEM((4, 16, HALFW), bf),
            pltpu.VMEM((16, HALFW), bf),
            pltpu.VMEM((2, 4, 4, 16, HALFW), bf),
            pltpu.VMEM((2, 4, 16, HALFW), bf),
            pltpu.VMEM((2, 16, HALFW), bf),
            pltpu.VMEM((16, HALFW), jnp.float32),
            pltpu.VMEM((8, HALFW), jnp.float32),
            pltpu.VMEM((8, HALFW), jnp.float32),
            pltpu.SemaphoreType.DMA((3,)),
            pltpu.SemaphoreType.DMA((3,)),
            pltpu.SemaphoreType.DMA((3,)),
            pltpu.SemaphoreType.DMA((3, 3, 4)),
            pltpu.SemaphoreType.DMA((3, 3, 4)),
            pltpu.SemaphoreType.DMA((2,)),
        ],
        compiler_params=pltpu.CompilerParams(
            collective_id=1, has_side_effects=True, vmem_limit_bytes=48 << 20),
        name="scatter_grads",
    )(g)


EPS = 1e-05
HALF = 15
ROWS = 768
D = 1024
NFFT = 256


def tables():
    omega = 2 * np.pi * (np.arange(128) + 0.5) / NFFT
    phase = omega[:, None] * np.arange(NFFT)[None]
    basis = np.concatenate([np.cos(phase), -np.sin(phase)], axis=0)
    lag = omega[:, None] * (np.arange(31) - HALF)[None]
    spread = np.zeros((NFFT, 128))
    spread[:, :31] = np.concatenate([np.cos(lag), np.sin(lag)], axis=0) * (2 / NFFT)
    back = np.zeros((128, NFFT))
    back[:31] = np.concatenate([np.cos(lag), -np.sin(lag)], axis=0).T * (2 / NFFT)
    f32 = jnp.float32
    return (jnp.asarray(basis, f32), jnp.asarray(basis.T, f32), jnp.asarray(spread, f32), jnp.asarray(back, f32))


def sigmoid(v):
    return 0.5 * jnp.tanh(0.5 * v) + 0.5


NT = (((1,), (1,)), ((), ()))
TN = (((0,), (0,)), ((), ()))
F32 = jnp.float32
BF = jnp.bfloat16


def nt(a, b):
    return lax.dot_general(a, b, NT, preferred_element_type=F32)


def mm(a, b):
    return jnp.dot(a, b, preferred_element_type=F32)


def row_mean(v):
    return jnp.sum(v, axis=-1, keepdims=True) * (1.0 / D)


FWD_AT, BWD_AT = (0, 208, 416, 592), (16, 208, 400, 592)


def colours(ids, table, across):
    lane = lax.broadcasted_iota(jnp.int32, (1, 128), 1)
    wide = lax.broadcasted_iota(jnp.int32, (1, NFFT), 1)
    counts = []
    for n, at in enumerate(FWD_AT + BWD_AT):
        length = 240 if n < 4 else 224
        r, o = divmod(at + 96, 128)

        def piece(k, o=o):
            if o == 0:
                return ids[k : k + 1, :]
            first = pltpu.roll(ids[k : k + 1, :], 128 - o, 1)
            return jnp.where(lane < 128 - o, first, pltpu.roll(ids[min(k + 1, 7) : min(k + 1, 7) + 1, :], 128 - o, 1))

        own = jnp.concatenate([piece(r), piece(r + 1)], axis=1)
        step = jnp.where(wide < length - HALF, pltpu.roll(own, NFFT - HALF, 1) - own, 0.0)
        count = jnp.max(step) + 1.0
        own = own + 1.0
        own = own - count * jnp.floor((own + 0.5) / count)
        own = jnp.where(wide < length, own, -1.0)
        rows = jnp.broadcast_to(own, (8, NFFT))
        table[n] = rows
        across[n] = jnp.broadcast_to(rows.T[:, 0:1], (NFFT, 128))
        if n >= 4:
            table[n + 4] = jnp.where((wide >= 16) & (wide < 208), rows, -1.0)
        counts.append(count.astype(jnp.int32))
    return counts


def mid_kernel(
    ids, basis, turned, spread, back, frames, cot, hf, hc, w_hbm,
    out_hbm, igrad_hbm, g_hbm,
    xe, ce, w, ln, glu, sig, mixed, work, act, dm, dpre, g, spec, prod, gains, extra, inv_in, mean_in,
    table, across, counts, out, sems,
):
    scale = 1.0 / math.sqrt(98304.0)

    def cp(src, dst, n):
        c = pltpu.make_async_copy(src, dst, sems.at[n])
        c.start()
        return c

    cols = lambda lo, n: (slice(None), pl.ds(lo, n))
    loads = [
        cp(w_hbm.at[cols(3072, 256)], w.at[cols(3072, 256)], 0),
        cp(hf.at[pl.ds(0, 32)], xe.at[pl.ds(0, 32)], 1),
        cp(hf.at[pl.ds(32, 32)], xe.at[pl.ds(800, 32)], 2),
        cp(frames, xe.at[pl.ds(32, ROWS)], 3),
        cp(w_hbm.at[cols(0, 2048)], w.at[cols(0, 2048)], 4),
        cp(w_hbm.at[cols(2048, 1024)], w.at[cols(2048, 1024)], 5),
        cp(cot, ce.at[pl.ds(16, ROWS)], 6),
        cp(hc.at[pl.ds(0, 16)], ce.at[pl.ds(0, 16)], 7),
        cp(hc.at[pl.ds(16, 16)], ce.at[pl.ds(784, 16)], 8),
    ]
    for n, count in enumerate(colours(ids, table, across)):
        counts[n] = count
    loads[0].wait()
    taps = w[:, 3072:3200].astype(F32).T
    gains[0:8, :] = jnp.broadcast_to(taps[31:32, :], (8, D))
    gains[8:16, :] = jnp.broadcast_to(taps[32:33, :], (8, D))
    spec[...] = jnp.dot(spread[...], taps, precision=lax.Precision.HIGHEST, preferred_element_type=F32)
    glu[pl.ds(832, 16), :] = jnp.zeros((16, D), BF)
    dm[pl.ds(800, 32), :] = jnp.zeros((32, D), BF)
    prod[...] = jnp.zeros((NFFT, D), F32)
    extra[...] = jnp.zeros((128, D), F32)
    for n in (1, 2, 3):
        loads[n].wait()

    def strips(i, n, off=0):
        return [pl.ds(pl.multiple_of(i * (16 * n) + off + 16 * u, 16), 16) for u in range(n)]

    @pl.loop(0, 13)
    def _(i):
        ats = strips(i, 4)
        gain = gains[0:1, :]
        xs = [xe[at, :].astype(F32) for at in ats]
        means = [row_mean(x) for x in xs]
        cens = [x - m for x, m in zip(xs, means)]
        invs = [lax.rsqrt(row_mean(c * c) + EPS) for c in cens]
        for at, c, inv, m in zip(ats, cens, invs, means):
            ln[at, :] = (c * inv * gain).astype(BF)
            inv_in[at, :] = jnp.broadcast_to(inv, (16, 128))
            mean_in[at, :] = jnp.broadcast_to(m, (16, 128))

    loads[4].wait()

    @pl.loop(0, 8)
    def _(i):
        j, r = i // 2, i % 2
        rows = pl.ds(pl.multiple_of(r * 416, 16), 416)
        c0 = pl.ds(pl.multiple_of(j * 256, 256), 256)
        c1 = pl.ds(pl.multiple_of(j * 256 + 1024, 256), 256)
        lhs = ln[rows, :]
        value = mm(lhs, w[:, c0])
        s = sigmoid(mm(lhs, w[:, c1]))
        glu[rows, c0] = (value * s).astype(BF)
        sig[rows, c0] = s

    for n in (5, 6, 7, 8):
        loads[n].wait()

    def picked(row, first, k):
        return jnp.concatenate(
            [jnp.where(table[row, 0:1, :] == (first + c).astype(F32), basis[...], 0.0) for c in range(k)],
            axis=0).astype(BF)

    def placed(row, first, k, lo, hi):
        own = across[row, lo:hi, :]
        own = jnp.concatenate([own, own], axis=1)
        return jnp.concatenate(
            [jnp.where(own == (first + c).astype(F32), turned[lo:hi, :], 0.0) for c in range(k)], axis=1).astype(BF)

    def forward(wi, first, k, add):
        base = pl.multiple_of(jnp.minimum(wi * 208, 592), 16)
        to = picked(wi, first, k)
        fro = placed(wi, first, k, 16, 224)
        for j in range(4):
            col = slice(j * 256, j * 256 + 256)
            x = mm(to, glu[pl.ds(base, 256), col])
            hr, hi = spec[:128, col], spec[128:, col]
            ys = []
            for c in range(k):
                xr, xi = x[256 * c : 256 * c + 128], x[256 * c + 128 : 256 * c + 256]
                ys += [(xr * hr - xi * hi).astype(BF), (xr * hi + xi * hr).astype(BF)]
            y = mm(fro, jnp.concatenate(ys, axis=0))
            if add:
                mixed[pl.ds(base, 208), col] += y
            else:
                mixed[pl.ds(base, 208), col] = y

    def backward(wi, first, k, add):
        base = pl.multiple_of(wi * 192, 16)
        to = picked(4 + wi, first, k)
        mid_to = picked(8 + wi, first, k)
        fro = placed(4 + wi, first, k, 16, 208)
        for j in range(4):
            col = slice(j * 256, j * 256 + 256)
            d = mm(to, dm[pl.ds(base, 256), col])
            q = mm(mid_to, glu[pl.ds(base + 16, 256), col])
            hr, hi = spec[:128, col], spec[128:, col]
            ys = []
            pr, pi = prod[:128, col], prod[128:, col]
            for c in range(k):
                lo, mi, up = 256 * c, 256 * c + 128, 256 * c + 256
                dr, di, qr, qi = d[lo:mi], d[mi:up], q[lo:mi], q[mi:up]
                ys += [(dr * hr + di * hi).astype(BF), (di * hr - dr * hi).astype(BF)]
                pr = pr + (qr * dr + qi * di)
                pi = pi + (qi * dr - qr * di)
            prod[:128, col] = pr
            prod[128:, col] = pi
            y = mm(fro, jnp.concatenate(ys, axis=0))
            if add:
                mixed[pl.ds(base, 192), col] += y
            else:
                mixed[pl.ds(base, 192), col] = y

    def by_class(run, wi, count, length, step):
        zero = jnp.int32(0)

        @pl.when(count <= 2)
        def _():
            run(wi, zero, 2, False)

        @pl.when(count == 3)
        def _():
            run(wi, zero, 3, False)

        @pl.when(count > 3)
        def _():
            base = pl.multiple_of(jnp.minimum(wi * step, 592), 16)
            mixed[pl.ds(base, length), :] = jnp.zeros((length, D), F32)

            @pl.loop(0, (count + 3) // 4)
            def _(n):
                run(wi, n * 4, 4, True)

    @pl.loop(0, 4)
    def _(wi):
        by_class(forward, wi, counts[wi], 208, 208)

    @pl.loop(0, 4)
    def _(j):
        col = pl.ds(pl.multiple_of(j * 256, 256), 256)
        work[:, col] = nt(ce[...], w[col, 2048:3072])

    def mid_rows(ats, central):
        gain = gains[8:9, :]
        cens = [mixed[at, :] for at in ats]
        cens = [m - row_mean(m) for m in cens]
        invs = [lax.rsqrt(row_mean(c * c) + EPS) for c in cens]
        normals = [c * inv for c, inv in zip(cens, invs)]
        us = []
        for at, normal in zip(ats, normals):
            y = normal * gain
            s = sigmoid(y)
            ys = y * s
            act[at, :] = ys.astype(BF)
            d_ln = work[at, :] * (s + ys * (1.0 - s))
            if central:
                dn = d_ln * normal
                extra[40:48, :] += dn[:8] + dn[8:]
            us.append(d_ln * gain)
        m1 = [row_mean(u) for u in us]
        m2 = [row_mean(u * n) for u, n in zip(us, normals)]
        for at, inv, u, n, a, b in zip(ats, invs, us, normals, m1, m2):
            dm[at, :] = (inv * (u - a - n * b)).astype(BF)

    mid_rows([pl.ds(0, 16), pl.ds(784, 16)], False)

    @pl.loop(0, 24)
    def _(i):
        mid_rows(strips(i, 2, 16), True)

    @pl.loop(0, 4)
    def _(j):
        col = pl.ds(pl.multiple_of(j * 256, 256), 256)
        y = mm(act[16:784, :], w[:, pl.ds(pl.multiple_of(2048 + j * 256, 256), 256)])
        out[:, col] = (xe[32:800, col].astype(F32) + y).astype(BF)
        lhs = act[16:784, col].T
        g[col, 2048:3072] = (mm(lhs, ce[16:784, :]) * scale).astype(BF)

    stores = [cp(out, out_hbm, 9), cp(g.at[cols(2048, 1024)], g_hbm.at[cols(2048, 1024)], 10)]

    @pl.loop(0, 4)
    def _(wi):
        by_class(backward, wi, counts[4 + wi], 192, 192)

    @pl.loop(0, 48)
    def _(i):
        at = pl.ds(pl.multiple_of(i * 16, 16), 16)
        ext = pl.ds(pl.multiple_of(i * 16 + 32, 16), 16)
        d = mixed[at, :]
        s = sig[ext, :]
        ds = d * s
        dpre[at, :1024] = ds.astype(BF)
        dpre[at, 1024:] = (d * glu[ext, :].astype(F32) * (1.0 - s)).astype(BF)

    @pl.loop(0, 4)
    def _(j):
        col = pl.ds(pl.multiple_of(j * 256, 256), 256)
        lhs = ln[32:800, col].T
        for n in range(4):
            c = slice(n * 512, n * 512 + 512)
            g[col, c] = (mm(lhs, dpre[:, c]) * scale).astype(BF)

    stores.append(cp(g.at[cols(0, 2048)], g_hbm.at[cols(0, 2048)], 11))
    gk = jnp.dot(back[...], prod[...], precision=lax.Precision.HIGHEST, preferred_element_type=F32)
    extra[0:31, :] = gk[0:31]

    @pl.loop(0, 4)
    def _(j):
        col = pl.ds(pl.multiple_of(j * 256, 256), 256)
        work[0:768, col] = nt(dpre[...], w[col, 0:2048])

    stores[0].wait()

    @pl.loop(0, 12)
    def _(i):
        ats, exts, ces = strips(i, 4), strips(i, 4, 32), strips(i, 4, 16)
        invs = [inv_in[e, 0:1] for e in exts]
        normals = [(xe[e, :].astype(F32) - mean_in[e, 0:1]) * inv for e, inv in zip(exts, invs)]
        us = []
        gain = gains[0:1, :]
        total = None
        for at, normal in zip(ats, normals):
            d = work[at, :]
            dn = d * normal
            dn = dn[:8] + dn[8:]
            total = dn if total is None else total + dn
            us.append(d * gain)
        extra[48:56, :] += total
        m1 = [row_mean(u) for u in us]
        m2 = [row_mean(u * n) for u, n in zip(us, normals)]
        for at, c, inv, u, n, a, b in zip(ats, ces, invs, us, normals, m1, m2):
            out[at, :] = (ce[c, :].astype(F32) + inv * (u - a - n * b)).astype(BF)

    stores.append(cp(out, igrad_hbm, 12))
    g_mid = jnp.sum(extra[40:48, :], axis=0, keepdims=True)
    g_in = jnp.sum(extra[48:56, :], axis=0, keepdims=True)
    extra[31:32, :] = g_in
    extra[32:33, :] = g_mid
    g[:, 3072:3200] = (extra[...].T * scale).astype(BF)
    g[:, 3200:3328] = jnp.zeros((D, 128), BF)
    stores.append(cp(g.at[cols(3072, 256)], g_hbm.at[cols(3072, 256)], 13))
    for s in stores[1:]:
        s.wait()


def mid(ids, consts, frames, cot, hf, hc, w):
    vm = pl.BlockSpec(memory_space=pltpu.VMEM)
    hbm = pl.BlockSpec(memory_space=pltpu.HBM)
    V = pltpu.VMEM
    return pl.pallas_call(
        mid_kernel,
        out_shape=(
            jax.ShapeDtypeStruct((ROWS, D), BF),
            jax.ShapeDtypeStruct((ROWS, D), BF),
            jax.ShapeDtypeStruct((D, WIDE), BF),
        ),
        in_specs=[vm, vm, vm, vm, vm, hbm, hbm, hbm, hbm, hbm],
        out_specs=(hbm, hbm, hbm),
        scratch_shapes=[
            V((832, D), BF), V((800, D), BF), V((D, WIDE), BF),
            V((832, D), BF), V((848, D), BF), V((832, D), F32),
            V((800, D), F32), V((800, D), F32), V((800, D), BF), V((832, D), BF),
            V((768, 2 * D), BF), V((D, WIDE), BF), V((NFFT, D), F32), V((NFFT, D), F32),
            V((16, D), F32), V((128, D), F32), V((832, 128), F32), V((832, 128), F32),
            V((12, 8, NFFT), F32), V((8, NFFT, 128), F32), pltpu.SMEM((8,), jnp.int32), V((ROWS, D), BF),
            pltpu.SemaphoreType.DMA((14,)),
        ],
        compiler_params=pltpu.CompilerParams(vmem_limit_bytes=60 << 20),
        name="block_pass",
    )(ids, *consts, frames, cot, hf, hc, w)


def shards(frames, cotangent, segments, w_in, w_out, kernel, gain_in, gain_mid):
    small = jnp.concatenate(
        [kernel.astype(F32), gain_in.astype(F32)[:, None], gain_mid.astype(F32)[:, None], jnp.zeros((8, 223), F32)], axis=1)
    full, f_halo, c_halo, ids = gather(w_in, w_out, small, segments.reshape(6, 128), frames[0], cotangent[0])
    block_out, input_grad, g = mid(
        ids, tables(), frames[0], cotangent[0], f_halo, c_halo, full.reshape(D, WIDE))
    r = scatter(g.reshape(4, 4, 4, 16, WIDE))
    return (block_out[None], input_grad[None], r[:, :2048], r[:, 2048:3072], r[:, 3072:3103], r[:, 3103], r[:, 3104])


def solution(mesh):
    rows = P("dp", "seq", None)
    mat = P(("dp", "seq"), None)
    vec = P(("dp", "seq"))
    return jax.shard_map(
        shards, mesh=mesh, in_specs=(rows, rows, P("dp", "seq"), mat, mat, mat, vec, vec),
        out_specs=(rows, rows, mat, mat, mat, vec, vec), check_vma=False)
```

```python
import math

import jax
import jax.numpy as jnp
import numpy as np
from jax import lax
from jax.experimental import pallas as pl
from jax.experimental.pallas import tpu as pltpu
from jax.sharding import PartitionSpec as P

MESH = pl.DeviceIdType.MESH
HALFW = 1664
WIDE = 2 * HALFW
PARTS = ((0, 512, 256), (512, 512, 256), (1024, 640, 384))
ORDERS = (("z", "x", "y"), ("x", "y", "z"), ("y", "z", "x"))
HALO = 32


def place():
    d, s = lax.axis_index("dp"), lax.axis_index("seq")
    return {"y": d // 4, "x": d % 4, "z": s // 2}, s % 2


def dev(coords, core):
    return (coords["y"] * 4 + coords["x"], coords["z"] * 2 + core)


def moved(coords, axis, by):
    out = dict(coords)
    out[axis] = (coords[axis] + by + 4) % 4
    return out


def greet(targets):
    barrier = pltpu.get_barrier_semaphore()
    for t in targets:
        pl.semaphore_signal(barrier, inc=1, device_id=t, device_id_type=MESH)
    pl.semaphore_wait(barrier, len(targets))


def block_index(coords, full, axis, value):
    out = []
    for a in ("y", "x", "z"):
        if a == axis:
            out.append(value)
        elif a in full:
            out.append(slice(None))
        else:
            out.append(coords[a])
    return tuple(out)


def gather_kernel(
    w_in_ref, w_out_ref, small_ref, seg_ref, frames_ref, cot_ref,
    out_ref, hf_ref, hc_ref, ids_ref,
    buf, shard, sib, segs, sib_sem, halo_send, halo_recv, a_send, a_recv, s_send, s_recv, out_sem,
):
    me, core = place()
    sibling = dev(me, 1 - core)
    seq = lax.axis_index("seq")
    right = (lax.axis_index("dp"), (seq + 1) % 8)
    left = (lax.axis_index("dp"), (seq + 7) % 8)
    cross = dev(moved(me, "z", 2 * core - 1), 1 - core)
    targets = [dev(moved(me, a, b), core) for a in "yxz" for b in (1, -1, 2)]
    for c in (0, 1):
        at = c * HALFW
        shard[:, at : at + 1024] = w_in_ref[:, c * 1024 : c * 1024 + 1024].astype(jnp.float32)
        shard[:, at + 1024 : at + 1536] = w_out_ref[:, c * 512 : c * 512 + 512].astype(jnp.float32)
        shard[:, at + 1536 : at + HALFW] = small_ref[...] if c == 0 else jnp.zeros((8, 128), jnp.float32)
    greet(targets + [sibling, cross])

    first = pltpu.make_async_remote_copy(
        src_ref=shard, dst_ref=sib, send_sem=sib_sem.at[0], recv_sem=sib_sem.at[1],
        device_id=sibling, device_id_type=MESH)
    first.start()
    halos = []
    rows = frames_ref.shape[0]
    for n, (src, dst, h) in enumerate(((frames_ref, hf_ref, HALO), (cot_ref, hc_ref, 16))):
        for m, (at, to, who) in enumerate(((rows - h, 0, right), (0, h, left))):
            halos.append(pltpu.make_async_remote_copy(
                src_ref=src.at[pl.ds(at, h)], dst_ref=dst.at[pl.ds(to, h)],
                send_sem=halo_send.at[n, m], recv_sem=halo_recv.at[n, m],
                device_id=who, device_id_type=MESH))
    for m, who in enumerate((right, left)):
        halos.append(pltpu.make_async_remote_copy(
            src_ref=seg_ref, dst_ref=segs.at[m], send_sem=halo_send.at[2, m], recv_sem=halo_recv.at[2, m],
            device_id=who, device_id_type=MESH))
    first.wait()
    mine, other = shard[...], sib[...]
    low = jnp.where(core == 0, mine[:, :HALFW], other[:, HALFW:])
    high = jnp.where(core == 0, other[:, :HALFW], mine[:, HALFW:])
    buf[me["y"], me["x"], me["z"], :, pl.ds(pl.multiple_of(core * HALFW, 128), HALFW)] = jnp.concatenate(
        [low, high], axis=0).astype(jnp.bfloat16)
    for cp in halos:
        cp.start()

    def cols(p, lo, width, c=core):
        return pl.ds(pl.multiple_of(c * HALFW + PARTS[p][0] + lo, 128), width)

    def send(p, ph, which, idx, lo, width, by):
        axis = ORDERS[p][ph]
        ref = buf.at[idx + (slice(None), cols(p, lo, width))]
        return pltpu.make_async_remote_copy(
            src_ref=ref, dst_ref=ref, send_sem=a_send.at[p, ph, which], recv_sem=a_recv.at[p, ph, which],
            device_id=dev(moved(me, axis, by), core), device_id_type=MESH)

    def to_sibling(p, which, idx, c=core):
        start, width, _ = PARTS[p]
        ref = buf.at[idx + (slice(None), cols(p, 0, width, c))]
        return pltpu.make_async_remote_copy(
            src_ref=ref, dst_ref=ref, send_sem=s_send.at[p, which], recv_sem=s_recv.at[p, which],
            device_id=sibling, device_id_type=MESH)

    def block(p, ph, by):
        axis = ORDERS[p][ph]
        return block_index(me, ORDERS[p][:ph], axis, (me[axis] + by + 4) % 4)

    sends = []

    def go(cp):
        cp.start()
        sends.append(cp)

    for ph in range(2):
        for p in range(3):
            width = PARTS[p][1]
            if ph > 0:
                for which, by in ((0, -1), (1, 1), (2, 2)):
                    send(p, 0, which, block(p, 0, by), 0, width, by).wait_recv()
            for which, by in ((0, 1), (1, -1), (2, 2)):
                go(send(p, ph, which, block(p, ph, 0), 0, width, by))
    for p in range(3):
        width = PARTS[p][1]
        for which, by in ((0, -1), (1, 1), (2, 2)):
            send(p, 1, which, block(p, 1, by), 0, width, by).wait_recv()
        own = block(p, 2, 0)
        for which, by in ((0, 1), (1, -1)):
            go(send(p, 2, which, own, 0, width, by))
        go(to_sibling(p, 0, own))
    for p in range(3):
        _, width, half = PARTS[p]
        for which, by, lo, w in ((0, -1, 0, half), (1, 1, half, width - half)):
            idx = block(p, 2, by)
            send(p, 2, which, idx, 0, width, -by).wait_recv()
            go(send(p, 2, which + 2, idx, lo, w, -by))
            go(to_sibling(p, 1 + which, idx))
    outs = []

    def flush(p, c, n):
        at = (slice(None),) * 4 + (cols(p, 0, PARTS[p][1], c),)
        cp = pltpu.make_async_copy(buf.at[at], out_ref.at[at], out_sem.at[p, n])
        cp.start()
        outs.append(cp)

    for p in range(3):
        _, width, half = PARTS[p]
        opp = block(p, 2, 2)
        send(p, 2, 2, opp, 0, half, 1).wait_recv()
        send(p, 2, 3, opp, half, width - half, -1).wait_recv()
        cp = to_sibling(p, 3, opp)
        cp.start()
        sends.append(cp)
        flush(p, core, 0)
    for cp in halos:
        cp.wait()
    own = seg_ref[...]
    before = jnp.where(seq == 0, jnp.broadcast_to(own[0:1, 0:1] - 1, (1, 128)), segs[0, 5:6, :])
    after = jnp.where(seq == 7, jnp.broadcast_to(own[5:6, 127:128] + 1, (1, 128)), segs[1, 0:1, :])
    ids_ref[...] = jnp.concatenate([before, own, after], axis=0).astype(jnp.float32)
    for p in range(3):
        for which, by in ((0, 0), (1, -1), (2, 1), (3, 2)):
            to_sibling(p, which, block(p, 2, by), 1 - core).wait_recv()
        flush(p, 1 - core, 1)
    for cp in sends:
        cp.wait_send()
    for cp in outs:
        cp.wait()


def gather(w_in, w_out, small, seg, frames, cot):
    bf = jnp.bfloat16
    vm = pl.BlockSpec(memory_space=pltpu.VMEM)
    hbm = pl.BlockSpec(memory_space=pltpu.HBM)
    return pl.pallas_call(
        gather_kernel,
        out_shape=(
            jax.ShapeDtypeStruct((4, 4, 4, 16, WIDE), bf),
            jax.ShapeDtypeStruct((2 * HALO, 1024), bf),
            jax.ShapeDtypeStruct((32, 1024), bf),
            jax.ShapeDtypeStruct((8, 128), jnp.float32),
        ),
        in_specs=[vm, vm, vm, vm, hbm, hbm],
        out_specs=(hbm, vm, vm, vm),
        scratch_shapes=[
            pltpu.VMEM((4, 4, 4, 16, WIDE), bf),
            pltpu.VMEM((8, WIDE), jnp.float32),
            pltpu.VMEM((8, WIDE), jnp.float32),
            pltpu.VMEM((2, 6, 128), jnp.int32),
            pltpu.SemaphoreType.DMA((2,)),
            pltpu.SemaphoreType.DMA((3, 2)),
            pltpu.SemaphoreType.DMA((3, 2)),
            pltpu.SemaphoreType.DMA((3, 3, 4)),
            pltpu.SemaphoreType.DMA((3, 3, 4)),
            pltpu.SemaphoreType.DMA((3, 4)),
            pltpu.SemaphoreType.DMA((3, 4)),
            pltpu.SemaphoreType.DMA((3, 2)),
        ],
        compiler_params=pltpu.CompilerParams(
            collective_id=0, has_side_effects=True, vmem_limit_bytes=60 << 20),
        name="gather_weights",
    )(w_in, w_out, small, seg, frames, cot)


def back_kernel(
    early, ln_hbm, dpre_hbm, w_hbm, frames, cot, inv_hbm, mean_hbm, gains, w_rows, small,
    o_in, o_out, o_small, igrad_hbm,
    acc, sibbuf, gsend, h0, f0, f1, f2, last, low, fin,
    ln, turned, dpre, w, xe, ce, inv_in, mean_in, work, out,
    load_sem, d_send, d_recv, a_send, a_recv, e_sem,
):
    scale = 1.0 / math.sqrt(98304.0)
    f32, bf = jnp.float32, jnp.bfloat16
    me, core = place()
    sibling = dev(me, 1 - core)
    full4 = (slice(None),) * 4

    def cp(src, dst, n):
        c = pltpu.make_async_copy(src, dst, load_sem.at[n])
        c.start()
        return c

    def early_cols(c):
        return full4 + (pl.ds(pl.multiple_of(c * 640, 128), 640),)

    def lane(p, lo, w):
        return pl.ds(PARTS[p][0] + lo, w)

    loads = [
        cp(ln_hbm, ln, 0),
        cp(dpre_hbm, dpre, 1),
        cp(early.at[early_cols(core)], acc.at[full4 + (lane(2, 0, 640),)], 2),
        cp(w_hbm.at[:, pl.ds(0, 1024)], w.at[:, pl.ds(0, 1024)], 3),
        cp(w_hbm.at[:, pl.ds(HALFW, 1024)], w.at[:, pl.ds(1024, 1024)], 4),
        cp(frames, xe, 5),
        cp(cot, ce, 6),
        cp(inv_hbm, inv_in, 7),
        cp(mean_hbm, mean_in, 8),
    ]
    targets = [dev(moved(me, a, b), core) for a in "yxz" for b in (1, -1, 2)]
    greet(targets + [sibling])

    def give(p):
        src = early.at[early_cols(1 - core)] if p == 2 else gsend.at[full4 + (lane(p, 0, 512),)]
        return pltpu.make_async_remote_copy(
            src_ref=src, dst_ref=sibbuf.at[full4 + (lane(p, 0, PARTS[p][1]),)],
            send_sem=d_send.at[p], recv_sem=d_recv.at[p], device_id=sibling, device_id_type=MESH)

    sends = []

    def go(c):
        c.start()
        sends.append(c)

    def axis_of(p, ph):
        return ORDERS[p][2 - ph]

    def block(p, ph, by):
        axis = axis_of(p, ph)
        return block_index(me, ORDERS[p][: 2 - ph], axis, (me[axis] + by + 4) % 4)

    def landing(p, ph, which, lo, w):
        ref = (f0, f1, f2)[ph]
        return ref.at[(which,) + (slice(None),) * (2 - ph) + (slice(None), lane(p, lo, w))]

    def send_half(p, which):
        _, width, half = PARTS[p]
        lo, w, by = ((0, half, 1), (half, width - half, -1))[which]
        return pltpu.make_async_remote_copy(
            src_ref=acc.at[block(p, 0, 2) + (slice(None), lane(p, lo, w))],
            dst_ref=h0.at[(slice(None),) * 3 + (lane(p, lo, w),)],
            send_sem=a_send.at[p, 0, which], recv_sem=a_recv.at[p, 0, which],
            device_id=dev(moved(me, axis_of(p, 0), by), core), device_id_type=MESH)

    def send_full(p, ph, which):
        width = PARTS[p][1]
        by = (1, -1, 2)[which]
        return pltpu.make_async_remote_copy(
            src_ref=acc.at[block(p, ph, by) + (slice(None), lane(p, 0, width))], dst_ref=landing(p, ph, which, 0, width),
            send_sem=a_send.at[p, ph, 2 + which], recv_sem=a_recv.at[p, ph, 2 + which],
            device_id=dev(moved(me, axis_of(p, ph), by), core), device_id_type=MESH)

    def over(p, ph, value, body):
        axis, full = axis_of(p, ph), ORDERS[p][: 2 - ph]
        names = [a for a in "yxz" if a in full]

        def at(k):
            by_name = {axis: value}
            if len(names) == 2:
                by_name[names[0]] = k
                by_name[names[1]] = slice(None)
            elif len(names) == 1:
                by_name[names[0]] = slice(None)
            return tuple(by_name[a] if a in by_name else me[a] for a in "yxz")

        if len(names) == 2:
            @pl.loop(0, 4)
            def _(k):
                body(at(k), (k, slice(None)))
        else:
            body(at(0), (slice(None),) * len(names))

    def start_halves(p):
        for which in (0, 1):
            go(send_half(p, which))

    def pass_on(p):
        start, width, half = PARTS[p]
        axis = axis_of(p, 0)
        for which, by, lo, w in ((0, 1, 0, half), (1, -1, half, width - half)):
            send_half(p, which).wait_recv()
            sl = pl.ds(start + lo, w)

            def body(at, dig, sl=sl):
                at = at + (slice(None), sl)
                acc[at] = (acc[at].astype(f32) + h0[dig + (slice(None), sl)].astype(f32)).astype(bf)
            over(p, 0, (me[axis] + by + 4) % 4, body)
            go(send_full(p, 0, which))

    def take(p, ph):
        start, width, _ = PARTS[p]
        count = 2 if ph == 0 else 3
        ref = (f0, f1, f2)[ph]
        for which in range(count):
            send_full(p, ph, which).wait_recv()
        sl = pl.ds(start, width)

        def body(at, dig):
            at = at + (slice(None), sl)
            total = acc[at].astype(f32)
            for which in range(count):
                total = total + ref[(which,) + dig + (slice(None), sl)].astype(f32)
            if ph < 2:
                acc[at] = total.astype(bf)
            else:
                last[:, sl] = total
        over(p, ph, me[axis_of(p, ph)], body)
        if ph < 2:
            for which in range(3):
                go(send_full(p, ph + 1, which))

    def product(p, half, store):
        @pl.loop(0, 4)
        def _(y):
            lhs = turned[pl.ds(pl.multiple_of(y * 256, 256), 256), :]
            rhs = dpre[:, pl.ds(pl.multiple_of(half * 1024 + p * 512, 512), 512)]
            r = jnp.dot(lhs, rhs, preferred_element_type=f32) * scale
            store(y, r.reshape(4, 4, 16, 512))

    def for_sibling(p):
        def store(y, r):
            gsend[y, :, :, :, lane(p, 0, 512)] = r.astype(bf)
        product(p, 1 - core, store)
        go(give(p))

    def for_own(p):
        give(p).wait_recv()

        def store(y, r):
            acc[y, :, :, :, lane(p, 0, 512)] = (r + sibbuf[y, :, :, :, lane(p, 0, 512)].astype(f32)).astype(bf)
        product(p, core, store)
        start_halves(p)

    def input_product(j):
        col = slice(j * 256, j * 256 + 256)
        work[:, col] = lax.dot_general(dpre[...], w[col, :], (((1,), (1,)), ((), ())), preferred_element_type=f32)

    def input_rows(n):
        @pl.loop(3 * n, 3 * n + 3)
        def _(i):
            ats = [pl.ds(pl.multiple_of(i * 64 + 16 * u, 16), 16) for u in range(4)]
            gain = gains[0:1, :]
            invs = [inv_in[at, 0:1] for at in ats]
            normals = [(xe[at, :].astype(f32) - mean_in[at, 0:1]) * inv for at, inv in zip(ats, invs)]
            us = [work[at, :] * gain for at in ats]
            m1 = [row_mean(u) for u in us]
            m2 = [row_mean(u * n) for u, n in zip(us, normals)]
            for at, inv, u, n, a, b in zip(ats, invs, us, normals, m1, m2):
                out[at, :] = (ce[at, :].astype(f32) + inv * (u - a - n * b)).astype(bf)

    go(give(2))
    loads[0].wait()
    turned[...] = ln[...].T
    loads[1].wait()
    for_sibling(0)
    loads[2].wait()
    give(2).wait_recv()

    @pl.loop(0, 4)
    def _(y):
        at = (y, slice(None), slice(None), slice(None), lane(2, 0, 640))
        acc[at] = (acc[at].astype(f32) + sibbuf[at].astype(f32)).astype(bf)
    start_halves(2)
    for_sibling(1)
    for_own(0)
    pass_on(2)
    for_own(1)
    for n in (3, 4):
        loads[n].wait()
    input_product(0)
    pass_on(0)
    take(2, 0)
    input_product(1)
    pass_on(1)
    take(0, 0)
    input_product(2)
    take(2, 1)
    take(1, 0)
    input_product(3)
    take(0, 1)
    for n in (5, 6, 7, 8):
        loads[n].wait()
    input_rows(0)
    take(1, 1)
    input_rows(1)
    take(2, 2)
    input_rows(2)
    take(0, 2)
    input_rows(3)
    stores = [cp(out, igrad_hbm, 9)]
    take(1, 2)
    top, bottom = last[0:8, :], last[8:16, :]
    low[...] = jnp.where(core == 0, bottom, top)
    swap = pltpu.make_async_remote_copy(
        src_ref=low, dst_ref=fin, send_sem=e_sem.at[0], recv_sem=e_sem.at[1], device_id=sibling, device_id_type=MESH)
    swap.start()
    mine = jnp.where(core == 0, top, bottom)
    swap.wait()
    theirs = fin[...]
    total = jnp.zeros((8, 1), f32)
    for c in (0, 1):
        own = jnp.where(core == c, mine, theirs)
        o_in[:, c * 1024 : c * 1024 + 1024] = own[:, :1024]
        o_out[:, c * 512 : c * 512 + 512] = own[:, 1024:1536]
        rows = w_rows[:, c * 1024 : c * 1024 + 1024].astype(f32)
        total = total + jnp.sum(rows * own[:, :1024], axis=-1, keepdims=True)
        if c == 0:
            rest = own[:, 1536:]
    total = total / small[:, 31:32]
    lanes = lax.broadcasted_iota(jnp.int32, (8, 128), 1)
    o_small[...] = jnp.where(lanes == 31, total, rest)
    for c in sends:
        c.wait_send()
    for c in stores:
        c.wait()


def back(early, ln, dpre, w, frames, cot, inv, mean, gains, w_rows, small):
    bf, f32 = jnp.bfloat16, jnp.float32
    vm = pl.BlockSpec(memory_space=pltpu.VMEM)
    hbm = pl.BlockSpec(memory_space=pltpu.HBM)
    V = pltpu.VMEM
    return pl.pallas_call(
        back_kernel,
        out_shape=(
            jax.ShapeDtypeStruct((8, 2048), f32),
            jax.ShapeDtypeStruct((8, 1024), f32),
            jax.ShapeDtypeStruct((8, 128), f32),
            jax.ShapeDtypeStruct((768, 1024), bf),
        ),
        in_specs=[hbm] * 8 + [vm] * 3,
        out_specs=(vm, vm, vm, hbm),
        scratch_shapes=[
            V((4, 4, 4, 16, HALFW), bf),
            V((4, 4, 4, 16, HALFW), bf),
            V((4, 4, 4, 16, 1024), bf),
            V((4, 4, 16, HALFW), bf),
            V((2, 4, 4, 16, HALFW), bf),
            V((3, 4, 16, HALFW), bf),
            V((3, 16, HALFW), bf),
            V((16, HALFW), f32),
            V((8, HALFW), f32),
            V((8, HALFW), f32),
            V((768, 1024), bf),
            V((1024, 768), bf),
            V((768, 2048), bf),
            V((1024, 2048), bf),
            V((768, 1024), bf),
            V((768, 1024), bf),
            V((768, 128), f32),
            V((768, 128), f32),
            V((768, 1024), f32),
            V((768, 1024), bf),
            pltpu.SemaphoreType.DMA((10,)),
            pltpu.SemaphoreType.DMA((3,)),
            pltpu.SemaphoreType.DMA((3,)),
            pltpu.SemaphoreType.DMA((3, 3, 5)),
            pltpu.SemaphoreType.DMA((3, 3, 5)),
            pltpu.SemaphoreType.DMA((2,)),
        ],
        compiler_params=pltpu.CompilerParams(
            collective_id=1, has_side_effects=True, vmem_limit_bytes=60 << 20),
        name="back_and_scatter",
    )(early, ln, dpre, w, frames, cot, inv, mean, gains, w_rows, small)


EPS = 1e-05
HALF = 15
ROWS = 768
D = 1024
NFFT = 256


def tables():
    omega = 2 * np.pi * (np.arange(128) + 0.5) / NFFT
    phase = omega[:, None] * np.arange(NFFT)[None]
    basis = np.concatenate([np.cos(phase), -np.sin(phase)], axis=0)
    lag = omega[:, None] * (np.arange(31) - HALF)[None]
    spread = np.zeros((NFFT, 128))
    spread[:, :31] = np.concatenate([np.cos(lag), np.sin(lag)], axis=0) * (2 / NFFT)
    back = np.zeros((128, NFFT))
    back[:31] = np.concatenate([np.cos(lag), -np.sin(lag)], axis=0).T * (2 / NFFT)
    f32 = jnp.float32
    return (jnp.asarray(basis, f32), jnp.asarray(basis.T, f32), jnp.asarray(spread, f32), jnp.asarray(back, f32))


def sigmoid(v):
    return 0.5 * jnp.tanh(0.5 * v) + 0.5


NT = (((1,), (1,)), ((), ()))
TN = (((0,), (0,)), ((), ()))
F32 = jnp.float32
BF = jnp.bfloat16


def nt(a, b):
    return lax.dot_general(a, b, NT, preferred_element_type=F32)


def mm(a, b):
    return jnp.dot(a, b, preferred_element_type=F32)


def row_mean(v):
    return jnp.sum(v, axis=-1, keepdims=True) * (1.0 / D)


FWD_AT, BWD_AT = (0, 208, 416, 592), (16, 208, 400, 592)


def colours(ids, table, across):
    lane = lax.broadcasted_iota(jnp.int32, (1, 128), 1)
    wide = lax.broadcasted_iota(jnp.int32, (1, NFFT), 1)
    counts = []
    for n, at in enumerate(FWD_AT + BWD_AT):
        length = 240 if n < 4 else 224
        r, o = divmod(at + 96, 128)

        def piece(k, o=o):
            if o == 0:
                return ids[k : k + 1, :]
            first = pltpu.roll(ids[k : k + 1, :], 128 - o, 1)
            return jnp.where(lane < 128 - o, first, pltpu.roll(ids[min(k + 1, 7) : min(k + 1, 7) + 1, :], 128 - o, 1))

        own = jnp.concatenate([piece(r), piece(r + 1)], axis=1)
        step = jnp.where(wide < length - HALF, pltpu.roll(own, NFFT - HALF, 1) - own, 0.0)
        count = jnp.max(step) + 1.0
        own = own + 1.0
        own = own - count * jnp.floor((own + 0.5) / count)
        own = jnp.where(wide < length, own, -1.0)
        rows = jnp.broadcast_to(own, (8, NFFT))
        table[n] = rows
        across[n] = jnp.broadcast_to(rows.T[:, 0:1], (NFFT, 128))
        if n >= 4:
            table[n + 4] = jnp.where((wide >= 16) & (wide < 208), rows, -1.0)
        counts.append(count.astype(jnp.int32))
    return counts


def mid_kernel(
    ids, basis, turned, spread, back, frames, cot, hf, hc, w_hbm,
    out_hbm, ln_hbm, dpre_hbm, early_hbm, inv_hbm, mean_hbm, gains,
    xe, ce, w, ln, glu, sig, mixed, work, act, dm, dpre, g, spec, prod, extra, inv_in, mean_in,
    table, across, counts, out, sems,
):
    scale = 1.0 / math.sqrt(98304.0)

    def cp(src, dst, n):
        c = pltpu.make_async_copy(src, dst, sems.at[n])
        c.start()
        return c

    cols = lambda lo, n: (slice(None), pl.ds(lo, n))
    loads = [
        cp(w_hbm.at[cols(1536, 128)], w.at[cols(3072, 128)], 0),
        cp(hf.at[pl.ds(0, 32)], xe.at[pl.ds(0, 32)], 1),
        cp(hf.at[pl.ds(32, 32)], xe.at[pl.ds(800, 32)], 2),
        cp(frames, xe.at[pl.ds(32, ROWS)], 3),
        cp(w_hbm.at[cols(0, 1024)], w.at[cols(0, 1024)], 4),
        cp(w_hbm.at[cols(1664, 1024)], w.at[cols(1024, 1024)], 5),
        cp(cot, ce.at[pl.ds(16, ROWS)], 6),
        cp(hc.at[pl.ds(0, 16)], ce.at[pl.ds(0, 16)], 7),
        cp(hc.at[pl.ds(16, 16)], ce.at[pl.ds(784, 16)], 8),
        cp(w_hbm.at[cols(1024, 512)], w.at[cols(2048, 512)], 9),
        cp(w_hbm.at[cols(2688, 512)], w.at[cols(2560, 512)], 10),
    ]
    for n, count in enumerate(colours(ids, table, across)):
        counts[n] = count
    loads[0].wait()
    taps = w[:, 3072:3200].astype(F32).T
    gains[0:8, :] = jnp.broadcast_to(taps[31:32, :], (8, D))
    gains[8:16, :] = jnp.broadcast_to(taps[32:33, :], (8, D))
    spec[...] = jnp.dot(spread[...], taps, precision=lax.Precision.HIGHEST, preferred_element_type=F32)
    glu[pl.ds(832, 16), :] = jnp.zeros((16, D), BF)
    dm[pl.ds(800, 32), :] = jnp.zeros((32, D), BF)
    prod[...] = jnp.zeros((NFFT, D), F32)
    extra[...] = jnp.zeros((128, D), F32)
    for n in (1, 2, 3):
        loads[n].wait()

    def strips(i, n, off=0):
        return [pl.ds(pl.multiple_of(i * (16 * n) + off + 16 * u, 16), 16) for u in range(n)]

    @pl.loop(0, 13)
    def _(i):
        ats = strips(i, 4)
        gain = gains[0:1, :]
        xs = [xe[at, :].astype(F32) for at in ats]
        means = [row_mean(x) for x in xs]
        cens = [x - m for x, m in zip(xs, means)]
        invs = [lax.rsqrt(row_mean(c * c) + EPS) for c in cens]
        for at, c, inv, m in zip(ats, cens, invs, means):
            ln[at, :] = (c * inv * gain).astype(BF)
            inv_in[at, :] = jnp.broadcast_to(inv, (16, 128))
            mean_in[at, :] = jnp.broadcast_to(m, (16, 128))

    stores = [
        cp(ln.at[pl.ds(32, ROWS)], ln_hbm, 11),
        cp(inv_in.at[pl.ds(32, ROWS)], inv_hbm, 12),
        cp(mean_in.at[pl.ds(32, ROWS)], mean_hbm, 13),
    ]
    loads[4].wait()
    loads[5].wait()

    @pl.loop(0, 8)
    def _(i):
        j, r = i // 2, i % 2
        rows = pl.ds(pl.multiple_of(r * 416, 16), 416)
        c0 = pl.ds(pl.multiple_of(j * 256, 256), 256)
        c1 = pl.ds(pl.multiple_of(j * 256 + 1024, 256), 256)
        lhs = ln[rows, :]
        value = mm(lhs, w[:, c0])
        s = sigmoid(mm(lhs, w[:, c1]))
        glu[rows, c0] = (value * s).astype(BF)
        sig[rows, c0] = s

    for n in (6, 7, 8, 9, 10):
        loads[n].wait()

    def picked(row, first, k):
        return jnp.concatenate(
            [jnp.where(table[row, 0:1, :] == (first + c).astype(F32), basis[...], 0.0) for c in range(k)],
            axis=0).astype(BF)

    def placed(row, first, k, lo, hi):
        own = across[row, lo:hi, :]
        own = jnp.concatenate([own, own], axis=1)
        return jnp.concatenate(
            [jnp.where(own == (first + c).astype(F32), turned[lo:hi, :], 0.0) for c in range(k)], axis=1).astype(BF)

    def forward(wi, first, k, add):
        base = pl.multiple_of(jnp.minimum(wi * 208, 592), 16)
        to = picked(wi, first, k)
        fro = placed(wi, first, k, 16, 224)
        for j in range(4):
            col = slice(j * 256, j * 256 + 256)
            x = mm(to, glu[pl.ds(base, 256), col])
            hr, hi = spec[:128, col], spec[128:, col]
            ys = []
            for c in range(k):
                xr, xi = x[256 * c : 256 * c + 128], x[256 * c + 128 : 256 * c + 256]
                ys += [(xr * hr - xi * hi).astype(BF), (xr * hi + xi * hr).astype(BF)]
            y = mm(fro, jnp.concatenate(ys, axis=0))
            if add:
                mixed[pl.ds(base, 208), col] += y
            else:
                mixed[pl.ds(base, 208), col] = y

    def backward(wi, first, k, add):
        base = pl.multiple_of(wi * 192, 16)
        to = picked(4 + wi, first, k)
        mid_to = picked(8 + wi, first, k)
        fro = placed(4 + wi, first, k, 16, 208)
        for j in range(4):
            col = slice(j * 256, j * 256 + 256)
            d = mm(to, dm[pl.ds(base, 256), col])
            q = mm(mid_to, glu[pl.ds(base + 16, 256), col])
            hr, hi = spec[:128, col], spec[128:, col]
            ys = []
            pr, pi = prod[:128, col], prod[128:, col]
            for c in range(k):
                lo, mi, up = 256 * c, 256 * c + 128, 256 * c + 256
                dr, di, qr, qi = d[lo:mi], d[mi:up], q[lo:mi], q[mi:up]
                ys += [(dr * hr + di * hi).astype(BF), (di * hr - dr * hi).astype(BF)]
                pr = pr + (qr * dr + qi * di)
                pi = pi + (qi * dr - qr * di)
            prod[:128, col] = pr
            prod[128:, col] = pi
            y = mm(fro, jnp.concatenate(ys, axis=0))
            if add:
                mixed[pl.ds(base, 192), col] += y
            else:
                mixed[pl.ds(base, 192), col] = y

    def by_class(run, wi, count, length, step):
        zero = jnp.int32(0)

        @pl.when(count <= 2)
        def _():
            run(wi, zero, 2, False)

        @pl.when(count == 3)
        def _():
            run(wi, zero, 3, False)

        @pl.when(count > 3)
        def _():
            base = pl.multiple_of(jnp.minimum(wi * step, 592), 16)
            mixed[pl.ds(base, length), :] = jnp.zeros((length, D), F32)

            @pl.loop(0, (count + 3) // 4)
            def _(n):
                run(wi, n * 4, 4, True)

    @pl.loop(0, 4)
    def _(wi):
        by_class(forward, wi, counts[wi], 208, 208)

    @pl.loop(0, 4)
    def _(j):
        col = pl.ds(pl.multiple_of(j * 256, 256), 256)
        work[:, col] = nt(ce[...], w[col, 2048:3072])

    def mid_rows(ats, central):
        gain = gains[8:9, :]
        cens = [mixed[at, :] for at in ats]
        cens = [m - row_mean(m) for m in cens]
        invs = [lax.rsqrt(row_mean(c * c) + EPS) for c in cens]
        normals = [c * inv for c, inv in zip(cens, invs)]
        us = []
        for at, normal in zip(ats, normals):
            y = normal * gain
            s = sigmoid(y)
            ys = y * s
            act[at, :] = ys.astype(BF)
            d_ln = work[at, :] * (s + ys * (1.0 - s))
            if central:
                dn = d_ln * normal
                extra[40:48, :] += dn[:8] + dn[8:]
            us.append(d_ln * gain)
        m1 = [row_mean(u) for u in us]
        m2 = [row_mean(u * n) for u, n in zip(us, normals)]
        for at, inv, u, n, a, b in zip(ats, invs, us, normals, m1, m2):
            dm[at, :] = (inv * (u - a - n * b)).astype(BF)

    mid_rows([pl.ds(0, 16), pl.ds(784, 16)], False)

    @pl.loop(0, 24)
    def _(i):
        mid_rows(strips(i, 2, 16), True)

    @pl.loop(0, 4)
    def _(j):
        col = pl.ds(pl.multiple_of(j * 256, 256), 256)
        y = mm(act[16:784, :], w[:, pl.ds(pl.multiple_of(2048 + j * 256, 256), 256)])
        out[:, col] = (xe[32:800, col].astype(F32) + y).astype(BF)
        lhs = act[16:784, col].T
        r = (mm(lhs, ce[16:784, :]) * scale).astype(BF)
        g[col, 0:512] = r[:, :512]
        g[col, 640:1152] = r[:, 512:]

    stores.append(cp(out, out_hbm, 14))

    @pl.loop(0, 4)
    def _(wi):
        by_class(backward, wi, counts[4 + wi], 192, 192)

    gk = jnp.dot(back[...], prod[...], precision=lax.Precision.HIGHEST, preferred_element_type=F32)
    extra[0:31, :] = gk[0:31]
    g_mid = jnp.sum(extra[40:48, :], axis=0, keepdims=True)
    extra[32:33, :] = g_mid
    g[:, 512:640] = (extra[...].T * scale).astype(BF)
    g[:, 1152:1280] = jnp.zeros((D, 128), BF)
    stores.append(cp(g, early_hbm, 15))

    for q in range(4):
        @pl.loop(q * 6, q * 6 + 6)
        def _(i):
            for u in range(2):
                at = pl.ds(pl.multiple_of(i * 32 + 16 * u, 16), 16)
                ext = pl.ds(pl.multiple_of(i * 32 + 16 * u + 32, 16), 16)
                d = mixed[at, :]
                s = sig[ext, :]
                dpre[at, :1024] = (d * s).astype(BF)
                dpre[at, 1024:] = (d * glu[ext, :].astype(F32) * (1.0 - s)).astype(BF)

        part = pl.ds(q * 192, 192)
        stores.append(cp(dpre.at[part], dpre_hbm.at[part], 16 + q))
    for s in stores:
        s.wait()


def mid(ids, consts, frames, cot, hf, hc, w):
    vm = pl.BlockSpec(memory_space=pltpu.VMEM)
    hbm = pl.BlockSpec(memory_space=pltpu.HBM)
    V = pltpu.VMEM
    return pl.pallas_call(
        mid_kernel,
        out_shape=(
            jax.ShapeDtypeStruct((ROWS, D), BF),
            jax.ShapeDtypeStruct((ROWS, D), BF),
            jax.ShapeDtypeStruct((ROWS, 2 * D), BF),
            jax.ShapeDtypeStruct((D, 1280), BF),
            jax.ShapeDtypeStruct((ROWS, 128), F32),
            jax.ShapeDtypeStruct((ROWS, 128), F32),
            jax.ShapeDtypeStruct((16, D), F32),
        ),
        in_specs=[vm, vm, vm, vm, vm, hbm, hbm, hbm, hbm, hbm],
        out_specs=(hbm,) * 6 + (vm,),
        scratch_shapes=[
            V((832, D), BF), V((800, D), BF), V((D, 3200), BF),
            V((832, D), BF), V((848, D), BF), V((832, D), F32),
            V((800, D), F32), V((800, D), F32), V((800, D), BF), V((832, D), BF),
            V((768, 2 * D), BF), V((D, 1280), BF), V((NFFT, D), F32), V((NFFT, D), F32),
            V((128, D), F32), V((832, 128), F32), V((832, 128), F32),
            V((12, 8, NFFT), F32), V((8, NFFT, 128), F32), pltpu.SMEM((8,), jnp.int32), V((ROWS, D), BF),
            pltpu.SemaphoreType.DMA((20,)),
        ],
        compiler_params=pltpu.CompilerParams(vmem_limit_bytes=60 << 20),
        name="block_pass",
    )(ids, *consts, frames, cot, hf, hc, w)


def shards(frames, cotangent, segments, w_in, w_out, kernel, gain_in, gain_mid):
    small = jnp.concatenate(
        [kernel.astype(F32), gain_in.astype(F32)[:, None], gain_mid.astype(F32)[:, None], jnp.zeros((8, 95), F32)], axis=1)
    x, cot = frames[0], cotangent[0]
    full, f_halo, c_halo, ids = gather(w_in, w_out, small, segments.reshape(6, 128), x, cot)
    full = full.reshape(D, WIDE)
    block_out, ln, dpre, early, inv, mean, gains = mid(ids, tables(), x, cot, f_halo, c_halo, full)
    g_in, g_out, g_small, input_grad = back(
        early.reshape(4, 4, 4, 16, 1280), ln, dpre, full, x, cot, inv, mean, gains, w_in, small)
    return (block_out[None], input_grad[None], g_in, g_out, g_small[:, :31], g_small[:, 31], g_small[:, 32])


def solution(mesh):
    rows = P("dp", "seq", None)
    mat = P(("dp", "seq"), None)
    vec = P(("dp", "seq"))
    return jax.shard_map(
        shards, mesh=mesh, in_specs=(rows, rows, P("dp", "seq"), mat, mat, mat, vec, vec),
        out_specs=(rows, rows, mat, mat, mat, vec, vec), check_vma=False)
```

```python
import math

import jax
import jax.numpy as jnp
import numpy as np
from jax import lax
from jax.experimental import pallas as pl
from jax.experimental.pallas import tpu as pltpu
from jax.sharding import PartitionSpec as P

MESH = pl.DeviceIdType.MESH
HALFW = 1664
WIDE = 2 * HALFW
PARTS = ((0, 384), (384, 384), (768, 256), (1024, 128), (1152, 256), (1408, 256))
FIRST, SECOND = (0, 1, 2), (3, 4, 5)
ORDERS = (("z", "x", "y"), ("x", "y", "z"), ("y", "z", "x")) * 2
HALO = 32


def place():
    d, s = lax.axis_index("dp"), lax.axis_index("seq")
    return {"y": d // 4, "x": d % 4, "z": s // 2}, s % 2


def dev(coords, core):
    return (coords["y"] * 4 + coords["x"], coords["z"] * 2 + core)


def moved(coords, axis, by):
    out = dict(coords)
    out[axis] = (coords[axis] + by + 4) % 4
    return out


def greet(targets):
    for t in targets:
        pl.semaphore_signal(pltpu.get_barrier_semaphore(), inc=1, device_id=t, device_id_type=MESH)


def greeted(targets):
    pl.semaphore_wait(pltpu.get_barrier_semaphore(), len(targets))


def half_of(index, which):
    at = [isinstance(i, slice) for i in index].index(True)
    return index[:at] + (pl.ds(2 * which, 2),) + index[at + 1 :]


def block_index(coords, full, axis, value):
    out = []
    for a in ("y", "x", "z"):
        if a == axis:
            out.append(value)
        elif a in full:
            out.append(slice(None))
        else:
            out.append(coords[a])
    return tuple(out)


def gather_kernel(
    w_in_ref, w_out_ref, kern_ref, gain_ref, seg_ref, frames_ref, cot_ref,
    out_ref, hf_ref, hc_ref, ids_ref,
    buf, shard, sib, segs, sib_sem, halo_send, halo_recv, a_send, a_recv, s_send, s_recv, out_sem,
):
    me, core = place()
    f32, bf = jnp.float32, jnp.bfloat16
    sibling = dev(me, 1 - core)
    seq = lax.axis_index("seq")
    right = (lax.axis_index("dp"), (seq + 1) % 8)
    left = (lax.axis_index("dp"), (seq + 7) % 8)
    cross = dev(moved(me, "z", 2 * core - 1), 1 - core)
    targets = [dev(moved(me, a, b), core) for a in "yxz" for b in (1, -1, 2)] + [sibling, cross]
    greet(targets)
    for c in (0, 1):
        at = c * HALFW
        shard[:, at : at + 1024] = w_in_ref[:, c * 1024 : c * 1024 + 1024].astype(f32)
        shard[:, at + 1024 : at + 1536] = w_out_ref[:, c * 512 : c * 512 + 512].astype(f32)
        shard[:, at + 1536 : at + HALFW] = jnp.zeros((8, 128), f32)
    shard[:, 1536 : 1536 + 31] = kern_ref[...].astype(f32)
    eye = lax.broadcasted_iota(jnp.int32, (8, 8), 0) == lax.broadcasted_iota(jnp.int32, (8, 8), 1)
    for n in (0, 1):
        row = jnp.broadcast_to(gain_ref[n : n + 1, :], (8, 8))
        shard[:, 1567 + n : 1568 + n] = jnp.sum(jnp.where(eye, row, 0.0), axis=1, keepdims=True)
    greeted(targets)

    first = pltpu.make_async_remote_copy(
        src_ref=shard, dst_ref=sib, send_sem=sib_sem.at[0], recv_sem=sib_sem.at[1],
        device_id=sibling, device_id_type=MESH)
    first.start()
    halos = []
    rows = frames_ref.shape[0]
    for n, (src, dst, h) in enumerate(((frames_ref, hf_ref, HALO), (cot_ref, hc_ref, 16))):
        for m, (at, to, who) in enumerate(((rows - h, 0, right), (0, h, left))):
            halos.append(pltpu.make_async_remote_copy(
                src_ref=src.at[pl.ds(at, h)], dst_ref=dst.at[pl.ds(to, h)],
                send_sem=halo_send.at[n, m], recv_sem=halo_recv.at[n, m],
                device_id=who, device_id_type=MESH))
    for m, who in enumerate((right, left)):
        halos.append(pltpu.make_async_remote_copy(
            src_ref=seg_ref, dst_ref=segs.at[m], send_sem=halo_send.at[2, m], recv_sem=halo_recv.at[2, m],
            device_id=who, device_id_type=MESH))
    first.wait()
    mine, other = shard[...], sib[...]
    low = jnp.where(core == 0, mine[:, :HALFW], other[:, HALFW:])
    high = jnp.where(core == 0, other[:, :HALFW], mine[:, HALFW:])
    buf[me["y"], me["x"], me["z"], :, pl.ds(pl.multiple_of(core * HALFW, 128), HALFW)] = jnp.concatenate(
        [low, high], axis=0).astype(bf)

    def cols(p, c=core):
        return pl.ds(pl.multiple_of(c * HALFW + PARTS[p][0], 128), PARTS[p][1])

    def send(p, ph, which, idx, by):
        axis = ORDERS[p][ph]
        ref = buf.at[idx + (slice(None), cols(p))]
        return pltpu.make_async_remote_copy(
            src_ref=ref, dst_ref=ref, send_sem=a_send.at[p, ph, which], recv_sem=a_recv.at[p, ph, which],
            device_id=dev(moved(me, axis, by), core), device_id_type=MESH)

    def to_sibling(p, which, idx, c=core):
        ref = buf.at[idx + (slice(None), cols(p, c))]
        return pltpu.make_async_remote_copy(
            src_ref=ref, dst_ref=ref, send_sem=s_send.at[p, which], recv_sem=s_recv.at[p, which],
            device_id=sibling, device_id_type=MESH)

    def block(p, ph, by):
        axis = ORDERS[p][ph]
        return block_index(me, ORDERS[p][:ph], axis, (me[axis] + by + 4) % 4)

    sends, outs = [], []

    def go(cp):
        cp.start()
        sends.append(cp)

    def start(p, ph):
        if ph > 0:
            for which, by in ((0, -1), (1, 1), (2, 2)):
                send(p, ph - 1, which, block(p, ph - 1, by), by).wait_recv()
        own = block(p, ph, 0)
        for which, by in ((0, 1), (1, -1), (2, 2))[: 3 if ph < 2 else 2]:
            go(send(p, ph, which, own, by))
        if ph == 2:
            go(to_sibling(p, 0, own))

    def pass_on(p):
        for which, by in ((0, -1), (1, 1)):
            idx = block(p, 2, by)
            send(p, 2, which, idx, -by).wait_recv()
            go(send(p, 2, which + 2, half_of(idx, which), -by))
            go(to_sibling(p, 1 + which, idx))

    def flush(p, c, n):
        at = (slice(None),) * 4 + (cols(p, c),)
        cp = pltpu.make_async_copy(buf.at[at], out_ref.at[at], out_sem.at[p, n])
        cp.start()
        outs.append(cp)

    def finish(p):
        idx = block(p, 2, 2)
        for which in (0, 1):
            send(p, 2, 2 + which, half_of(idx, which), 1).wait_recv()
        go(to_sibling(p, 3, idx))
        flush(p, core, 0)

    def from_sibling(p):
        for which, by in ((0, 0), (1, -1), (2, 1), (3, 2)):
            to_sibling(p, which, block(p, 2, by), 1 - core).wait_recv()
        flush(p, 1 - core, 1)

    for ph in (0, 1):
        for p in FIRST + SECOND:
            start(p, ph)
            if ph == 0 and p == 2:
                for cp in halos:
                    cp.start()
    for p in FIRST:
        start(p, 2)
    for p in FIRST:
        pass_on(p)
    for p in SECOND:
        start(p, 2)
    for p in FIRST:
        finish(p)
    for cp in halos:
        cp.wait()
    own = seg_ref[...]
    before = jnp.where(seq == 0, jnp.broadcast_to(own[:, 0:1] - 1, (1, 128)), segs[0, :, 640:768])
    after = jnp.where(seq == 7, jnp.broadcast_to(own[:, 767:768] + 1, (1, 128)), segs[1, :, 0:128])
    ids_ref[...] = jnp.concatenate(
        [before] + [own[:, n * 128 : n * 128 + 128] for n in range(6)] + [after], axis=0).astype(f32)
    for p in SECOND:
        pass_on(p)
    for p in FIRST:
        from_sibling(p)
    for p in SECOND:
        finish(p)
    for p in SECOND:
        from_sibling(p)
    for cp in sends:
        cp.wait_send()
    for cp in outs:
        cp.wait()


def gather(w_in, w_out, kern, gain, seg, frames, cot):
    bf = jnp.bfloat16
    vm = pl.BlockSpec(memory_space=pltpu.VMEM)
    hbm = pl.BlockSpec(memory_space=pltpu.HBM)
    return pl.pallas_call(
        gather_kernel,
        out_shape=(
            jax.ShapeDtypeStruct((4, 4, 4, 16, WIDE), bf),
            jax.ShapeDtypeStruct((2 * HALO, 1024), bf),
            jax.ShapeDtypeStruct((32, 1024), bf),
            jax.ShapeDtypeStruct((8, 128), jnp.float32),
        ),
        in_specs=[vm, vm, vm, vm, vm, hbm, hbm],
        out_specs=(hbm, vm, vm, vm),
        scratch_shapes=[
            pltpu.VMEM((4, 4, 4, 16, WIDE), bf),
            pltpu.VMEM((8, WIDE), jnp.float32),
            pltpu.VMEM((8, WIDE), jnp.float32),
            pltpu.VMEM((2, 1, 768), jnp.int32),
            pltpu.SemaphoreType.DMA((2,)),
            pltpu.SemaphoreType.DMA((3, 2)),
            pltpu.SemaphoreType.DMA((3, 2)),
            pltpu.SemaphoreType.DMA((6, 3, 4)),
            pltpu.SemaphoreType.DMA((6, 3, 4)),
            pltpu.SemaphoreType.DMA((6, 4)),
            pltpu.SemaphoreType.DMA((6, 4)),
            pltpu.SemaphoreType.DMA((6, 2)),
        ],
        compiler_params=pltpu.CompilerParams(
            collective_id=0, has_side_effects=True, vmem_limit_bytes=60 << 20),
        name="gather_weights",
    )(w_in, w_out, kern, gain, seg, frames, cot)


def back_kernel(
    early, ln_hbm, dpre_hbm, w_hbm, frames, cot, inv_hbm, mean_hbm, gains, w_rows, gain,
    o_in, o_out, o_kern, o_vec, out,
    acc, sibbuf, gsend, h0, f0, f1, f2, last, low, fin,
    ln, turned, dpre, w, xe, ce, inv_in, mean_in, work,
    load_sem, d_send, d_recv, a_send, a_recv, e_sem,
):
    scale = 1.0 / math.sqrt(98304.0)
    f32, bf = jnp.float32, jnp.bfloat16
    me, core = place()
    sibling = dev(me, 1 - core)
    full4 = (slice(None),) * 4

    def cp(src, dst, n):
        c = pltpu.make_async_copy(src, dst, load_sem.at[n])
        c.start()
        return c

    def early_cols(c):
        return full4 + (pl.ds(pl.multiple_of(c * 640, 128), 640),)

    def lanes(p):
        return pl.ds(*PARTS[p])

    later = pl.ds(1024, 640)

    loads = [
        cp(ln_hbm, ln, 0),
        cp(dpre_hbm, dpre, 1),
        cp(early.at[early_cols(core)], acc.at[full4 + (later,)], 2),
        cp(w_hbm.at[:, pl.ds(0, 1024)], w.at[:, pl.ds(0, 1024)], 3),
        cp(w_hbm.at[:, pl.ds(HALFW, 1024)], w.at[:, pl.ds(1024, 1024)], 4),
        cp(frames, xe, 5),
        cp(cot, ce, 6),
        cp(inv_hbm, inv_in, 7),
        cp(mean_hbm, mean_in, 8),
    ]
    targets = [dev(moved(me, a, b), core) for a in "yxz" for b in (1, -1, 2)] + [sibling]
    greet(targets)

    def give(p):
        src = early.at[early_cols(1 - core)] if p == 3 else gsend.at[full4 + (lanes(p),)]
        return pltpu.make_async_remote_copy(
            src_ref=src, dst_ref=sibbuf.at[full4 + (later if p == 3 else lanes(p),)],
            send_sem=d_send.at[p], recv_sem=d_recv.at[p], device_id=sibling, device_id_type=MESH)

    sends = []

    def go(c):
        c.start()
        sends.append(c)

    def axis_of(p, ph):
        return ORDERS[p][2 - ph]

    def block(p, ph, by):
        axis = axis_of(p, ph)
        return block_index(me, ORDERS[p][: 2 - ph], axis, (me[axis] + by + 4) % 4)

    def send_half(p, which):
        return pltpu.make_async_remote_copy(
            src_ref=acc.at[half_of(block(p, 0, 2), which) + (slice(None), lanes(p))],
            dst_ref=h0.at[pl.ds(2 * which, 2), :, :, lanes(p)],
            send_sem=a_send.at[p, 0, which], recv_sem=a_recv.at[p, 0, which],
            device_id=dev(moved(me, axis_of(p, 0), (1, -1)[which]), core), device_id_type=MESH)

    def send_full(p, ph, which):
        by = (1, -1, 2)[which]
        dst = (f0, f1, f2)[ph].at[(which,) + (slice(None),) * (3 - ph) + (lanes(p),)]
        return pltpu.make_async_remote_copy(
            src_ref=acc.at[block(p, ph, by) + (slice(None), lanes(p))], dst_ref=dst,
            send_sem=a_send.at[p, ph, 2 + which], recv_sem=a_recv.at[p, ph, 2 + which],
            device_id=dev(moved(me, axis_of(p, ph), by), core), device_id_type=MESH)

    def over(p, ph, value, body, span=(0, 4)):
        axis, full = axis_of(p, ph), ORDERS[p][: 2 - ph]
        names = [a for a in "yxz" if a in full]

        def at(k):
            by_name = {axis: value}
            if len(names) == 2:
                by_name[names[0]] = k
                by_name[names[1]] = slice(None)
            elif len(names) == 1:
                by_name[names[0]] = slice(None)
            return tuple(by_name[a] if a in by_name else me[a] for a in "yxz")

        if len(names) == 2:
            @pl.loop(*span)
            def _(k):
                body(at(k), (k, slice(None)))
        else:
            body(at(0), (slice(None),) * len(names))

    def start_halves(p):
        for which in (0, 1):
            go(send_half(p, which))

    def pass_on(p):
        axis = axis_of(p, 0)
        for which, by in ((0, 1), (1, -1)):
            send_half(p, which).wait_recv()

            def body(at, dig):
                at = at + (slice(None), lanes(p))
                acc[at] = (acc[at].astype(f32) + h0[dig + (slice(None), lanes(p))].astype(f32)).astype(bf)
            over(p, 0, (me[axis] + by + 4) % 4, body, (2 * which, 2 * which + 2))
            go(send_full(p, 0, which))

    def take(p, ph):
        count = 2 if ph == 0 else 3
        ref = (f0, f1, f2)[ph]
        for which in range(count):
            send_full(p, ph, which).wait_recv()
        sl = lanes(p)

        def body(at, dig):
            at = at + (slice(None), sl)
            total = acc[at].astype(f32)
            for which in range(count):
                total = total + ref[(which,) + dig + (slice(None), sl)].astype(f32)
            if ph < 2:
                acc[at] = total.astype(bf)
            else:
                last[:, sl] = total
        over(p, ph, me[axis_of(p, ph)], body)
        if ph < 2:
            for which in range(3):
                go(send_full(p, ph + 1, which))

    def product(p, half, store):
        at, width = PARTS[p]

        @pl.loop(0, 4)
        def _(y):
            lhs = turned[pl.ds(pl.multiple_of(y * 256, 256), 256), :]
            rhs = dpre[:, pl.ds(pl.multiple_of(half * 1024 + at, 128), width)]
            r = jnp.dot(lhs, rhs, preferred_element_type=f32) * scale
            store(y, r.reshape(4, 4, 16, width))

    def for_sibling(p):
        def store(y, r):
            gsend[y, :, :, :, lanes(p)] = r.astype(bf)
        product(p, 1 - core, store)

    def for_own(p):
        give(p).wait_recv()

        def store(y, r):
            acc[y, :, :, :, lanes(p)] = (r + sibbuf[y, :, :, :, lanes(p)].astype(f32)).astype(bf)
        product(p, core, store)
        start_halves(p)

    def input_product(j):
        col = slice(j * 256, j * 256 + 256)
        work[:, col] = lax.dot_general(dpre[...], w[col, :], (((1,), (1,)), ((), ())), preferred_element_type=f32)

    def input_rows(n):
        @pl.loop(3 * n, 3 * n + 3)
        def _(i):
            ats = [pl.ds(pl.multiple_of(i * 64 + 16 * u, 16), 16) for u in range(4)]
            gain = gains[0:1, :]
            invs = [inv_in[at, 0:1] for at in ats]
            normals = [(xe[at, :].astype(f32) - mean_in[at, 0:1]) * inv for at, inv in zip(ats, invs)]
            us = [work[at, :] * gain for at in ats]
            m1 = [row_mean(u) for u in us]
            m2 = [row_mean(u * n) for u, n in zip(us, normals)]
            for at, inv, u, n, a, b in zip(ats, invs, us, normals, m1, m2):
                out[at, :] = (ce[at, :].astype(f32) + inv * (u - a - n * b)).astype(bf)

    loads[0].wait()
    turned[...] = ln[...].T
    loads[1].wait()
    for_sibling(0)
    greeted(targets)
    go(give(3))
    go(give(0))
    for_sibling(1)
    go(give(1))
    loads[2].wait()
    give(3).wait_recv()

    @pl.loop(0, 4)
    def _(y):
        at = (y, slice(None), slice(None), slice(None), later)
        acc[at] = (acc[at].astype(f32) + sibbuf[at].astype(f32)).astype(bf)
    for p in SECOND:
        start_halves(p)
    for_sibling(2)
    go(give(2))
    for_own(0)
    for p in SECOND:
        pass_on(p)
    for_own(1)
    for_own(2)
    pass_on(0)
    for n in (3, 4):
        loads[n].wait()
    input_product(0)
    pass_on(1)
    pass_on(2)
    for p in SECOND:
        take(p, 0)
    input_product(1)
    take(0, 0)
    input_product(2)
    for p in SECOND:
        take(p, 1)
    take(1, 0)
    take(2, 0)
    input_product(3)
    for n in (5, 6, 7, 8):
        loads[n].wait()
    take(0, 1)
    for p in SECOND:
        take(p, 2)
    input_rows(0)
    take(1, 1)
    take(2, 1)
    input_rows(1)
    take(0, 2)
    input_rows(2)
    take(1, 2)
    take(2, 2)
    top, bottom = last[0:8, :], last[8:16, :]
    low[...] = jnp.where(core == 0, bottom, top)
    swap = pltpu.make_async_remote_copy(
        src_ref=low, dst_ref=fin, send_sem=e_sem.at[0], recv_sem=e_sem.at[1], device_id=sibling, device_id_type=MESH)
    swap.start()
    input_rows(3)
    mine = jnp.where(core == 0, top, bottom)
    swap.wait()
    theirs = fin[...]
    total = jnp.zeros((8, 1), f32)
    for c in (0, 1):
        own = jnp.where(core == c, mine, theirs)
        o_in[:, c * 1024 : c * 1024 + 1024] = own[:, :1024]
        o_out[:, c * 512 : c * 512 + 512] = own[:, 1024:1536]
        rows = w_rows[:, c * 1024 : c * 1024 + 1024].astype(f32)
        total = total + jnp.sum(rows * own[:, :1024], axis=-1, keepdims=True)
        if c == 0:
            rest = own[:, 1536:]
    eye = lax.broadcasted_iota(jnp.int32, (8, 8), 0) == lax.broadcasted_iota(jnp.int32, (8, 8), 1)
    column = jnp.sum(jnp.where(eye, jnp.broadcast_to(gain[0:1, :], (8, 8)), 0.0), axis=1, keepdims=True)
    o_kern[...] = rest[:, 0:31]
    pair = []
    for v in (total / column, rest[:, 32:33]):
        pair.append(jnp.sum(jnp.where(eye, jnp.broadcast_to(v, (8, 8)), 0.0), axis=0, keepdims=True))
    o_vec[...] = jnp.concatenate(pair, axis=0)
    for c in sends:
        c.wait_send()


def back(early, ln, dpre, w, frames, cot, inv, mean, gains, w_rows, gain):
    bf, f32 = jnp.bfloat16, jnp.float32
    vm = pl.BlockSpec(memory_space=pltpu.VMEM)
    hbm = pl.BlockSpec(memory_space=pltpu.HBM)
    V = pltpu.VMEM
    return pl.pallas_call(
        back_kernel,
        out_shape=(
            jax.ShapeDtypeStruct((8, 2048), f32),
            jax.ShapeDtypeStruct((8, 1024), f32),
            jax.ShapeDtypeStruct((8, 31), f32),
            jax.ShapeDtypeStruct((2, 8), f32),
            jax.ShapeDtypeStruct((768, 1024), bf),
        ),
        in_specs=[hbm] * 8 + [vm] * 3,
        out_specs=(vm, vm, vm, vm, vm),
        scratch_shapes=[
            V((4, 4, 4, 16, HALFW), bf),
            V((4, 4, 4, 16, HALFW), bf),
            V((4, 4, 4, 16, 1024), bf),
            V((4, 4, 16, HALFW), bf),
            V((2, 4, 4, 16, HALFW), bf),
            V((3, 4, 16, HALFW), bf),
            V((3, 16, HALFW), bf),
            V((16, HALFW), f32),
            V((8, HALFW), f32),
            V((8, HALFW), f32),
            V((768, 1024), bf),
            V((1024, 768), bf),
            V((768, 2048), bf),
            V((1024, 2048), bf),
            V((768, 1024), bf),
            V((768, 1024), bf),
            V((768, 128), f32),
            V((768, 128), f32),
            V((768, 1024), f32),
            pltpu.SemaphoreType.DMA((10,)),
            pltpu.SemaphoreType.DMA((4,)),
            pltpu.SemaphoreType.DMA((4,)),
            pltpu.SemaphoreType.DMA((6, 3, 5)),
            pltpu.SemaphoreType.DMA((6, 3, 5)),
            pltpu.SemaphoreType.DMA((2,)),
        ],
        compiler_params=pltpu.CompilerParams(
            collective_id=1, has_side_effects=True, vmem_limit_bytes=60 << 20),
        name="back_and_scatter",
    )(early, ln, dpre, w, frames, cot, inv, mean, gains, w_rows, gain)


EPS = 1e-05
HALF = 15
ROWS = 768
D = 1024
NFFT = 256


def tables():
    omega = 2 * np.pi * (np.arange(128) + 0.5) / NFFT
    phase = omega[:, None] * np.arange(NFFT)[None]
    basis = np.concatenate([np.cos(phase), -np.sin(phase)], axis=0)
    lag = omega[:, None] * (np.arange(31) - HALF)[None]
    spread = np.zeros((NFFT, 128))
    spread[:, :31] = np.concatenate([np.cos(lag), np.sin(lag)], axis=0) * (2 / NFFT)
    back = np.zeros((128, NFFT))
    back[:31] = np.concatenate([np.cos(lag), -np.sin(lag)], axis=0).T * (2 / NFFT)
    f32 = jnp.float32
    return (jnp.asarray(basis, f32), jnp.asarray(basis.T, f32), jnp.asarray(spread, f32), jnp.asarray(back, f32))


def sigmoid(v):
    return 0.5 * jnp.tanh(0.5 * v) + 0.5


NT = (((1,), (1,)), ((), ()))
TN = (((0,), (0,)), ((), ()))
F32 = jnp.float32
BF = jnp.bfloat16


def nt(a, b):
    return lax.dot_general(a, b, NT, preferred_element_type=F32)


def mm(a, b):
    return jnp.dot(a, b, preferred_element_type=F32)


def row_mean(v):
    return jnp.sum(v, axis=-1, keepdims=True) * (1.0 / D)


FWD_AT, BWD_AT = (0, 208, 416, 592), (16, 208, 400, 592)


def colours(ids, table, across):
    lane = lax.broadcasted_iota(jnp.int32, (1, 128), 1)
    wide = lax.broadcasted_iota(jnp.int32, (1, NFFT), 1)
    counts = []
    for n, at in enumerate(FWD_AT + BWD_AT):
        length = 240 if n < 4 else 224
        r, o = divmod(at + 96, 128)

        def piece(k, o=o):
            if o == 0:
                return ids[k : k + 1, :]
            first = pltpu.roll(ids[k : k + 1, :], 128 - o, 1)
            return jnp.where(lane < 128 - o, first, pltpu.roll(ids[min(k + 1, 7) : min(k + 1, 7) + 1, :], 128 - o, 1))

        own = jnp.concatenate([piece(r), piece(r + 1)], axis=1)
        step = jnp.where(wide < length - HALF, pltpu.roll(own, NFFT - HALF, 1) - own, 0.0)
        count = jnp.max(step) + 1.0
        own = own + 1.0
        own = own - count * jnp.floor((own + 0.5) / count)
        own = jnp.where(wide < length, own, -1.0)
        rows = jnp.broadcast_to(own, (8, NFFT))
        table[n] = rows
        across[n] = jnp.broadcast_to(rows.T[:, 0:1], (NFFT, 128))
        if n >= 4:
            table[n + 4] = jnp.where((wide >= 16) & (wide < 208), rows, -1.0)
        counts.append(count.astype(jnp.int32))
    return counts


def mid_kernel(
    ids, basis, turned, spread, back, frames, cot, hf, hc, w_hbm,
    out_hbm, ln_hbm, dpre_hbm, early_hbm, inv_hbm, mean_hbm, gains,
    xe, ce, w, ln, glu, sig, mixed, work, act, dm, dpre, g, spec, prod, extra, inv_in, mean_in,
    table, across, counts, out, sems,
):
    scale = 1.0 / math.sqrt(98304.0)

    def cp(src, dst, n):
        c = pltpu.make_async_copy(src, dst, sems.at[n])
        c.start()
        return c

    cols = lambda lo, n: (slice(None), pl.ds(lo, n))
    loads = [
        cp(w_hbm.at[cols(1536, 128)], w.at[cols(3072, 128)], 0),
        cp(hf.at[pl.ds(0, 32)], xe.at[pl.ds(0, 32)], 1),
        cp(hf.at[pl.ds(32, 32)], xe.at[pl.ds(800, 32)], 2),
        cp(frames, xe.at[pl.ds(32, ROWS)], 3),
        cp(w_hbm.at[cols(0, 1024)], w.at[cols(0, 1024)], 4),
        cp(w_hbm.at[cols(1664, 1024)], w.at[cols(1024, 1024)], 5),
        cp(cot, ce.at[pl.ds(16, ROWS)], 6),
        cp(hc.at[pl.ds(0, 16)], ce.at[pl.ds(0, 16)], 7),
        cp(hc.at[pl.ds(16, 16)], ce.at[pl.ds(784, 16)], 8),
        cp(w_hbm.at[cols(1024, 512)], w.at[cols(2048, 512)], 9),
        cp(w_hbm.at[cols(2688, 512)], w.at[cols(2560, 512)], 10),
    ]
    for n, count in enumerate(colours(ids, table, across)):
        counts[n] = count
    loads[0].wait()
    taps = w[:, 3072:3200].astype(F32).T
    gains[0:8, :] = jnp.broadcast_to(taps[31:32, :], (8, D))
    gains[8:16, :] = jnp.broadcast_to(taps[32:33, :], (8, D))
    spec[...] = jnp.dot(spread[...], taps, precision=lax.Precision.HIGHEST, preferred_element_type=F32)
    glu[pl.ds(832, 16), :] = jnp.zeros((16, D), BF)
    dm[pl.ds(800, 32), :] = jnp.zeros((32, D), BF)
    prod[...] = jnp.zeros((NFFT, D), F32)
    extra[...] = jnp.zeros((128, D), F32)
    for n in (1, 2, 3):
        loads[n].wait()

    def strips(i, n, off=0):
        return [pl.ds(pl.multiple_of(i * (16 * n) + off + 16 * u, 16), 16) for u in range(n)]

    @pl.loop(0, 13)
    def _(i):
        ats = strips(i, 4)
        gain = gains[0:1, :]
        xs = [xe[at, :].astype(F32) for at in ats]
        means = [row_mean(x) for x in xs]
        cens = [x - m for x, m in zip(xs, means)]
        invs = [lax.rsqrt(row_mean(c * c) + EPS) for c in cens]
        for at, c, inv, m in zip(ats, cens, invs, means):
            ln[at, :] = (c * inv * gain).astype(BF)
            inv_in[at, :] = jnp.broadcast_to(inv, (16, 128))
            mean_in[at, :] = jnp.broadcast_to(m, (16, 128))

    stores = [
        cp(ln.at[pl.ds(32, ROWS)], ln_hbm, 11),
        cp(inv_in.at[pl.ds(32, ROWS)], inv_hbm, 12),
        cp(mean_in.at[pl.ds(32, ROWS)], mean_hbm, 13),
    ]
    loads[4].wait()
    loads[5].wait()

    @pl.loop(0, 8)
    def _(i):
        j, r = i // 2, i % 2
        rows = pl.ds(pl.multiple_of(r * 416, 16), 416)
        c0 = pl.ds(pl.multiple_of(j * 256, 256), 256)
        c1 = pl.ds(pl.multiple_of(j * 256 + 1024, 256), 256)
        lhs = ln[rows, :]
        value = mm(lhs, w[:, c0])
        s = sigmoid(mm(lhs, w[:, c1]))
        glu[rows, c0] = (value * s).astype(BF)
        sig[rows, c0] = s

    for n in (6, 7, 8, 9, 10):
        loads[n].wait()

    def picked(row, first, k):
        return jnp.concatenate(
            [jnp.where(table[row, 0:1, :] == (first + c).astype(F32), basis[...], 0.0) for c in range(k)],
            axis=0).astype(BF)

    def placed(row, first, k, lo, hi):
        own = across[row, lo:hi, :]
        own = jnp.concatenate([own, own], axis=1)
        return jnp.concatenate(
            [jnp.where(own == (first + c).astype(F32), turned[lo:hi, :], 0.0) for c in range(k)], axis=1).astype(BF)

    def forward(wi, first, k, add):
        base = pl.multiple_of(jnp.minimum(wi * 208, 592), 16)
        to = picked(wi, first, k)
        fro = placed(wi, first, k, 16, 224)
        for j in range(4):
            col = slice(j * 256, j * 256 + 256)
            x = mm(to, glu[pl.ds(base, 256), col])
            hr, hi = spec[:128, col], spec[128:, col]
            ys = []
            for c in range(k):
                xr, xi = x[256 * c : 256 * c + 128], x[256 * c + 128 : 256 * c + 256]
                ys += [(xr * hr - xi * hi).astype(BF), (xr * hi + xi * hr).astype(BF)]
            y = mm(fro, jnp.concatenate(ys, axis=0))
            if add:
                mixed[pl.ds(base, 208), col] += y
            else:
                mixed[pl.ds(base, 208), col] = y

    def backward(wi, first, k, add):
        base = pl.multiple_of(wi * 192, 16)
        to = picked(4 + wi, first, k)
        mid_to = picked(8 + wi, first, k)
        fro = placed(4 + wi, first, k, 16, 208)
        for j in range(4):
            col = slice(j * 256, j * 256 + 256)
            d = mm(to, dm[pl.ds(base, 256), col])
            q = mm(mid_to, glu[pl.ds(base + 16, 256), col])
            hr, hi = spec[:128, col], spec[128:, col]
            ys = []
            pr, pi = prod[:128, col], prod[128:, col]
            for c in range(k):
                lo, mi, up = 256 * c, 256 * c + 128, 256 * c + 256
                dr, di, qr, qi = d[lo:mi], d[mi:up], q[lo:mi], q[mi:up]
                ys += [(dr * hr + di * hi).astype(BF), (di * hr - dr * hi).astype(BF)]
                pr = pr + (qr * dr + qi * di)
                pi = pi + (qi * dr - qr * di)
            prod[:128, col] = pr
            prod[128:, col] = pi
            y = mm(fro, jnp.concatenate(ys, axis=0))
            if add:
                mixed[pl.ds(base, 192), col] += y
            else:
                mixed[pl.ds(base, 192), col] = y

    def by_class(run, wi, count, length, step):
        zero = jnp.int32(0)

        @pl.when(count <= 2)
        def _():
            run(wi, zero, 2, False)

        @pl.when(count == 3)
        def _():
            run(wi, zero, 3, False)

        @pl.when(count > 3)
        def _():
            base = pl.multiple_of(jnp.minimum(wi * step, 592), 16)
            mixed[pl.ds(base, length), :] = jnp.zeros((length, D), F32)

            @pl.loop(0, (count + 3) // 4)
            def _(n):
                run(wi, n * 4, 4, True)

    @pl.loop(0, 4)
    def _(wi):
        by_class(forward, wi, counts[wi], 208, 208)

    @pl.loop(0, 4)
    def _(j):
        col = pl.ds(pl.multiple_of(j * 256, 256), 256)
        work[:, col] = nt(ce[...], w[col, 2048:3072])

    def mid_rows(ats, central):
        gain = gains[8:9, :]
        cens = [mixed[at, :] for at in ats]
        cens = [m - row_mean(m) for m in cens]
        invs = [lax.rsqrt(row_mean(c * c) + EPS) for c in cens]
        normals = [c * inv for c, inv in zip(cens, invs)]
        us = []
        for at, normal in zip(ats, normals):
            y = normal * gain
            s = sigmoid(y)
            ys = y * s
            act[at, :] = ys.astype(BF)
            d_ln = work[at, :] * (s + ys * (1.0 - s))
            if central:
                dn = d_ln * normal
                extra[40:48, :] += dn[:8] + dn[8:]
            us.append(d_ln * gain)
        m1 = [row_mean(u) for u in us]
        m2 = [row_mean(u * n) for u, n in zip(us, normals)]
        for at, inv, u, n, a, b in zip(ats, invs, us, normals, m1, m2):
            dm[at, :] = (inv * (u - a - n * b)).astype(BF)

    mid_rows([pl.ds(0, 16), pl.ds(784, 16)], False)

    @pl.loop(0, 24)
    def _(i):
        mid_rows(strips(i, 2, 16), True)

    @pl.loop(0, 4)
    def _(j):
        col = pl.ds(pl.multiple_of(j * 256, 256), 256)
        y = mm(act[16:784, :], w[:, pl.ds(pl.multiple_of(2048 + j * 256, 256), 256)])
        out[:, col] = (xe[32:800, col].astype(F32) + y).astype(BF)
        lhs = act[16:784, col].T
        r = (mm(lhs, ce[16:784, :]) * scale).astype(BF)
        g[col, 0:512] = r[:, :512]
        g[col, 640:1152] = r[:, 512:]

    stores.append(cp(out, out_hbm, 14))

    @pl.loop(0, 4)
    def _(wi):
        by_class(backward, wi, counts[4 + wi], 192, 192)

    gk = jnp.dot(back[...], prod[...], precision=lax.Precision.HIGHEST, preferred_element_type=F32)
    extra[0:31, :] = gk[0:31]
    g_mid = jnp.sum(extra[40:48, :], axis=0, keepdims=True)
    extra[32:33, :] = g_mid
    g[:, 512:640] = (extra[...].T * scale).astype(BF)
    g[:, 1152:1280] = jnp.zeros((D, 128), BF)
    stores.append(cp(g, early_hbm, 15))

    for q in range(4):
        @pl.loop(q * 6, q * 6 + 6)
        def _(i):
            for u in range(2):
                at = pl.ds(pl.multiple_of(i * 32 + 16 * u, 16), 16)
                ext = pl.ds(pl.multiple_of(i * 32 + 16 * u + 32, 16), 16)
                d = mixed[at, :]
                s = sig[ext, :]
                dpre[at, :1024] = (d * s).astype(BF)
                dpre[at, 1024:] = (d * glu[ext, :].astype(F32) * (1.0 - s)).astype(BF)

        part = pl.ds(q * 192, 192)
        stores.append(cp(dpre.at[part], dpre_hbm.at[part], 16 + q))
    for s in stores:
        s.wait()


def mid(ids, consts, frames, cot, hf, hc, w):
    vm = pl.BlockSpec(memory_space=pltpu.VMEM)
    hbm = pl.BlockSpec(memory_space=pltpu.HBM)
    V = pltpu.VMEM
    return pl.pallas_call(
        mid_kernel,
        out_shape=(
            jax.ShapeDtypeStruct((ROWS, D), BF),
            jax.ShapeDtypeStruct((ROWS, D), BF),
            jax.ShapeDtypeStruct((ROWS, 2 * D), BF),
            jax.ShapeDtypeStruct((D, 1280), BF),
            jax.ShapeDtypeStruct((ROWS, 128), F32),
            jax.ShapeDtypeStruct((ROWS, 128), F32),
            jax.ShapeDtypeStruct((16, D), F32),
        ),
        in_specs=[vm, vm, vm, vm, vm, hbm, hbm, hbm, hbm, hbm],
        out_specs=(hbm,) * 6 + (vm,),
        scratch_shapes=[
            V((832, D), BF), V((800, D), BF), V((D, 3200), BF),
            V((832, D), BF), V((848, D), BF), V((832, D), F32),
            V((800, D), F32), V((800, D), F32), V((800, D), BF), V((832, D), BF),
            V((768, 2 * D), BF), V((D, 1280), BF), V((NFFT, D), F32), V((NFFT, D), F32),
            V((128, D), F32), V((832, 128), F32), V((832, 128), F32),
            V((12, 8, NFFT), F32), V((8, NFFT, 128), F32), pltpu.SMEM((8,), jnp.int32), V((ROWS, D), BF),
            pltpu.SemaphoreType.DMA((20,)),
        ],
        compiler_params=pltpu.CompilerParams(vmem_limit_bytes=60 << 20),
        name="block_pass",
    )(ids, *consts, frames, cot, hf, hc, w)


def shards(frames, cotangent, segments, w_in, w_out, kernel, gain_in, gain_mid):
    gain = jnp.stack([gain_in, gain_mid]).astype(F32)
    x, cot = frames[0], cotangent[0]
    full, f_halo, c_halo, ids = gather(w_in, w_out, kernel, gain, segments, x, cot)
    full = full.reshape(D, WIDE)
    block_out, ln, dpre, early, inv, mean, gains = mid(ids, tables(), x, cot, f_halo, c_halo, full)
    g_in, g_out, g_kern, g_vec, input_grad = back(
        early.reshape(4, 4, 4, 16, 1280), ln, dpre, full, x, cot, inv, mean, gains, w_in, gain)
    return (block_out[None], input_grad[None], g_in, g_out, g_kern, g_vec[0], g_vec[1])


def solution(mesh):
    rows = P("dp", "seq", None)
    mat = P(("dp", "seq"), None)
    vec = P(("dp", "seq"))
    return jax.shard_map(
        shards, mesh=mesh, in_specs=(rows, rows, P("dp", "seq"), mat, mat, mat, vec, vec),
        out_specs=(rows, rows, mat, mat, mat, vec, vec), check_vma=False)
```

```python
import math

import jax
import jax.numpy as jnp
import numpy as np
from jax import lax
from jax.experimental import pallas as pl
from jax.experimental.pallas import tpu as pltpu
from jax.sharding import PartitionSpec as P

MESH = pl.DeviceIdType.MESH
HALFW = 1664
WIDE = 2 * HALFW
OUT_PARTS = ((0, 384), (384, 384), (768, 384), (1152, 128), (1280, 128), (1408, 256))
PARTS = ((0, 384), (384, 384), (768, 256), (1024, 128), (1152, 256), (1408, 256))
FIRST, SECOND = (0, 1, 2), (3, 4, 5)
ORDERS = (("z", "x", "y"), ("x", "y", "z"), ("y", "z", "x")) * 2
HALO = 32


def place():
    d, s = lax.axis_index("dp"), lax.axis_index("seq")
    return {"y": d // 4, "x": d % 4, "z": s // 2}, s % 2


def dev(coords, core):
    return (coords["y"] * 4 + coords["x"], coords["z"] * 2 + core)


def moved(coords, axis, by):
    out = dict(coords)
    out[axis] = (coords[axis] + by + 4) % 4
    return out


def greet(targets):
    for t in targets:
        pl.semaphore_signal(pltpu.get_barrier_semaphore(), inc=1, device_id=t, device_id_type=MESH)


def greeted(targets):
    pl.semaphore_wait(pltpu.get_barrier_semaphore(), len(targets))


def half_of(index, which):
    at = [isinstance(i, slice) for i in index].index(True)
    return index[:at] + (pl.ds(2 * which, 2),) + index[at + 1 :]


def block_index(coords, full, axis, value):
    out = []
    for a in ("y", "x", "z"):
        if a == axis:
            out.append(value)
        elif a in full:
            out.append(slice(None))
        else:
            out.append(coords[a])
    return tuple(out)


def gather_kernel(
    w_in_ref, w_out_ref, kern_ref, gain_ref, seg_ref, spread, frames_ref, cot_ref,
    out_ref, hc_ref, ln_hbm, glu_hbm, sig_hbm, inv_hbm, mean_hbm, gains, spec, table, across, counts,
    buf, shard, sib, segs, xe, hat, ln, glu, sig, inv_in, mean_in, load_sem, store_sem, sib_sem, halo_send, halo_recv, a_send, a_recv, s_send, s_recv, out_sem,
):
    me, core = place()
    f32, bf = jnp.float32, jnp.bfloat16
    sibling = dev(me, 1 - core)
    seq = lax.axis_index("seq")
    right = (lax.axis_index("dp"), (seq + 1) % 8)
    left = (lax.axis_index("dp"), (seq + 7) % 8)
    cross = dev(moved(me, "z", 2 * core - 1), 1 - core)
    targets = [dev(moved(me, a, b), core) for a in "yxz" for b in (1, -1, 2)] + [sibling, cross]
    greet(targets)
    rows = frames_ref.shape[0]
    load = pltpu.make_async_copy(frames_ref, xe.at[pl.ds(HALO, rows)], load_sem)
    load.start()
    for c in (0, 1):
        at = c * HALFW
        shard[:, at : at + 1024] = w_in_ref[:, c * 1024 : c * 1024 + 1024].astype(f32)
        shard[:, at + 1024 : at + 1152] = jnp.zeros((8, 128), f32)
        shard[:, at + 1152 : at + HALFW] = w_out_ref[:, c * 512 : c * 512 + 512].astype(f32)
    shard[:, 1024 : 1024 + 31] = kern_ref[...].astype(f32)
    eye = lax.broadcasted_iota(jnp.int32, (8, 8), 0) == lax.broadcasted_iota(jnp.int32, (8, 8), 1)
    for n in (0, 1):
        row = jnp.broadcast_to(gain_ref[n : n + 1, :], (8, 8))
        shard[:, 1055 + n : 1056 + n] = jnp.sum(jnp.where(eye, row, 0.0), axis=1, keepdims=True)
    greeted(targets)

    first = pltpu.make_async_remote_copy(
        src_ref=shard, dst_ref=sib, send_sem=sib_sem.at[0], recv_sem=sib_sem.at[1],
        device_id=sibling, device_id_type=MESH)
    first.start()
    halos = []
    for n, (src, dst, h, end) in enumerate(((frames_ref, xe, HALO, HALO + rows), (cot_ref, hc_ref, 16, 16))):
        for m, (at, to, who) in enumerate(((rows - h, 0, right), (0, end, left))):
            halos.append(pltpu.make_async_remote_copy(
                src_ref=src.at[pl.ds(at, h)], dst_ref=dst.at[pl.ds(to, h)],
                send_sem=halo_send.at[n, m], recv_sem=halo_recv.at[n, m],
                device_id=who, device_id_type=MESH))
    for m, who in enumerate((right, left)):
        halos.append(pltpu.make_async_remote_copy(
            src_ref=seg_ref, dst_ref=segs.at[m], send_sem=halo_send.at[2, m], recv_sem=halo_recv.at[2, m],
            device_id=who, device_id_type=MESH))
    first.wait()
    mine, other = shard[...], sib[...]
    low = jnp.where(core == 0, mine[:, :HALFW], other[:, HALFW:])
    high = jnp.where(core == 0, other[:, :HALFW], mine[:, HALFW:])
    buf[me["y"], me["x"], me["z"], :, pl.ds(pl.multiple_of(core * HALFW, 128), HALFW)] = jnp.concatenate(
        [low, high], axis=0).astype(bf)

    def cols(p, c=core):
        return pl.ds(pl.multiple_of(c * HALFW + OUT_PARTS[p][0], 128), OUT_PARTS[p][1])

    def send(p, ph, which, idx, by):
        axis = ORDERS[p][ph]
        ref = buf.at[idx + (slice(None), cols(p))]
        return pltpu.make_async_remote_copy(
            src_ref=ref, dst_ref=ref, send_sem=a_send.at[p, ph, which], recv_sem=a_recv.at[p, ph, which],
            device_id=dev(moved(me, axis, by), core), device_id_type=MESH)

    def to_sibling(p, which, idx, c=core):
        ref = buf.at[idx + (slice(None), cols(p, c))]
        return pltpu.make_async_remote_copy(
            src_ref=ref, dst_ref=ref, send_sem=s_send.at[p, which], recv_sem=s_recv.at[p, which],
            device_id=sibling, device_id_type=MESH)

    def block(p, ph, by):
        axis = ORDERS[p][ph]
        return block_index(me, ORDERS[p][:ph], axis, (me[axis] + by + 4) % 4)

    sends, outs = [], []

    def go(cp):
        cp.start()
        sends.append(cp)

    def start(p, ph):
        if ph > 0:
            for which, by in ((0, -1), (1, 1), (2, 2)):
                send(p, ph - 1, which, block(p, ph - 1, by), by).wait_recv()
        own = block(p, ph, 0)
        for which, by in ((0, 1), (1, -1), (2, 2))[: 3 if ph < 2 else 2]:
            go(send(p, ph, which, own, by))
        if ph == 2:
            go(to_sibling(p, 0, own))

    def pass_on(p):
        for which, by in ((0, -1), (1, 1)):
            idx = block(p, 2, by)
            send(p, 2, which, idx, -by).wait_recv()
            go(send(p, 2, which + 2, half_of(idx, which), -by))
            go(to_sibling(p, 1 + which, idx))

    def flush(p, c, n):
        at = (slice(None),) * 4 + (cols(p, c),)
        cp = pltpu.make_async_copy(buf.at[at], out_ref.at[at], out_sem.at[p, n])
        cp.start()
        outs.append(cp)

    def finish(p):
        idx = block(p, 2, 2)
        for which in (0, 1):
            send(p, 2, 2 + which, half_of(idx, which), 1).wait_recv()
        go(to_sibling(p, 3, idx))
        flush(p, core, 0)

    def from_sibling(p):
        for which, by in ((0, 0), (1, -1), (2, 1), (3, 2)):
            to_sibling(p, which, block(p, 2, by), 1 - core).wait_recv()
        flush(p, 1 - core, 1)

    def strips(i, n):
        return [pl.ds(pl.multiple_of(i * (16 * n) + 16 * u, 16), 16) for u in range(n)]

    def normalise(lo, hi):
        @pl.loop(lo, hi)
        def _(i):
            ats = strips(i, 4)
            xs = [xe[at, :].astype(f32) for at in ats]
            means = [row_mean(x) for x in xs]
            cens = [x - m for x, m in zip(xs, means)]
            invs = [lax.rsqrt(row_mean(c * c) + EPS) for c in cens]
            for at, c, inv, m in zip(ats, cens, invs, means):
                hat[at, :] = c * inv
                inv_in[at, :] = jnp.broadcast_to(inv, (16, 128))
                mean_in[at, :] = jnp.broadcast_to(m, (16, 128))

    def keep(src, dst, n):
        cp = pltpu.make_async_copy(src, dst, store_sem.at[n])
        cp.start()
        outs.append(cp)

    for p in FIRST + SECOND:
        start(p, 0)
    for cp in halos:
        cp.start()
    load.wait()
    for cp in halos:
        cp.wait()
    normalise(0, 4)
    for p in FIRST + SECOND:
        start(p, 1)
    normalise(4, 10)
    for p in FIRST:
        start(p, 2)
    normalise(10, 13)
    inner = pl.ds(HALO, rows)
    keep(inv_in.at[inner], inv_hbm, 0)
    keep(mean_in.at[inner], mean_hbm, 1)
    own = seg_ref[...]
    before = jnp.where(seq == 0, jnp.broadcast_to(own[:, 0:1] - 1, (1, 128)), segs[0, :, 640:768])
    after = jnp.where(seq == 7, jnp.broadcast_to(own[:, 767:768] + 1, (1, 128)), segs[1, :, 0:128])
    ids = jnp.concatenate(
        [before] + [own[:, n * 128 : n * 128 + 128] for n in range(6)] + [after], axis=0).astype(f32)
    colours(ids, table, across, counts)
    for p in FIRST:
        pass_on(p)
    for p in SECOND:
        start(p, 2)
    for p in FIRST:
        finish(p)
    for p in SECOND:
        pass_on(p)
    for p in FIRST:
        from_sibling(p)
    taps = buf[:, :, :, :, 1024:1152].reshape(1024, 128).astype(f32).T
    gains[0:8, :] = jnp.broadcast_to(taps[31:32, :], (8, 1024))
    gains[8:16, :] = jnp.broadcast_to(taps[32:33, :], (8, 1024))

    @pl.loop(0, 13)
    def _(i):
        for at in strips(i, 4):
            ln[at, :] = (hat[at, :] * gains[0:1, :]).astype(bf)
    keep(ln.at[inner], ln_hbm, 2)

    def project(j):
        col = slice(j * 256, j * 256 + 256)
        w0 = buf[:, :, :, :, j * 256 : j * 256 + 256].reshape(1024, 256)
        w1 = buf[:, :, :, :, HALFW + j * 256 : HALFW + j * 256 + 256].reshape(1024, 256)

        @pl.loop(0, 2)
        def _(r):
            at = pl.ds(pl.multiple_of(r * 416, 16), 416)
            lhs = ln[at, :]
            value = mm(lhs, w0)
            s = sigmoid(mm(lhs, w1))
            glu[at, col] = (value * s).astype(bf)
            sig[at, col] = s
        keep(glu.at[:, col], glu_hbm.at[:, col], 3 + 2 * j)
        keep(sig.at[inner, col], sig_hbm.at[:, col], 4 + 2 * j)

    project(0)
    for p in SECOND:
        finish(p)
    project(1)
    project(2)
    for p in SECOND:
        from_sibling(p)
    spec[...] = jnp.dot(spread[...], taps, precision=lax.Precision.HIGHEST, preferred_element_type=f32)
    project(3)
    for cp in sends:
        cp.wait_send()
    for cp in outs:
        cp.wait()


def gather(w_in, w_out, kern, gain, seg, spread, frames, cot):
    bf = jnp.bfloat16
    vm = pl.BlockSpec(memory_space=pltpu.VMEM)
    hbm = pl.BlockSpec(memory_space=pltpu.HBM)
    return pl.pallas_call(
        gather_kernel,
        out_shape=(
            jax.ShapeDtypeStruct((4, 4, 4, 16, WIDE), bf),
            jax.ShapeDtypeStruct((32, 1024), bf),
            jax.ShapeDtypeStruct((768, 1024), bf),
            jax.ShapeDtypeStruct((832, 1024), bf),
            jax.ShapeDtypeStruct((768, 1024), jnp.float32),
            jax.ShapeDtypeStruct((768, 128), jnp.float32),
            jax.ShapeDtypeStruct((768, 128), jnp.float32),
            jax.ShapeDtypeStruct((16, 1024), jnp.float32),
            jax.ShapeDtypeStruct((NFFT, 1024), jnp.float32),
            jax.ShapeDtypeStruct((12, 8, NFFT), jnp.float32),
            jax.ShapeDtypeStruct((8, NFFT, 128), jnp.float32),
            jax.ShapeDtypeStruct((8, 128), jnp.int32),
        ),
        in_specs=[vm, vm, vm, vm, vm, vm, hbm, hbm],
        out_specs=(hbm, vm, hbm, hbm, hbm, hbm, hbm, vm, vm, vm, vm, vm),
        scratch_shapes=[
            pltpu.VMEM((4, 4, 4, 16, WIDE), bf),
            pltpu.VMEM((8, WIDE), jnp.float32),
            pltpu.VMEM((8, WIDE), jnp.float32),
            pltpu.VMEM((2, 1, 768), jnp.int32),
            pltpu.VMEM((832, 1024), bf),
            pltpu.VMEM((832, 1024), jnp.float32),
            pltpu.VMEM((832, 1024), bf),
            pltpu.VMEM((832, 1024), bf),
            pltpu.VMEM((832, 1024), jnp.float32),
            pltpu.VMEM((832, 128), jnp.float32),
            pltpu.VMEM((832, 128), jnp.float32),
            pltpu.SemaphoreType.DMA,
            pltpu.SemaphoreType.DMA((11,)),
            pltpu.SemaphoreType.DMA((2,)),
            pltpu.SemaphoreType.DMA((3, 2)),
            pltpu.SemaphoreType.DMA((3, 2)),
            pltpu.SemaphoreType.DMA((6, 3, 4)),
            pltpu.SemaphoreType.DMA((6, 3, 4)),
            pltpu.SemaphoreType.DMA((6, 4)),
            pltpu.SemaphoreType.DMA((6, 4)),
            pltpu.SemaphoreType.DMA((6, 2)),
        ],
        compiler_params=pltpu.CompilerParams(
            collective_id=0, has_side_effects=True, vmem_limit_bytes=60 << 20),
        name="gather_weights",
    )(w_in, w_out, kern, gain, seg, spread, frames, cot)


def back_kernel(
    early, ln_hbm, dpre_hbm, w_hbm, frames, cot, inv_hbm, mean_hbm, gains, w_rows, gain,
    o_in, o_out, o_kern, o_vec, out,
    acc, sibbuf, gsend, h0, f0, f1, f2, last, low, fin,
    ln, turned, dpre, w, xe, ce, inv_in, mean_in, work,
    load_sem, d_send, d_recv, a_send, a_recv, e_sem,
):
    scale = 1.0 / math.sqrt(98304.0)
    f32, bf = jnp.float32, jnp.bfloat16
    me, core = place()
    sibling = dev(me, 1 - core)
    full4 = (slice(None),) * 4

    def cp(src, dst, n):
        c = pltpu.make_async_copy(src, dst, load_sem.at[n])
        c.start()
        return c

    def early_cols(c):
        return full4 + (pl.ds(pl.multiple_of(c * 640, 128), 640),)

    def lanes(p):
        return pl.ds(*PARTS[p])

    later = pl.ds(1024, 640)

    loads = [
        cp(ln_hbm, ln, 0),
        cp(dpre_hbm, dpre, 1),
        cp(early.at[early_cols(core)], acc.at[full4 + (later,)], 2),
        cp(w_hbm.at[:, pl.ds(0, 1024)], w.at[:, pl.ds(0, 1024)], 3),
        cp(w_hbm.at[:, pl.ds(HALFW, 1024)], w.at[:, pl.ds(1024, 1024)], 4),
        cp(frames, xe, 5),
        cp(cot, ce, 6),
        cp(inv_hbm, inv_in, 7),
        cp(mean_hbm, mean_in, 8),
    ]
    targets = [dev(moved(me, a, b), core) for a in "yxz" for b in (1, -1, 2)] + [sibling]
    greet(targets)

    def give(p):
        src = early.at[early_cols(1 - core)] if p == 3 else gsend.at[full4 + (lanes(p),)]
        return pltpu.make_async_remote_copy(
            src_ref=src, dst_ref=sibbuf.at[full4 + (later if p == 3 else lanes(p),)],
            send_sem=d_send.at[p], recv_sem=d_recv.at[p], device_id=sibling, device_id_type=MESH)

    sends = []

    def go(c):
        c.start()
        sends.append(c)

    def axis_of(p, ph):
        return ORDERS[p][2 - ph]

    def block(p, ph, by):
        axis = axis_of(p, ph)
        return block_index(me, ORDERS[p][: 2 - ph], axis, (me[axis] + by + 4) % 4)

    def send_half(p, which):
        return pltpu.make_async_remote_copy(
            src_ref=acc.at[half_of(block(p, 0, 2), which) + (slice(None), lanes(p))],
            dst_ref=h0.at[pl.ds(2 * which, 2), :, :, lanes(p)],
            send_sem=a_send.at[p, 0, which], recv_sem=a_recv.at[p, 0, which],
            device_id=dev(moved(me, axis_of(p, 0), (1, -1)[which]), core), device_id_type=MESH)

    def send_full(p, ph, which):
        by = (1, -1, 2)[which]
        dst = (f0, f1, f2)[ph].at[(which,) + (slice(None),) * (3 - ph) + (lanes(p),)]
        return pltpu.make_async_remote_copy(
            src_ref=acc.at[block(p, ph, by) + (slice(None), lanes(p))], dst_ref=dst,
            send_sem=a_send.at[p, ph, 2 + which], recv_sem=a_recv.at[p, ph, 2 + which],
            device_id=dev(moved(me, axis_of(p, ph), by), core), device_id_type=MESH)

    def over(p, ph, value, body, span=(0, 4)):
        axis, full = axis_of(p, ph), ORDERS[p][: 2 - ph]
        names = [a for a in "yxz" if a in full]

        def at(k):
            by_name = {axis: value}
            if len(names) == 2:
                by_name[names[0]] = k
                by_name[names[1]] = slice(None)
            elif len(names) == 1:
                by_name[names[0]] = slice(None)
            return tuple(by_name[a] if a in by_name else me[a] for a in "yxz")

        if len(names) == 2:
            @pl.loop(*span)
            def _(k):
                body(at(k), (k, slice(None)))
        else:
            body(at(0), (slice(None),) * len(names))

    def start_halves(p):
        for which in (0, 1):
            go(send_half(p, which))

    def pass_on(p):
        axis = axis_of(p, 0)
        for which, by in ((0, 1), (1, -1)):
            send_half(p, which).wait_recv()

            def body(at, dig):
                at = at + (slice(None), lanes(p))
                acc[at] = (acc[at].astype(f32) + h0[dig + (slice(None), lanes(p))].astype(f32)).astype(bf)
            over(p, 0, (me[axis] + by + 4) % 4, body, (2 * which, 2 * which + 2))
            go(send_full(p, 0, which))

    def take(p, ph):
        count = 2 if ph == 0 else 3
        ref = (f0, f1, f2)[ph]
        for which in range(count):
            send_full(p, ph, which).wait_recv()
        sl = lanes(p)

        def body(at, dig):
            at = at + (slice(None), sl)
            total = acc[at].astype(f32)
            for which in range(count):
                total = total + ref[(which,) + dig + (slice(None), sl)].astype(f32)
            if ph < 2:
                acc[at] = total.astype(bf)
            else:
                last[:, sl] = total
        over(p, ph, me[axis_of(p, ph)], body)
        if ph < 2:
            for which in range(3):
                go(send_full(p, ph + 1, which))

    def product(p, half, store):
        at, width = PARTS[p]

        @pl.loop(0, 4)
        def _(y):
            lhs = turned[pl.ds(pl.multiple_of(y * 256, 256), 256), :]
            rhs = dpre[:, pl.ds(pl.multiple_of(half * 1024 + at, 128), width)]
            r = jnp.dot(lhs, rhs, preferred_element_type=f32) * scale
            store(y, r.reshape(4, 4, 16, width))

    def for_sibling(p):
        def store(y, r):
            gsend[y, :, :, :, lanes(p)] = r.astype(bf)
        product(p, 1 - core, store)

    def for_own(p):
        give(p).wait_recv()

        def store(y, r):
            acc[y, :, :, :, lanes(p)] = (r + sibbuf[y, :, :, :, lanes(p)].astype(f32)).astype(bf)
        product(p, core, store)
        start_halves(p)

    def input_product(j):
        col = slice(j * 256, j * 256 + 256)
        work[:, col] = lax.dot_general(dpre[...], w[col, :], (((1,), (1,)), ((), ())), preferred_element_type=f32)

    def input_rows(n):
        @pl.loop(3 * n, 3 * n + 3)
        def _(i):
            ats = [pl.ds(pl.multiple_of(i * 64 + 16 * u, 16), 16) for u in range(4)]
            gain = gains[0:1, :]
            invs = [inv_in[at, 0:1] for at in ats]
            normals = [(xe[at, :].astype(f32) - mean_in[at, 0:1]) * inv for at, inv in zip(ats, invs)]
            us = [work[at, :] * gain for at in ats]
            m1 = [row_mean(u) for u in us]
            m2 = [row_mean(u * n) for u, n in zip(us, normals)]
            for at, inv, u, n, a, b in zip(ats, invs, us, normals, m1, m2):
                out[at, :] = (ce[at, :].astype(f32) + inv * (u - a - n * b)).astype(bf)

    loads[0].wait()
    turned[...] = ln[...].T
    loads[1].wait()
    for_sibling(0)
    greeted(targets)
    go(give(3))
    go(give(0))
    for_sibling(1)
    go(give(1))
    loads[2].wait()
    give(3).wait_recv()

    @pl.loop(0, 4)
    def _(y):
        at = (y, slice(None), slice(None), slice(None), later)
        acc[at] = (acc[at].astype(f32) + sibbuf[at].astype(f32)).astype(bf)
    for p in SECOND:
        start_halves(p)
    for_sibling(2)
    go(give(2))
    for_own(0)
    for p in SECOND:
        pass_on(p)
    for_own(1)
    for_own(2)
    pass_on(0)
    for n in (3, 4):
        loads[n].wait()
    input_product(0)
    pass_on(1)
    pass_on(2)
    for p in SECOND:
        take(p, 0)
    input_product(1)
    take(0, 0)
    input_product(2)
    for p in SECOND:
        take(p, 1)
    take(1, 0)
    take(2, 0)
    input_product(3)
    for n in (5, 6, 7, 8):
        loads[n].wait()
    take(0, 1)
    for p in SECOND:
        take(p, 2)
    input_rows(0)
    take(1, 1)
    take(2, 1)
    input_rows(1)
    take(0, 2)
    input_rows(2)
    take(1, 2)
    take(2, 2)
    top, bottom = last[0:8, :], last[8:16, :]
    low[...] = jnp.where(core == 0, bottom, top)
    swap = pltpu.make_async_remote_copy(
        src_ref=low, dst_ref=fin, send_sem=e_sem.at[0], recv_sem=e_sem.at[1], device_id=sibling, device_id_type=MESH)
    swap.start()
    input_rows(3)
    mine = jnp.where(core == 0, top, bottom)
    swap.wait()
    theirs = fin[...]
    total = jnp.zeros((8, 1), f32)
    for c in (0, 1):
        own = jnp.where(core == c, mine, theirs)
        o_in[:, c * 1024 : c * 1024 + 1024] = own[:, :1024]
        o_out[:, c * 512 : c * 512 + 512] = own[:, 1152:1664]
        rows = w_rows[:, c * 1024 : c * 1024 + 1024].astype(f32)
        total = total + jnp.sum(rows * own[:, :1024], axis=-1, keepdims=True)
        if c == 0:
            rest = own[:, 1024:1152]
    eye = lax.broadcasted_iota(jnp.int32, (8, 8), 0) == lax.broadcasted_iota(jnp.int32, (8, 8), 1)
    column = jnp.sum(jnp.where(eye, jnp.broadcast_to(gain[0:1, :], (8, 8)), 0.0), axis=1, keepdims=True)
    o_kern[...] = rest[:, 0:31]
    pair = []
    for v in (total / column, rest[:, 32:33]):
        pair.append(jnp.sum(jnp.where(eye, jnp.broadcast_to(v, (8, 8)), 0.0), axis=0, keepdims=True))
    o_vec[...] = jnp.concatenate(pair, axis=0)
    for c in sends:
        c.wait_send()


def back(early, ln, dpre, w, frames, cot, inv, mean, gains, w_rows, gain):
    bf, f32 = jnp.bfloat16, jnp.float32
    vm = pl.BlockSpec(memory_space=pltpu.VMEM)
    hbm = pl.BlockSpec(memory_space=pltpu.HBM)
    V = pltpu.VMEM
    return pl.pallas_call(
        back_kernel,
        out_shape=(
            jax.ShapeDtypeStruct((8, 2048), f32),
            jax.ShapeDtypeStruct((8, 1024), f32),
            jax.ShapeDtypeStruct((8, 31), f32),
            jax.ShapeDtypeStruct((2, 8), f32),
            jax.ShapeDtypeStruct((768, 1024), bf),
        ),
        in_specs=[hbm] * 8 + [vm] * 3,
        out_specs=(vm, vm, vm, vm, vm),
        scratch_shapes=[
            V((4, 4, 4, 16, HALFW), bf),
            V((4, 4, 4, 16, HALFW), bf),
            V((4, 4, 4, 16, 1024), bf),
            V((4, 4, 16, HALFW), bf),
            V((2, 4, 4, 16, HALFW), bf),
            V((3, 4, 16, HALFW), bf),
            V((3, 16, HALFW), bf),
            V((16, HALFW), f32),
            V((8, HALFW), f32),
            V((8, HALFW), f32),
            V((768, 1024), bf),
            V((1024, 768), bf),
            V((768, 2048), bf),
            V((1024, 2048), bf),
            V((768, 1024), bf),
            V((768, 1024), bf),
            V((768, 128), f32),
            V((768, 128), f32),
            V((768, 1024), f32),
            pltpu.SemaphoreType.DMA((10,)),
            pltpu.SemaphoreType.DMA((4,)),
            pltpu.SemaphoreType.DMA((4,)),
            pltpu.SemaphoreType.DMA((6, 3, 5)),
            pltpu.SemaphoreType.DMA((6, 3, 5)),
            pltpu.SemaphoreType.DMA((2,)),
        ],
        compiler_params=pltpu.CompilerParams(
            collective_id=1, has_side_effects=True, vmem_limit_bytes=60 << 20),
        name="back_and_scatter",
    )(early, ln, dpre, w, frames, cot, inv, mean, gains, w_rows, gain)


EPS = 1e-05
HALF = 15
ROWS = 768
D = 1024
NFFT = 256


def tables():
    omega = 2 * np.pi * (np.arange(128) + 0.5) / NFFT
    phase = omega[:, None] * np.arange(NFFT)[None]
    basis = np.concatenate([np.cos(phase), -np.sin(phase)], axis=0)
    lag = omega[:, None] * (np.arange(31) - HALF)[None]
    spread = np.zeros((NFFT, 128))
    spread[:, :31] = np.concatenate([np.cos(lag), np.sin(lag)], axis=0) * (2 / NFFT)
    back = np.zeros((128, NFFT))
    back[:31] = np.concatenate([np.cos(lag), -np.sin(lag)], axis=0).T * (2 / NFFT)
    f32 = jnp.float32
    return (jnp.asarray(basis, f32), jnp.asarray(basis.T, f32), jnp.asarray(spread, f32), jnp.asarray(back, f32))


def sigmoid(v):
    return 0.5 * jnp.tanh(0.5 * v) + 0.5


NT = (((1,), (1,)), ((), ()))
TN = (((0,), (0,)), ((), ()))
F32 = jnp.float32
BF = jnp.bfloat16


def nt(a, b):
    return lax.dot_general(a, b, NT, preferred_element_type=F32)


def mm(a, b):
    return jnp.dot(a, b, preferred_element_type=F32)


def row_mean(v):
    return jnp.sum(v, axis=-1, keepdims=True) * (1.0 / D)


FWD_AT, BWD_AT = (0, 208, 416, 592), (16, 208, 400, 592)


def colours(ids, table, across, counts):
    lane = lax.broadcasted_iota(jnp.int32, (1, 128), 1)
    wide = lax.broadcasted_iota(jnp.int32, (1, NFFT), 1)
    for n, at in enumerate(FWD_AT + BWD_AT):
        length = 240 if n < 4 else 224
        r, o = divmod(at + 96, 128)

        def piece(k, o=o):
            if o == 0:
                return ids[k : k + 1, :]
            first = pltpu.roll(ids[k : k + 1, :], 128 - o, 1)
            return jnp.where(lane < 128 - o, first, pltpu.roll(ids[min(k + 1, 7) : min(k + 1, 7) + 1, :], 128 - o, 1))

        own = jnp.concatenate([piece(r), piece(r + 1)], axis=1)
        step = jnp.where(wide < length - HALF, pltpu.roll(own, NFFT - HALF, 1) - own, 0.0)
        count = jnp.max(step, axis=1, keepdims=True) + 1.0
        own = own + 1.0
        own = own - count * jnp.floor((own + 0.5) / count)
        own = jnp.where(wide < length, own, -1.0)
        rows = jnp.broadcast_to(own, (8, NFFT))
        table[n] = rows
        across[n] = jnp.broadcast_to(rows.T[:, 0:1], (NFFT, 128))
        if n >= 4:
            table[n + 4] = jnp.where((wide >= 16) & (wide < 208), rows, -1.0)
        counts[n : n + 1, :] = jnp.broadcast_to(count, (1, 128)).astype(jnp.int32)


def mid_kernel(
    counts, gains, basis, turned, back, frames, cot, hc, w_hbm, glu_hbm, sig_hbm, spec_hbm, table_hbm, across_hbm,
    out_hbm, dpre_hbm, early_hbm,
    xe, ce, w, glu, sig, mixed, work, act, dm, dpre, g, spec, prod, extra, table, across, out, sems,
):
    scale = 1.0 / math.sqrt(98304.0)

    def cp(src, dst, n):
        c = pltpu.make_async_copy(src, dst, sems.at[n])
        c.start()
        return c

    cols = lambda lo, n: (slice(None), pl.ds(lo, n))
    loads = [
        cp(table_hbm, table, 0),
        cp(across_hbm, across, 1),
        cp(spec_hbm, spec, 2),
        cp(glu_hbm, glu.at[pl.ds(0, 832)], 3),
        cp(cot, ce.at[pl.ds(16, ROWS)], 4),
        cp(hc.at[pl.ds(0, 16)], ce.at[pl.ds(0, 16)], 5),
        cp(hc.at[pl.ds(16, 16)], ce.at[pl.ds(784, 16)], 6),
        cp(w_hbm.at[cols(1152, 512)], w.at[cols(0, 512)], 7),
        cp(w_hbm.at[cols(2816, 512)], w.at[cols(512, 512)], 8),
        cp(frames, xe, 9),
        cp(sig_hbm, sig, 10),
    ]
    glu[pl.ds(832, 16), :] = jnp.zeros((16, D), BF)
    dm[pl.ds(800, 32), :] = jnp.zeros((32, D), BF)
    prod[...] = jnp.zeros((NFFT, D), F32)
    extra[...] = jnp.zeros((128, D), F32)
    stores = []
    for n in range(4):
        loads[n].wait()

    def strips(i, n, off=0):
        return [pl.ds(pl.multiple_of(i * (16 * n) + off + 16 * u, 16), 16) for u in range(n)]

    def picked(row, first, k):
        return jnp.concatenate(
            [jnp.where(table[row, 0:1, :] == (first + c).astype(F32), basis[...], 0.0) for c in range(k)],
            axis=0).astype(BF)

    def placed(row, first, k, lo, hi):
        own = across[row, lo:hi, :]
        own = jnp.concatenate([own, own], axis=1)
        return jnp.concatenate(
            [jnp.where(own == (first + c).astype(F32), turned[lo:hi, :], 0.0) for c in range(k)], axis=1).astype(BF)

    def forward(wi, first, k, add):
        base = pl.multiple_of(jnp.minimum(wi * 208, 592), 16)
        to = picked(wi, first, k)
        fro = placed(wi, first, k, 16, 224)
        for j in range(4):
            col = slice(j * 256, j * 256 + 256)
            x = mm(to, glu[pl.ds(base, 256), col])
            hr, hi = spec[:128, col], spec[128:, col]
            ys = []
            for c in range(k):
                xr, xi = x[256 * c : 256 * c + 128], x[256 * c + 128 : 256 * c + 256]
                ys += [(xr * hr - xi * hi).astype(BF), (xr * hi + xi * hr).astype(BF)]
            y = mm(fro, jnp.concatenate(ys, axis=0))
            if add:
                mixed[pl.ds(base, 208), col] += y
            else:
                mixed[pl.ds(base, 208), col] = y

    def backward(wi, first, k, add):
        base = pl.multiple_of(wi * 192, 16)
        to = picked(4 + wi, first, k)
        mid_to = picked(8 + wi, first, k)
        fro = placed(4 + wi, first, k, 16, 208)
        for j in range(4):
            col = slice(j * 256, j * 256 + 256)
            d = mm(to, dm[pl.ds(base, 256), col])
            q = mm(mid_to, glu[pl.ds(base + 16, 256), col])
            hr, hi = spec[:128, col], spec[128:, col]
            ys = []
            pr, pi = prod[:128, col], prod[128:, col]
            for c in range(k):
                lo, mi, up = 256 * c, 256 * c + 128, 256 * c + 256
                dr, di, qr, qi = d[lo:mi], d[mi:up], q[lo:mi], q[mi:up]
                ys += [(dr * hr + di * hi).astype(BF), (di * hr - dr * hi).astype(BF)]
                pr = pr + (qr * dr + qi * di)
                pi = pi + (qi * dr - qr * di)
            prod[:128, col] = pr
            prod[128:, col] = pi
            y = mm(fro, jnp.concatenate(ys, axis=0))
            if add:
                mixed[pl.ds(base, 192), col] += y
            else:
                mixed[pl.ds(base, 192), col] = y

    def by_class(run, wi, count, length, step):
        zero = jnp.int32(0)

        @pl.when(count <= 2)
        def _():
            run(wi, zero, 2, False)

        @pl.when(count == 3)
        def _():
            run(wi, zero, 3, False)

        @pl.when(count > 3)
        def _():
            base = pl.multiple_of(jnp.minimum(wi * step, 592), 16)
            mixed[pl.ds(base, length), :] = jnp.zeros((length, D), F32)

            @pl.loop(0, (count + 3) // 4)
            def _(n):
                run(wi, n * 4, 4, True)

    @pl.loop(0, 4)
    def _(wi):
        by_class(forward, wi, counts[wi, 0], 208, 208)

    for n in range(4, 11):
        loads[n].wait()

    @pl.loop(0, 4)
    def _(j):
        col = pl.ds(pl.multiple_of(j * 256, 256), 256)
        work[:, col] = nt(ce[...], w[col, :])

    def mid_rows(ats, central):
        gain = gains[8:9, :]
        cens = [mixed[at, :] for at in ats]
        cens = [m - row_mean(m) for m in cens]
        invs = [lax.rsqrt(row_mean(c * c) + EPS) for c in cens]
        normals = [c * inv for c, inv in zip(cens, invs)]
        us = []
        for at, normal in zip(ats, normals):
            y = normal * gain
            s = sigmoid(y)
            ys = y * s
            act[at, :] = ys.astype(BF)
            d_ln = work[at, :] * (s + ys * (1.0 - s))
            if central:
                dn = d_ln * normal
                extra[40:48, :] += dn[:8] + dn[8:]
            us.append(d_ln * gain)
        m1 = [row_mean(u) for u in us]
        m2 = [row_mean(u * n) for u, n in zip(us, normals)]
        for at, inv, u, n, a, b in zip(ats, invs, us, normals, m1, m2):
            dm[at, :] = (inv * (u - a - n * b)).astype(BF)

    mid_rows([pl.ds(0, 16), pl.ds(784, 16)], False)

    @pl.loop(0, 24)
    def _(i):
        mid_rows(strips(i, 2, 16), True)

    @pl.loop(0, 4)
    def _(j):
        col = pl.ds(pl.multiple_of(j * 256, 256), 256)
        y = mm(act[16:784, :], w[:, col])
        out[:, col] = (xe[:, col].astype(F32) + y).astype(BF)
        lhs = act[16:784, col].T
        r = (mm(lhs, ce[16:784, :]) * scale).astype(BF)
        g[col, 128:640] = r[:, :512]
        g[col, 768:1280] = r[:, 512:]

    stores.append(cp(out, out_hbm, 11))

    @pl.loop(0, 4)
    def _(wi):
        by_class(backward, wi, counts[4 + wi, 0], 192, 192)

    gk = jnp.dot(back[...], prod[...], precision=lax.Precision.HIGHEST, preferred_element_type=F32)
    extra[0:31, :] = gk[0:31]
    g_mid = jnp.sum(extra[40:48, :], axis=0, keepdims=True)
    extra[32:33, :] = g_mid
    g[:, 0:128] = (extra[...].T * scale).astype(BF)
    g[:, 640:768] = jnp.zeros((D, 128), BF)
    stores.append(cp(g, early_hbm, 12))

    for q in range(4):
        @pl.loop(q * 6, q * 6 + 6)
        def _(i):
            for u in range(2):
                at = pl.ds(pl.multiple_of(i * 32 + 16 * u, 16), 16)
                ext = pl.ds(pl.multiple_of(i * 32 + 16 * u + 32, 16), 16)
                d = mixed[at, :]
                s = sig[at, :]
                dpre[at, :1024] = (d * s).astype(BF)
                dpre[at, 1024:] = (d * glu[ext, :].astype(F32) * (1.0 - s)).astype(BF)

        part = pl.ds(q * 192, 192)
        stores.append(cp(dpre.at[part], dpre_hbm.at[part], 13 + q))
    for s in stores:
        s.wait()


def mid(counts, gains, consts, *rest):
    vm = pl.BlockSpec(memory_space=pltpu.VMEM)
    hbm = pl.BlockSpec(memory_space=pltpu.HBM)
    V = pltpu.VMEM
    return pl.pallas_call(
        mid_kernel,
        out_shape=(
            jax.ShapeDtypeStruct((ROWS, D), BF),
            jax.ShapeDtypeStruct((ROWS, 2 * D), BF),
            jax.ShapeDtypeStruct((D, 1280), BF),
        ),
        in_specs=[pl.BlockSpec(memory_space=pltpu.SMEM), vm, vm, vm, vm] + [hbm] * 9,
        out_specs=(hbm,) * 3,
        scratch_shapes=[
            V((768, D), BF), V((800, D), BF), V((D, D), BF),
            V((848, D), BF), V((768, D), F32),
            V((800, D), F32), V((800, D), F32), V((800, D), BF), V((832, D), BF),
            V((768, 2 * D), BF), V((D, 1280), BF), V((NFFT, D), F32), V((NFFT, D), F32),
            V((128, D), F32), V((12, 8, NFFT), F32), V((8, NFFT, 128), F32), V((ROWS, D), BF),
            pltpu.SemaphoreType.DMA((17,)),
        ],
        compiler_params=pltpu.CompilerParams(vmem_limit_bytes=60 << 20),
        name="block_pass",
    )(counts, gains, *consts, *rest)


def shards(frames, cotangent, segments, w_in, w_out, kernel, gain_in, gain_mid):
    gain = jnp.stack([gain_in, gain_mid]).astype(F32)
    x, cot = frames[0], cotangent[0]
    basis, turned, spread, back_table = tables()
    full, c_halo, ln, glu, sig, inv, mean, gains, spec, table, across, counts = gather(
        w_in, w_out, kernel, gain, segments, spread, x, cot)
    full = full.reshape(D, WIDE)
    block_out, dpre, early = mid(
        counts, gains, (basis, turned, back_table), x, cot, c_halo, full, glu, sig, spec, table, across)
    g_in, g_out, g_kern, g_vec, input_grad = back(
        early.reshape(4, 4, 4, 16, 1280), ln, dpre, full, x, cot, inv, mean, gains, w_in, gain)
    return (block_out[None], input_grad[None], g_in, g_out, g_kern, g_vec[0], g_vec[1])


def solution(mesh):
    rows = P("dp", "seq", None)
    mat = P(("dp", "seq"), None)
    vec = P(("dp", "seq"))
    return jax.shard_map(
        shards, mesh=mesh, in_specs=(rows, rows, P("dp", "seq"), mat, mat, mat, vec, vec),
        out_specs=(rows, rows, mat, mat, mat, vec, vec), check_vma=False)
```

```python
import math

import jax
import jax.numpy as jnp
import numpy as np
from jax import lax
from jax.experimental import pallas as pl
from jax.experimental.pallas import tpu as pltpu
from jax.sharding import PartitionSpec as P

MESH = pl.DeviceIdType.MESH
HALFW = 1664
WIDE = 2 * HALFW
OUT_PARTS = ((0, 384), (384, 384), (768, 384), (1152, 128), (1280, 128), (1408, 256))
PARTS = ((0, 384), (384, 384), (768, 256), (1024, 128), (1152, 256), (1408, 256))
FIRST, SECOND = (0, 1, 2), (3, 4, 5)
ORDERS = (("z", "x", "y"), ("x", "y", "z"), ("y", "z", "x")) * 2
HALO = 32


def place():
    d, s = lax.axis_index("dp"), lax.axis_index("seq")
    return {"y": d // 4, "x": d % 4, "z": s // 2}, s % 2


def dev(coords, core):
    return (coords["y"] * 4 + coords["x"], coords["z"] * 2 + core)


def moved(coords, axis, by):
    out = dict(coords)
    out[axis] = (coords[axis] + by + 4) % 4
    return out


def greet(targets):
    for t in targets:
        pl.semaphore_signal(pltpu.get_barrier_semaphore(), inc=1, device_id=t, device_id_type=MESH)


def greeted(targets):
    pl.semaphore_wait(pltpu.get_barrier_semaphore(), len(targets))


def half_of(index, which):
    at = [isinstance(i, slice) for i in index].index(True)
    return index[:at] + (pl.ds(2 * which, 2),) + index[at + 1 :]


def block_index(coords, full, axis, value):
    out = []
    for a in ("y", "x", "z"):
        if a == axis:
            out.append(value)
        elif a in full:
            out.append(slice(None))
        else:
            out.append(coords[a])
    return tuple(out)


def gather_kernel(
    w_in_ref, w_out_ref, kern_ref, gain_ref, seg_ref, spread, frames_ref, cot_ref,
    out_ref, hc_ref, ln_hbm, glu_hbm, sig_hbm, inv_hbm, mean_hbm, gains, spec, table, across, counts,
    buf, shard, sib, segs, xe, hat, ln, glu, sig, inv_in, mean_in, load_sem, store_sem, sib_sem, halo_send, halo_recv, a_send, a_recv, s_send, s_recv, out_sem,
):
    me, core = place()
    f32, bf = jnp.float32, jnp.bfloat16
    sibling = dev(me, 1 - core)
    seq = lax.axis_index("seq")
    right = (lax.axis_index("dp"), (seq + 1) % 8)
    left = (lax.axis_index("dp"), (seq + 7) % 8)
    cross = dev(moved(me, "z", 2 * core - 1), 1 - core)
    targets = [dev(moved(me, a, b), core) for a in "yxz" for b in (1, -1, 2)] + [sibling, cross]
    greet(targets)
    rows = frames_ref.shape[0]
    load = pltpu.make_async_copy(frames_ref, xe.at[pl.ds(HALO, rows)], load_sem)
    load.start()
    for c in (0, 1):
        at = c * HALFW
        shard[:, at : at + 1024] = w_in_ref[:, c * 1024 : c * 1024 + 1024].astype(f32)
        shard[:, at + 1024 : at + 1152] = jnp.zeros((8, 128), f32)
        shard[:, at + 1152 : at + HALFW] = w_out_ref[:, c * 512 : c * 512 + 512].astype(f32)
    shard[:, 1024 : 1024 + 31] = kern_ref[...].astype(f32)
    eye = lax.broadcasted_iota(jnp.int32, (8, 8), 0) == lax.broadcasted_iota(jnp.int32, (8, 8), 1)
    for n in (0, 1):
        row = jnp.broadcast_to(gain_ref[n : n + 1, :], (8, 8))
        shard[:, 1055 + n : 1056 + n] = jnp.sum(jnp.where(eye, row, 0.0), axis=1, keepdims=True)
    greeted(targets)

    first = pltpu.make_async_remote_copy(
        src_ref=shard, dst_ref=sib, send_sem=sib_sem.at[0], recv_sem=sib_sem.at[1],
        device_id=sibling, device_id_type=MESH)
    first.start()
    halos = []
    for n, (src, dst, h, end) in enumerate(((frames_ref, xe, HALO, HALO + rows), (cot_ref, hc_ref, 16, 16))):
        for m, (at, to, who) in enumerate(((rows - h, 0, right), (0, end, left))):
            halos.append(pltpu.make_async_remote_copy(
                src_ref=src.at[pl.ds(at, h)], dst_ref=dst.at[pl.ds(to, h)],
                send_sem=halo_send.at[n, m], recv_sem=halo_recv.at[n, m],
                device_id=who, device_id_type=MESH))
    for m, who in enumerate((right, left)):
        halos.append(pltpu.make_async_remote_copy(
            src_ref=seg_ref, dst_ref=segs.at[m], send_sem=halo_send.at[2, m], recv_sem=halo_recv.at[2, m],
            device_id=who, device_id_type=MESH))
    first.wait()
    mine, other = shard[...], sib[...]
    low = jnp.where(core == 0, mine[:, :HALFW], other[:, HALFW:])
    high = jnp.where(core == 0, other[:, :HALFW], mine[:, HALFW:])
    buf[me["y"], me["x"], me["z"], :, pl.ds(pl.multiple_of(core * HALFW, 128), HALFW)] = jnp.concatenate(
        [low, high], axis=0).astype(bf)

    def cols(p, c=core):
        return pl.ds(pl.multiple_of(c * HALFW + OUT_PARTS[p][0], 128), OUT_PARTS[p][1])

    def send(p, ph, which, idx, by):
        axis = ORDERS[p][ph]
        ref = buf.at[idx + (slice(None), cols(p))]
        return pltpu.make_async_remote_copy(
            src_ref=ref, dst_ref=ref, send_sem=a_send.at[p, ph, which], recv_sem=a_recv.at[p, ph, which],
            device_id=dev(moved(me, axis, by), core), device_id_type=MESH)

    def to_sibling(p, which, idx, c=core):
        ref = buf.at[idx + (slice(None), cols(p, c))]
        return pltpu.make_async_remote_copy(
            src_ref=ref, dst_ref=ref, send_sem=s_send.at[p, which], recv_sem=s_recv.at[p, which],
            device_id=sibling, device_id_type=MESH)

    def block(p, ph, by):
        axis = ORDERS[p][ph]
        return block_index(me, ORDERS[p][:ph], axis, (me[axis] + by + 4) % 4)

    sends, outs = [], []

    def go(cp):
        cp.start()
        sends.append(cp)

    def start(p, ph):
        if ph > 0:
            for which, by in ((0, -1), (1, 1), (2, 2)):
                send(p, ph - 1, which, block(p, ph - 1, by), by).wait_recv()
        own = block(p, ph, 0)
        for which, by in ((0, 1), (1, -1), (2, 2))[: 3 if ph < 2 else 2]:
            go(send(p, ph, which, own, by))
        if ph == 2:
            go(to_sibling(p, 0, own))

    def pass_on(p):
        for which, by in ((0, -1), (1, 1)):
            idx = block(p, 2, by)
            send(p, 2, which, idx, -by).wait_recv()
            go(send(p, 2, which + 2, half_of(idx, which), -by))
            go(to_sibling(p, 1 + which, idx))

    def flush(p, c, n):
        at = (slice(None),) * 4 + (cols(p, c),)
        cp = pltpu.make_async_copy(buf.at[at], out_ref.at[at], out_sem.at[p, n])
        cp.start()
        outs.append(cp)

    def finish(p):
        idx = block(p, 2, 2)
        for which in (0, 1):
            send(p, 2, 2 + which, half_of(idx, which), 1).wait_recv()
        go(to_sibling(p, 3, idx))
        flush(p, core, 0)

    def from_sibling(p):
        for which, by in ((0, 0), (1, -1), (2, 1), (3, 2)):
            to_sibling(p, which, block(p, 2, by), 1 - core).wait_recv()
        flush(p, 1 - core, 1)

    def strips(i, n):
        return [pl.ds(pl.multiple_of(i * (16 * n) + 16 * u, 16), 16) for u in range(n)]

    def normalise(lo, hi):
        @pl.loop(lo, hi)
        def _(i):
            ats = strips(i, 4)
            xs = [xe[at, :].astype(f32) for at in ats]
            means = [row_mean(x) for x in xs]
            cens = [x - m for x, m in zip(xs, means)]
            invs = [lax.rsqrt(row_mean(c * c) + EPS) for c in cens]
            for at, c, inv, m in zip(ats, cens, invs, means):
                hat[at, :] = c * inv
                inv_in[at, :] = jnp.broadcast_to(inv, (16, 128))
                mean_in[at, :] = jnp.broadcast_to(m, (16, 128))

    def keep(src, dst, n):
        cp = pltpu.make_async_copy(src, dst, store_sem.at[n])
        cp.start()
        outs.append(cp)

    for p in FIRST + SECOND:
        start(p, 0)
    for cp in halos:
        cp.start()
    load.wait()
    normalise(1, 4)
    for p in FIRST + SECOND:
        start(p, 1)
    normalise(4, 12)
    for p in FIRST:
        start(p, 2)
    for cp in halos:
        cp.wait()
    for n in (0, 12):
        normalise(n, n + 1)
    inner = pl.ds(HALO, rows)
    keep(inv_in.at[inner], inv_hbm, 0)
    keep(mean_in.at[inner], mean_hbm, 1)
    own = seg_ref[...]
    before = jnp.where(seq == 0, jnp.broadcast_to(own[:, 0:1] - 1, (1, 128)), segs[0, :, 640:768])
    after = jnp.where(seq == 7, jnp.broadcast_to(own[:, 767:768] + 1, (1, 128)), segs[1, :, 0:128])
    ids = jnp.concatenate(
        [before] + [own[:, n * 128 : n * 128 + 128] for n in range(6)] + [after], axis=0).astype(f32)
    colours(ids, table, across, counts)
    for p in FIRST:
        pass_on(p)
    for p in SECOND:
        start(p, 2)
    for p in FIRST:
        finish(p)
    for p in FIRST:
        from_sibling(p)
    taps = buf[:, :, :, :, 1024:1152].reshape(1024, 128).astype(f32).T
    gains[0:8, :] = jnp.broadcast_to(taps[31:32, :], (8, 1024))
    gains[8:16, :] = jnp.broadcast_to(taps[32:33, :], (8, 1024))

    @pl.loop(0, 13)
    def _(i):
        for at in strips(i, 4):
            ln[at, :] = (hat[at, :] * gains[0:1, :]).astype(bf)
    keep(ln.at[inner], ln_hbm, 2)

    def project(j):
        col = slice(j * 256, j * 256 + 256)
        w0 = buf[:, :, :, :, j * 256 : j * 256 + 256].reshape(1024, 256)
        w1 = buf[:, :, :, :, HALFW + j * 256 : HALFW + j * 256 + 256].reshape(1024, 256)

        @pl.loop(0, 2)
        def _(r):
            at = pl.ds(pl.multiple_of(r * 416, 16), 416)
            lhs = ln[at, :]
            value = mm(lhs, w0)
            s = sigmoid(mm(lhs, w1))
            glu[at, col] = (value * s).astype(bf)
            sig[at, col] = s
        keep(glu.at[:, col], glu_hbm.at[:, col], 3 + 2 * j)
        keep(sig.at[inner, col], sig_hbm.at[:, col], 4 + 2 * j)

    for p in SECOND:
        pass_on(p)
    project(0)
    project(1)
    for p in SECOND:
        finish(p)
    project(2)
    spec[...] = jnp.dot(spread[...], taps, precision=lax.Precision.HIGHEST, preferred_element_type=f32)
    for p in SECOND:
        from_sibling(p)
    project(3)
    for cp in sends:
        cp.wait_send()
    for cp in outs:
        cp.wait()


def gather(w_in, w_out, kern, gain, seg, spread, frames, cot):
    bf = jnp.bfloat16
    vm = pl.BlockSpec(memory_space=pltpu.VMEM)
    hbm = pl.BlockSpec(memory_space=pltpu.HBM)
    return pl.pallas_call(
        gather_kernel,
        out_shape=(
            jax.ShapeDtypeStruct((4, 4, 4, 16, WIDE), bf),
            jax.ShapeDtypeStruct((32, 1024), bf),
            jax.ShapeDtypeStruct((768, 1024), bf),
            jax.ShapeDtypeStruct((832, 1024), bf),
            jax.ShapeDtypeStruct((768, 1024), jnp.float32),
            jax.ShapeDtypeStruct((768, 128), jnp.float32),
            jax.ShapeDtypeStruct((768, 128), jnp.float32),
            jax.ShapeDtypeStruct((16, 1024), jnp.float32),
            jax.ShapeDtypeStruct((NFFT, 1024), jnp.float32),
            jax.ShapeDtypeStruct((12, 8, NFFT), jnp.float32),
            jax.ShapeDtypeStruct((8, NFFT, 128), jnp.float32),
            jax.ShapeDtypeStruct((8, 128), jnp.int32),
        ),
        in_specs=[vm, vm, vm, vm, vm, vm, hbm, hbm],
        out_specs=(hbm, vm, hbm, hbm, hbm, hbm, hbm, vm, vm, vm, vm, vm),
        scratch_shapes=[
            pltpu.VMEM((4, 4, 4, 16, WIDE), bf),
            pltpu.VMEM((8, WIDE), jnp.float32),
            pltpu.VMEM((8, WIDE), jnp.float32),
            pltpu.VMEM((2, 1, 768), jnp.int32),
            pltpu.VMEM((832, 1024), bf),
            pltpu.VMEM((832, 1024), jnp.float32),
            pltpu.VMEM((832, 1024), bf),
            pltpu.VMEM((832, 1024), bf),
            pltpu.VMEM((832, 1024), jnp.float32),
            pltpu.VMEM((832, 128), jnp.float32),
            pltpu.VMEM((832, 128), jnp.float32),
            pltpu.SemaphoreType.DMA,
            pltpu.SemaphoreType.DMA((11,)),
            pltpu.SemaphoreType.DMA((2,)),
            pltpu.SemaphoreType.DMA((3, 2)),
            pltpu.SemaphoreType.DMA((3, 2)),
            pltpu.SemaphoreType.DMA((6, 3, 4)),
            pltpu.SemaphoreType.DMA((6, 3, 4)),
            pltpu.SemaphoreType.DMA((6, 4)),
            pltpu.SemaphoreType.DMA((6, 4)),
            pltpu.SemaphoreType.DMA((6, 2)),
        ],
        compiler_params=pltpu.CompilerParams(
            collective_id=0, has_side_effects=True, vmem_limit_bytes=60 << 20),
        name="gather_weights",
    )(w_in, w_out, kern, gain, seg, spread, frames, cot)


def back_kernel(
    early, ln_hbm, dpre_hbm, w_hbm, frames, cot, inv_hbm, mean_hbm, gains, w_rows, gain,
    o_in, o_out, o_kern, o_vec, out,
    acc, sibbuf, gsend, h0, f0, f1, f2, last, low, fin,
    ln, turned, dpre, w, xe, ce, inv_in, mean_in, work,
    load_sem, d_send, d_recv, a_send, a_recv, e_sem,
):
    scale = 1.0 / math.sqrt(98304.0)
    f32, bf = jnp.float32, jnp.bfloat16
    me, core = place()
    sibling = dev(me, 1 - core)
    full4 = (slice(None),) * 4

    def cp(src, dst, n):
        c = pltpu.make_async_copy(src, dst, load_sem.at[n])
        c.start()
        return c

    def early_cols(c):
        return full4 + (pl.ds(pl.multiple_of(c * 640, 128), 640),)

    def lanes(p):
        return pl.ds(*PARTS[p])

    later = pl.ds(1024, 640)

    loads = [
        cp(ln_hbm, ln, 0),
        cp(dpre_hbm, dpre, 1),
        cp(early.at[early_cols(core)], acc.at[full4 + (later,)], 2),
        cp(w_hbm.at[:, pl.ds(0, 1024)], w.at[:, pl.ds(0, 1024)], 3),
        cp(w_hbm.at[:, pl.ds(HALFW, 1024)], w.at[:, pl.ds(1024, 1024)], 4),
        cp(frames, xe, 5),
        cp(cot, ce, 6),
        cp(inv_hbm, inv_in, 7),
        cp(mean_hbm, mean_in, 8),
    ]
    targets = [dev(moved(me, a, b), core) for a in "yxz" for b in (1, -1, 2)] + [sibling]
    greet(targets)

    def give(p):
        src = early.at[early_cols(1 - core)] if p == 3 else gsend.at[full4 + (lanes(p),)]
        return pltpu.make_async_remote_copy(
            src_ref=src, dst_ref=sibbuf.at[full4 + (later if p == 3 else lanes(p),)],
            send_sem=d_send.at[p], recv_sem=d_recv.at[p], device_id=sibling, device_id_type=MESH)

    sends = []

    def go(c):
        c.start()
        sends.append(c)

    def axis_of(p, ph):
        return ORDERS[p][2 - ph]

    def block(p, ph, by):
        axis = axis_of(p, ph)
        return block_index(me, ORDERS[p][: 2 - ph], axis, (me[axis] + by + 4) % 4)

    def send_half(p, which):
        return pltpu.make_async_remote_copy(
            src_ref=acc.at[half_of(block(p, 0, 2), which) + (slice(None), lanes(p))],
            dst_ref=h0.at[pl.ds(2 * which, 2), :, :, lanes(p)],
            send_sem=a_send.at[p, 0, which], recv_sem=a_recv.at[p, 0, which],
            device_id=dev(moved(me, axis_of(p, 0), (1, -1)[which]), core), device_id_type=MESH)

    def send_full(p, ph, which):
        by = (1, -1, 2)[which]
        dst = (f0, f1, f2)[ph].at[(which,) + (slice(None),) * (3 - ph) + (lanes(p),)]
        return pltpu.make_async_remote_copy(
            src_ref=acc.at[block(p, ph, by) + (slice(None), lanes(p))], dst_ref=dst,
            send_sem=a_send.at[p, ph, 2 + which], recv_sem=a_recv.at[p, ph, 2 + which],
            device_id=dev(moved(me, axis_of(p, ph), by), core), device_id_type=MESH)

    def over(p, ph, value, body, span=(0, 4)):
        axis, full = axis_of(p, ph), ORDERS[p][: 2 - ph]
        names = [a for a in "yxz" if a in full]

        def at(k):
            by_name = {axis: value}
            if len(names) == 2:
                by_name[names[0]] = k
                by_name[names[1]] = slice(None)
            elif len(names) == 1:
                by_name[names[0]] = slice(None)
            return tuple(by_name[a] if a in by_name else me[a] for a in "yxz")

        if len(names) == 2:
            @pl.loop(*span)
            def _(k):
                body(at(k), (k, slice(None)))
        else:
            body(at(0), (slice(None),) * len(names))

    def start_halves(p):
        for which in (0, 1):
            go(send_half(p, which))

    def pass_on(p):
        axis = axis_of(p, 0)
        for which, by in ((0, 1), (1, -1)):
            send_half(p, which).wait_recv()

            def body(at, dig):
                at = at + (slice(None), lanes(p))
                acc[at] = (acc[at].astype(f32) + h0[dig + (slice(None), lanes(p))].astype(f32)).astype(bf)
            over(p, 0, (me[axis] + by + 4) % 4, body, (2 * which, 2 * which + 2))
            go(send_full(p, 0, which))

    def take(p, ph):
        count = 2 if ph == 0 else 3
        ref = (f0, f1, f2)[ph]
        for which in range(count):
            send_full(p, ph, which).wait_recv()
        sl = lanes(p)

        def body(at, dig):
            at = at + (slice(None), sl)
            total = acc[at].astype(f32)
            for which in range(count):
                total = total + ref[(which,) + dig + (slice(None), sl)].astype(f32)
            if ph < 2:
                acc[at] = total.astype(bf)
            else:
                last[:, sl] = total
        over(p, ph, me[axis_of(p, ph)], body)
        if ph < 2:
            for which in range(3):
                go(send_full(p, ph + 1, which))

    def product(p, half, store):
        at, width = PARTS[p]

        @pl.loop(0, 4)
        def _(y):
            lhs = turned[pl.ds(pl.multiple_of(y * 256, 256), 256), :]
            rhs = dpre[:, pl.ds(pl.multiple_of(half * 1024 + at, 128), width)]
            r = jnp.dot(lhs, rhs, preferred_element_type=f32) * scale
            store(y, r.reshape(4, 4, 16, width))

    def for_sibling(p):
        def store(y, r):
            gsend[y, :, :, :, lanes(p)] = r.astype(bf)
        product(p, 1 - core, store)

    def for_own(p):
        give(p).wait_recv()

        def store(y, r):
            acc[y, :, :, :, lanes(p)] = (r + sibbuf[y, :, :, :, lanes(p)].astype(f32)).astype(bf)
        product(p, core, store)
        start_halves(p)

    def input_product(j):
        col = slice(j * 256, j * 256 + 256)
        work[:, col] = lax.dot_general(dpre[...], w[col, :], (((1,), (1,)), ((), ())), preferred_element_type=f32)

    def input_rows(n):
        @pl.loop(3 * n, 3 * n + 3)
        def _(i):
            ats = [pl.ds(pl.multiple_of(i * 64 + 16 * u, 16), 16) for u in range(4)]
            gain = gains[0:1, :]
            invs = [inv_in[at, 0:1] for at in ats]
            normals = [(xe[at, :].astype(f32) - mean_in[at, 0:1]) * inv for at, inv in zip(ats, invs)]
            us = [work[at, :] * gain for at in ats]
            m1 = [row_mean(u) for u in us]
            m2 = [row_mean(u * n) for u, n in zip(us, normals)]
            for at, inv, u, n, a, b in zip(ats, invs, us, normals, m1, m2):
                out[at, :] = (ce[at, :].astype(f32) + inv * (u - a - n * b)).astype(bf)

    loads[0].wait()
    turned[...] = ln[...].T
    loads[1].wait()
    for_sibling(0)
    greeted(targets)
    go(give(3))
    go(give(0))
    for_sibling(1)
    go(give(1))
    loads[2].wait()
    give(3).wait_recv()

    @pl.loop(0, 4)
    def _(y):
        at = (y, slice(None), slice(None), slice(None), later)
        acc[at] = (acc[at].astype(f32) + sibbuf[at].astype(f32)).astype(bf)
    for p in SECOND:
        start_halves(p)
    for_sibling(2)
    go(give(2))
    for_own(0)
    for p in SECOND:
        pass_on(p)
    for_own(1)
    for_own(2)
    pass_on(0)
    for n in (3, 4):
        loads[n].wait()
    input_product(0)
    pass_on(1)
    pass_on(2)
    for p in SECOND:
        take(p, 0)
    input_product(1)
    take(0, 0)
    input_product(2)
    for p in SECOND:
        take(p, 1)
    take(1, 0)
    take(2, 0)
    input_product(3)
    for n in (5, 6, 7, 8):
        loads[n].wait()
    take(0, 1)
    for p in SECOND:
        take(p, 2)
    input_rows(0)
    take(1, 1)
    take(2, 1)
    input_rows(1)
    take(0, 2)
    input_rows(2)
    take(1, 2)
    take(2, 2)
    top, bottom = last[0:8, :], last[8:16, :]
    low[...] = jnp.where(core == 0, bottom, top)
    swap = pltpu.make_async_remote_copy(
        src_ref=low, dst_ref=fin, send_sem=e_sem.at[0], recv_sem=e_sem.at[1], device_id=sibling, device_id_type=MESH)
    swap.start()
    input_rows(3)
    mine = jnp.where(core == 0, top, bottom)
    swap.wait()
    theirs = fin[...]
    total = jnp.zeros((8, 1), f32)
    for c in (0, 1):
        own = jnp.where(core == c, mine, theirs)
        o_in[:, c * 1024 : c * 1024 + 1024] = own[:, :1024]
        o_out[:, c * 512 : c * 512 + 512] = own[:, 1152:1664]
        rows = w_rows[:, c * 1024 : c * 1024 + 1024].astype(f32)
        total = total + jnp.sum(rows * own[:, :1024], axis=-1, keepdims=True)
        if c == 0:
            rest = own[:, 1024:1152]
    eye = lax.broadcasted_iota(jnp.int32, (8, 8), 0) == lax.broadcasted_iota(jnp.int32, (8, 8), 1)
    column = jnp.sum(jnp.where(eye, jnp.broadcast_to(gain[0:1, :], (8, 8)), 0.0), axis=1, keepdims=True)
    o_kern[...] = rest[:, 0:31]
    pair = []
    for v in (total / column, rest[:, 32:33]):
        pair.append(jnp.sum(jnp.where(eye, jnp.broadcast_to(v, (8, 8)), 0.0), axis=0, keepdims=True))
    o_vec[...] = jnp.concatenate(pair, axis=0)
    for c in sends:
        c.wait_send()


def back(early, ln, dpre, w, frames, cot, inv, mean, gains, w_rows, gain):
    bf, f32 = jnp.bfloat16, jnp.float32
    vm = pl.BlockSpec(memory_space=pltpu.VMEM)
    hbm = pl.BlockSpec(memory_space=pltpu.HBM)
    V = pltpu.VMEM
    return pl.pallas_call(
        back_kernel,
        out_shape=(
            jax.ShapeDtypeStruct((8, 2048), f32),
            jax.ShapeDtypeStruct((8, 1024), f32),
            jax.ShapeDtypeStruct((8, 31), f32),
            jax.ShapeDtypeStruct((2, 8), f32),
            jax.ShapeDtypeStruct((768, 1024), bf),
        ),
        in_specs=[hbm] * 8 + [vm] * 3,
        out_specs=(vm, vm, vm, vm, vm),
        scratch_shapes=[
            V((4, 4, 4, 16, HALFW), bf),
            V((4, 4, 4, 16, HALFW), bf),
            V((4, 4, 4, 16, 1024), bf),
            V((4, 4, 16, HALFW), bf),
            V((2, 4, 4, 16, HALFW), bf),
            V((3, 4, 16, HALFW), bf),
            V((3, 16, HALFW), bf),
            V((16, HALFW), f32),
            V((8, HALFW), f32),
            V((8, HALFW), f32),
            V((768, 1024), bf),
            V((1024, 768), bf),
            V((768, 2048), bf),
            V((1024, 2048), bf),
            V((768, 1024), bf),
            V((768, 1024), bf),
            V((768, 128), f32),
            V((768, 128), f32),
            V((768, 1024), f32),
            pltpu.SemaphoreType.DMA((10,)),
            pltpu.SemaphoreType.DMA((4,)),
            pltpu.SemaphoreType.DMA((4,)),
            pltpu.SemaphoreType.DMA((6, 3, 5)),
            pltpu.SemaphoreType.DMA((6, 3, 5)),
            pltpu.SemaphoreType.DMA((2,)),
        ],
        compiler_params=pltpu.CompilerParams(
            collective_id=1, has_side_effects=True, vmem_limit_bytes=60 << 20),
        name="back_and_scatter",
    )(early, ln, dpre, w, frames, cot, inv, mean, gains, w_rows, gain)


EPS = 1e-05
HALF = 15
ROWS = 768
D = 1024
NFFT = 256


def tables():
    omega = 2 * np.pi * (np.arange(128) + 0.5) / NFFT
    phase = omega[:, None] * np.arange(NFFT)[None]
    basis = np.concatenate([np.cos(phase), -np.sin(phase)], axis=0)
    lag = omega[:, None] * (np.arange(31) - HALF)[None]
    spread = np.zeros((NFFT, 128))
    spread[:, :31] = np.concatenate([np.cos(lag), np.sin(lag)], axis=0) * (2 / NFFT)
    back = np.zeros((128, NFFT))
    back[:31] = np.concatenate([np.cos(lag), -np.sin(lag)], axis=0).T * (2 / NFFT)
    f32 = jnp.float32
    return (jnp.asarray(basis, f32), jnp.asarray(basis.T, f32), jnp.asarray(spread, f32), jnp.asarray(back, f32))


def sigmoid(v):
    return 0.5 * jnp.tanh(0.5 * v) + 0.5


NT = (((1,), (1,)), ((), ()))
TN = (((0,), (0,)), ((), ()))
F32 = jnp.float32
BF = jnp.bfloat16


def nt(a, b):
    return lax.dot_general(a, b, NT, preferred_element_type=F32)


def mm(a, b):
    return jnp.dot(a, b, preferred_element_type=F32)


def row_mean(v):
    return jnp.sum(v, axis=-1, keepdims=True) * (1.0 / D)


FWD_AT, BWD_AT = (0, 208, 416, 592), (16, 208, 400, 592)


def colours(ids, table, across, counts):
    lane = lax.broadcasted_iota(jnp.int32, (1, 128), 1)
    wide = lax.broadcasted_iota(jnp.int32, (1, NFFT), 1)
    for n, at in enumerate(FWD_AT + BWD_AT):
        length = 240 if n < 4 else 224
        r, o = divmod(at + 96, 128)

        def piece(k, o=o):
            if o == 0:
                return ids[k : k + 1, :]
            first = pltpu.roll(ids[k : k + 1, :], 128 - o, 1)
            return jnp.where(lane < 128 - o, first, pltpu.roll(ids[min(k + 1, 7) : min(k + 1, 7) + 1, :], 128 - o, 1))

        own = jnp.concatenate([piece(r), piece(r + 1)], axis=1)
        step = jnp.where(wide < length - HALF, pltpu.roll(own, NFFT - HALF, 1) - own, 0.0)
        count = jnp.max(step, axis=1, keepdims=True) + 1.0
        own = own + 1.0
        own = own - count * jnp.floor((own + 0.5) / count)
        own = jnp.where(wide < length, own, -1.0)
        rows = jnp.broadcast_to(own, (8, NFFT))
        table[n] = rows
        across[n] = jnp.broadcast_to(rows.T[:, 0:1], (NFFT, 128))
        if n >= 4:
            table[n + 4] = jnp.where((wide >= 16) & (wide < 208), rows, -1.0)
        counts[n : n + 1, :] = jnp.broadcast_to(count, (1, 128)).astype(jnp.int32)


def mid_kernel(
    counts, gains, basis, turned, back, frames, cot, hc, w_hbm, glu_hbm, sig_hbm, spec_hbm, table_hbm, across_hbm,
    out_hbm, dpre_hbm, early_hbm,
    xe, ce, w, glu, sig, mixed, work, act, dm, dpre, g, spec, prod, extra, table, across, out, sems,
):
    scale = 1.0 / math.sqrt(98304.0)

    def cp(src, dst, n):
        c = pltpu.make_async_copy(src, dst, sems.at[n])
        c.start()
        return c

    cols = lambda lo, n: (slice(None), pl.ds(lo, n))
    loads = [
        cp(table_hbm, table, 0),
        cp(across_hbm, across, 1),
        cp(spec_hbm, spec, 2),
        cp(glu_hbm, glu.at[pl.ds(0, 832)], 3),
        cp(cot, ce.at[pl.ds(16, ROWS)], 4),
        cp(hc.at[pl.ds(0, 16)], ce.at[pl.ds(0, 16)], 5),
        cp(hc.at[pl.ds(16, 16)], ce.at[pl.ds(784, 16)], 6),
        cp(w_hbm.at[cols(1152, 512)], w.at[cols(0, 512)], 7),
        cp(w_hbm.at[cols(2816, 512)], w.at[cols(512, 512)], 8),
        cp(frames, xe, 9),
        cp(sig_hbm, sig, 10),
    ]
    glu[pl.ds(832, 16), :] = jnp.zeros((16, D), BF)
    dm[pl.ds(800, 32), :] = jnp.zeros((32, D), BF)
    prod[...] = jnp.zeros((NFFT, D), F32)
    extra[...] = jnp.zeros((128, D), F32)
    stores = []
    for n in range(4):
        loads[n].wait()

    def strips(i, n, off=0):
        return [pl.ds(pl.multiple_of(i * (16 * n) + off + 16 * u, 16), 16) for u in range(n)]

    def picked(row, first, k):
        return jnp.concatenate(
            [jnp.where(table[row, 0:1, :] == (first + c).astype(F32), basis[...], 0.0) for c in range(k)],
            axis=0).astype(BF)

    def placed(row, first, k, lo, hi):
        own = across[row, lo:hi, :]
        own = jnp.concatenate([own, own], axis=1)
        return jnp.concatenate(
            [jnp.where(own == (first + c).astype(F32), turned[lo:hi, :], 0.0) for c in range(k)], axis=1).astype(BF)

    def forward(wi, first, k, add):
        base = pl.multiple_of(jnp.minimum(wi * 208, 592), 16)
        to = picked(wi, first, k)
        fro = placed(wi, first, k, 16, 224)
        for j in range(4):
            col = slice(j * 256, j * 256 + 256)
            x = mm(to, glu[pl.ds(base, 256), col])
            hr, hi = spec[:128, col], spec[128:, col]
            ys = []
            for c in range(k):
                xr, xi = x[256 * c : 256 * c + 128], x[256 * c + 128 : 256 * c + 256]
                ys += [(xr * hr - xi * hi).astype(BF), (xr * hi + xi * hr).astype(BF)]
            y = mm(fro, jnp.concatenate(ys, axis=0))
            if add:
                mixed[pl.ds(base, 208), col] += y
            else:
                mixed[pl.ds(base, 208), col] = y

    def backward(wi, first, k, add):
        base = pl.multiple_of(wi * 192, 16)
        to = picked(4 + wi, first, k)
        mid_to = picked(8 + wi, first, k)
        fro = placed(4 + wi, first, k, 16, 208)
        for j in range(4):
            col = slice(j * 256, j * 256 + 256)
            d = mm(to, dm[pl.ds(base, 256), col])
            q = mm(mid_to, glu[pl.ds(base + 16, 256), col])
            hr, hi = spec[:128, col], spec[128:, col]
            ys = []
            pr, pi = prod[:128, col], prod[128:, col]
            for c in range(k):
                lo, mi, up = 256 * c, 256 * c + 128, 256 * c + 256
                dr, di, qr, qi = d[lo:mi], d[mi:up], q[lo:mi], q[mi:up]
                ys += [(dr * hr + di * hi).astype(BF), (di * hr - dr * hi).astype(BF)]
                pr = pr + (qr * dr + qi * di)
                pi = pi + (qi * dr - qr * di)
            prod[:128, col] = pr
            prod[128:, col] = pi
            y = mm(fro, jnp.concatenate(ys, axis=0))
            if add:
                mixed[pl.ds(base, 192), col] += y
            else:
                mixed[pl.ds(base, 192), col] = y

    def by_class(run, wi, count):
        zero = jnp.int32(0)

        @pl.when(count <= 2)
        def _():
            run(wi, zero, 2, False)

        @pl.when(count == 3)
        def _():
            run(wi, zero, 3, False)

        @pl.when(count > 3)
        def _():
            run(wi, zero, 4, False)

            @pl.loop(0, (count - 3) // 2)
            def _(n):
                run(wi, 4 + n * 2, 2, True)

    @pl.loop(0, 4)
    def _(wi):
        by_class(forward, wi, counts[wi, 0])

    for n in range(4, 11):
        loads[n].wait()

    @pl.loop(0, 4)
    def _(j):
        col = pl.ds(pl.multiple_of(j * 256, 256), 256)
        work[:, col] = nt(ce[...], w[col, :])

    def mid_rows(ats, central):
        gain = gains[8:9, :]
        cens = [mixed[at, :] for at in ats]
        cens = [m - row_mean(m) for m in cens]
        invs = [lax.rsqrt(row_mean(c * c) + EPS) for c in cens]
        normals = [c * inv for c, inv in zip(cens, invs)]
        us = []
        for at, normal in zip(ats, normals):
            y = normal * gain
            s = sigmoid(y)
            ys = y * s
            act[at, :] = ys.astype(BF)
            d_ln = work[at, :] * (s + ys * (1.0 - s))
            if central:
                dn = d_ln * normal
                extra[40:48, :] += dn[:8] + dn[8:]
            us.append(d_ln * gain)
        m1 = [row_mean(u) for u in us]
        m2 = [row_mean(u * n) for u, n in zip(us, normals)]
        for at, inv, u, n, a, b in zip(ats, invs, us, normals, m1, m2):
            dm[at, :] = (inv * (u - a - n * b)).astype(BF)

    mid_rows([pl.ds(0, 16), pl.ds(784, 16)], False)

    @pl.loop(0, 12)
    def _(i):
        mid_rows(strips(i, 4, 16), True)

    @pl.loop(0, 4)
    def _(j):
        col = pl.ds(pl.multiple_of(j * 256, 256), 256)
        y = mm(act[16:784, :], w[:, col])
        out[:, col] = (xe[:, col].astype(F32) + y).astype(BF)
        lhs = act[16:784, col].T
        r = (mm(lhs, ce[16:784, :]) * scale).astype(BF)
        g[col, 128:640] = r[:, :512]
        g[col, 768:1280] = r[:, 512:]

    stores.append(cp(out, out_hbm, 11))

    @pl.loop(0, 4)
    def _(wi):
        by_class(backward, wi, counts[4 + wi, 0])

    gk = jnp.dot(back[...], prod[...], precision=lax.Precision.HIGHEST, preferred_element_type=F32)
    extra[0:31, :] = gk[0:31]
    g_mid = jnp.sum(extra[40:48, :], axis=0, keepdims=True)
    extra[32:33, :] = g_mid
    g[:, 0:128] = (extra[...].T * scale).astype(BF)
    g[:, 640:768] = jnp.zeros((D, 128), BF)
    stores.append(cp(g, early_hbm, 12))

    for q in range(4):
        @pl.loop(q * 6, q * 6 + 6)
        def _(i):
            for u in range(2):
                at = pl.ds(pl.multiple_of(i * 32 + 16 * u, 16), 16)
                ext = pl.ds(pl.multiple_of(i * 32 + 16 * u + 32, 16), 16)
                d = mixed[at, :]
                s = sig[at, :]
                dpre[at, :1024] = (d * s).astype(BF)
                dpre[at, 1024:] = (d * glu[ext, :].astype(F32) * (1.0 - s)).astype(BF)

        part = pl.ds(q * 192, 192)
        stores.append(cp(dpre.at[part], dpre_hbm.at[part], 13 + q))
    for s in stores:
        s.wait()


def mid(counts, gains, consts, *rest):
    vm = pl.BlockSpec(memory_space=pltpu.VMEM)
    hbm = pl.BlockSpec(memory_space=pltpu.HBM)
    V = pltpu.VMEM
    return pl.pallas_call(
        mid_kernel,
        out_shape=(
            jax.ShapeDtypeStruct((ROWS, D), BF),
            jax.ShapeDtypeStruct((ROWS, 2 * D), BF),
            jax.ShapeDtypeStruct((D, 1280), BF),
        ),
        in_specs=[pl.BlockSpec(memory_space=pltpu.SMEM), vm, vm, vm, vm] + [hbm] * 9,
        out_specs=(hbm,) * 3,
        scratch_shapes=[
            V((768, D), BF), V((800, D), BF), V((D, D), BF),
            V((848, D), BF), V((768, D), F32),
            V((800, D), F32), V((800, D), F32), V((800, D), BF), V((832, D), BF),
            V((768, 2 * D), BF), V((D, 1280), BF), V((NFFT, D), F32), V((NFFT, D), F32),
            V((128, D), F32), V((12, 8, NFFT), F32), V((8, NFFT, 128), F32), V((ROWS, D), BF),
            pltpu.SemaphoreType.DMA((17,)),
        ],
        compiler_params=pltpu.CompilerParams(vmem_limit_bytes=60 << 20),
        name="block_pass",
    )(counts, gains, *consts, *rest)


def shards(frames, cotangent, segments, w_in, w_out, kernel, gain_in, gain_mid):
    gain = jnp.stack([gain_in, gain_mid]).astype(F32)
    x, cot = frames[0], cotangent[0]
    basis, turned, spread, back_table = tables()
    full, c_halo, ln, glu, sig, inv, mean, gains, spec, table, across, counts = gather(
        w_in, w_out, kernel, gain, segments, spread, x, cot)
    full = full.reshape(D, WIDE)
    block_out, dpre, early = mid(
        counts, gains, (basis, turned, back_table), x, cot, c_halo, full, glu, sig, spec, table, across)
    g_in, g_out, g_kern, g_vec, input_grad = back(
        early.reshape(4, 4, 4, 16, 1280), ln, dpre, full, x, cot, inv, mean, gains, w_in, gain)
    return (block_out[None], input_grad[None], g_in, g_out, g_kern, g_vec[0], g_vec[1])


def solution(mesh):
    rows = P("dp", "seq", None)
    mat = P(("dp", "seq"), None)
    vec = P(("dp", "seq"))
    return jax.shard_map(
        shards, mesh=mesh, in_specs=(rows, rows, P("dp", "seq"), mat, mat, mat, vec, vec),
        out_specs=(rows, rows, mat, mat, mat, vec, vec), check_vma=False)
```

```python
import math

import jax
import jax.numpy as jnp
import numpy as np
from jax import lax
from jax.experimental import pallas as pl
from jax.experimental.pallas import tpu as pltpu
from jax.sharding import PartitionSpec as P

MESH = pl.DeviceIdType.MESH
HALFW = 1664
WIDE = 2 * HALFW
OUT_PARTS = ((0, 384), (384, 384), (768, 384), (1152, 128), (1280, 128), (1408, 256))
PARTS = ((0, 384), (384, 384), (768, 256), (1024, 128), (1152, 256), (1408, 256))
FIRST, SECOND = (0, 1, 2), (3, 4, 5)
ORDERS = (("z", "x", "y"), ("x", "y", "z"), ("y", "z", "x")) * 2
HALO = 32


def place():
    d, s = lax.axis_index("dp"), lax.axis_index("seq")
    return {"y": d // 4, "x": d % 4, "z": s // 2}, s % 2


def dev(coords, core):
    return (coords["y"] * 4 + coords["x"], coords["z"] * 2 + core)


def moved(coords, axis, by):
    out = dict(coords)
    out[axis] = (coords[axis] + by + 4) % 4
    return out


def greet(targets):
    for t in targets:
        pl.semaphore_signal(pltpu.get_barrier_semaphore(), inc=1, device_id=t, device_id_type=MESH)


def greeted(targets):
    pl.semaphore_wait(pltpu.get_barrier_semaphore(), len(targets))


def half_of(index, which):
    at = [isinstance(i, slice) for i in index].index(True)
    return index[:at] + (pl.ds(2 * which, 2),) + index[at + 1 :]


def block_index(coords, full, axis, value):
    out = []
    for a in ("y", "x", "z"):
        if a == axis:
            out.append(value)
        elif a in full:
            out.append(slice(None))
        else:
            out.append(coords[a])
    return tuple(out)


def gather_kernel(
    w_in_ref, w_out_ref, kern_ref, gain_ref, seg_ref, spread, frames_ref, cot_ref,
    out_ref, hc_ref, ln_hbm, glu_hbm, sig_hbm, inv_hbm, mean_hbm, gains, spec, table, across, counts,
    buf, shard, sib, segs, xe, hat, ln, glu, sig, inv_in, mean_in, load_sem, store_sem, sib_sem, halo_send, halo_recv, a_send, a_recv, s_send, s_recv, out_sem,
):
    me, core = place()
    f32, bf = jnp.float32, jnp.bfloat16
    sibling = dev(me, 1 - core)
    seq = lax.axis_index("seq")
    right = (lax.axis_index("dp"), (seq + 1) % 8)
    left = (lax.axis_index("dp"), (seq + 7) % 8)
    cross = dev(moved(me, "z", 2 * core - 1), 1 - core)
    targets = [dev(moved(me, a, b), core) for a in "yxz" for b in (1, -1, 2)] + [sibling, cross]
    greet(targets)
    rows = frames_ref.shape[0]
    load = pltpu.make_async_copy(frames_ref, xe.at[pl.ds(HALO, rows)], load_sem)
    load.start()
    for c in (0, 1):
        at = c * HALFW
        shard[:, at : at + 1024] = w_in_ref[:, c * 1024 : c * 1024 + 1024].astype(f32)
        shard[:, at + 1024 : at + 1152] = jnp.zeros((8, 128), f32)
        shard[:, at + 1152 : at + HALFW] = w_out_ref[:, c * 512 : c * 512 + 512].astype(f32)
    shard[:, 1024 : 1024 + 31] = kern_ref[...].astype(f32)
    eye = lax.broadcasted_iota(jnp.int32, (8, 8), 0) == lax.broadcasted_iota(jnp.int32, (8, 8), 1)
    for n in (0, 1):
        row = jnp.broadcast_to(gain_ref[n : n + 1, :], (8, 8))
        shard[:, 1055 + n : 1056 + n] = jnp.sum(jnp.where(eye, row, 0.0), axis=1, keepdims=True)
    greeted(targets)

    first = pltpu.make_async_remote_copy(
        src_ref=shard, dst_ref=sib, send_sem=sib_sem.at[0], recv_sem=sib_sem.at[1],
        device_id=sibling, device_id_type=MESH)
    first.start()
    halos = []
    for n, (src, dst, h, end) in enumerate(((frames_ref, xe, HALO, HALO + rows), (cot_ref, hc_ref, 16, 16))):
        for m, (at, to, who) in enumerate(((rows - h, 0, right), (0, end, left))):
            halos.append(pltpu.make_async_remote_copy(
                src_ref=src.at[pl.ds(at, h)], dst_ref=dst.at[pl.ds(to, h)],
                send_sem=halo_send.at[n, m], recv_sem=halo_recv.at[n, m],
                device_id=who, device_id_type=MESH))
    for m, who in enumerate((right, left)):
        halos.append(pltpu.make_async_remote_copy(
            src_ref=seg_ref, dst_ref=segs.at[m], send_sem=halo_send.at[2, m], recv_sem=halo_recv.at[2, m],
            device_id=who, device_id_type=MESH))
    first.wait()
    mine, other = shard[...], sib[...]
    low = jnp.where(core == 0, mine[:, :HALFW], other[:, HALFW:])
    high = jnp.where(core == 0, other[:, :HALFW], mine[:, HALFW:])
    buf[me["y"], me["x"], me["z"], :, pl.ds(pl.multiple_of(core * HALFW, 128), HALFW)] = jnp.concatenate(
        [low, high], axis=0).astype(bf)

    def cols(p, c=core):
        return pl.ds(pl.multiple_of(c * HALFW + OUT_PARTS[p][0], 128), OUT_PARTS[p][1])

    def send(p, ph, which, idx, by):
        axis = ORDERS[p][ph]
        ref = buf.at[idx + (slice(None), cols(p))]
        return pltpu.make_async_remote_copy(
            src_ref=ref, dst_ref=ref, send_sem=a_send.at[p, ph, which], recv_sem=a_recv.at[p, ph, which],
            device_id=dev(moved(me, axis, by), core), device_id_type=MESH)

    def to_sibling(p, which, idx, c=core):
        ref = buf.at[idx + (slice(None), cols(p, c))]
        return pltpu.make_async_remote_copy(
            src_ref=ref, dst_ref=ref, send_sem=s_send.at[p, which], recv_sem=s_recv.at[p, which],
            device_id=sibling, device_id_type=MESH)

    def block(p, ph, by):
        axis = ORDERS[p][ph]
        return block_index(me, ORDERS[p][:ph], axis, (me[axis] + by + 4) % 4)

    sends, outs = [], []

    def go(cp):
        cp.start()
        sends.append(cp)

    def start(p, ph):
        if ph > 0:
            for which, by in ((0, -1), (1, 1), (2, 2)):
                send(p, ph - 1, which, block(p, ph - 1, by), by).wait_recv()
        own = block(p, ph, 0)
        for which, by in ((0, 1), (1, -1), (2, 2))[: 3 if ph < 2 else 2]:
            go(send(p, ph, which, own, by))
        if ph == 2:
            go(to_sibling(p, 0, own))

    def pass_on(p):
        for which, by in ((0, -1), (1, 1)):
            idx = block(p, 2, by)
            send(p, 2, which, idx, -by).wait_recv()
            go(send(p, 2, which + 2, half_of(idx, which), -by))
            go(to_sibling(p, 1 + which, idx))

    def flush(p, c, n):
        at = (slice(None),) * 4 + (cols(p, c),)
        cp = pltpu.make_async_copy(buf.at[at], out_ref.at[at], out_sem.at[p, n])
        cp.start()
        outs.append(cp)

    def finish(p):
        idx = block(p, 2, 2)
        for which in (0, 1):
            send(p, 2, 2 + which, half_of(idx, which), 1).wait_recv()
        go(to_sibling(p, 3, idx))
        flush(p, core, 0)

    def from_sibling(p):
        for which, by in ((0, 0), (1, -1), (2, 1), (3, 2)):
            to_sibling(p, which, block(p, 2, by), 1 - core).wait_recv()
        flush(p, 1 - core, 1)

    def strips(i, n):
        return [pl.ds(pl.multiple_of(i * (16 * n) + 16 * u, 16), 16) for u in range(n)]

    def normalise(lo, hi):
        @pl.loop(lo, hi)
        def _(i):
            ats = strips(i, 4)
            xs = [xe[at, :].astype(f32) for at in ats]
            means = [row_mean(x) for x in xs]
            cens = [x - m for x, m in zip(xs, means)]
            invs = [lax.rsqrt(row_mean(c * c) + EPS) for c in cens]
            for at, c, inv, m in zip(ats, cens, invs, means):
                hat[at, :] = c * inv
                inv_in[at, :] = jnp.broadcast_to(inv, (16, 128))
                mean_in[at, :] = jnp.broadcast_to(m, (16, 128))

    def keep(src, dst, n):
        cp = pltpu.make_async_copy(src, dst, store_sem.at[n])
        cp.start()
        outs.append(cp)

    for p in FIRST + SECOND:
        start(p, 0)
    for cp in halos:
        cp.start()
    load.wait()
    normalise(1, 4)
    for p in FIRST + SECOND:
        start(p, 1)
    normalise(4, 12)
    for p in FIRST:
        start(p, 2)
    for cp in halos:
        cp.wait()
    for n in (0, 12):
        normalise(n, n + 1)
    inner = pl.ds(HALO, rows)
    keep(inv_in.at[inner], inv_hbm, 0)
    keep(mean_in.at[inner], mean_hbm, 1)
    own = seg_ref[...]
    before = jnp.where(seq == 0, jnp.broadcast_to(own[:, 0:1] - 1, (1, 128)), segs[0, :, 640:768])
    after = jnp.where(seq == 7, jnp.broadcast_to(own[:, 767:768] + 1, (1, 128)), segs[1, :, 0:128])
    ids = jnp.concatenate(
        [before] + [own[:, n * 128 : n * 128 + 128] for n in range(6)] + [after], axis=0).astype(f32)
    colours(ids, table, across, counts)
    for p in FIRST:
        pass_on(p)
    for p in SECOND:
        start(p, 2)
    for p in FIRST:
        finish(p)
    for p in FIRST:
        from_sibling(p)
    taps = buf[:, :, :, :, 1024:1152].reshape(1024, 128).astype(f32).T
    gains[0:8, :] = jnp.broadcast_to(taps[31:32, :], (8, 1024))
    gains[8:16, :] = jnp.broadcast_to(taps[32:33, :], (8, 1024))

    @pl.loop(0, 13)
    def _(i):
        for at in strips(i, 4):
            ln[at, :] = (hat[at, :] * gains[0:1, :]).astype(bf)
    keep(ln.at[inner], ln_hbm, 2)

    def project(j):
        col = slice(j * 256, j * 256 + 256)
        w0 = buf[:, :, :, :, j * 256 : j * 256 + 256].reshape(1024, 256)
        w1 = buf[:, :, :, :, HALFW + j * 256 : HALFW + j * 256 + 256].reshape(1024, 256)

        pairs = []
        for r in (0, 1):
            lhs = ln[r * 416 : r * 416 + 416, :]
            pairs.append((mm(lhs, w0), mm(lhs, w1)))
        for r, (value, gate) in enumerate(pairs):
            at = slice(r * 416, r * 416 + 416)
            s = sigmoid(gate)
            glu[at, col] = (value * s).astype(bf)
            sig[at, col] = s
        keep(glu.at[:, col], glu_hbm.at[:, col], 3 + 2 * j)
        keep(sig.at[inner, col], sig_hbm.at[:, col], 4 + 2 * j)

    for p in SECOND:
        pass_on(p)
    project(0)
    project(1)
    for p in SECOND:
        finish(p)
    project(2)
    spec[...] = jnp.dot(spread[...], taps, precision=lax.Precision.HIGHEST, preferred_element_type=f32)
    for p in SECOND:
        from_sibling(p)
    project(3)
    for cp in sends:
        cp.wait_send()
    for cp in outs:
        cp.wait()


def gather(w_in, w_out, kern, gain, seg, spread, frames, cot):
    bf = jnp.bfloat16
    vm = pl.BlockSpec(memory_space=pltpu.VMEM)
    hbm = pl.BlockSpec(memory_space=pltpu.HBM)
    return pl.pallas_call(
        gather_kernel,
        out_shape=(
            jax.ShapeDtypeStruct((4, 4, 4, 16, WIDE), bf),
            jax.ShapeDtypeStruct((32, 1024), bf),
            jax.ShapeDtypeStruct((768, 1024), bf),
            jax.ShapeDtypeStruct((832, 1024), bf),
            jax.ShapeDtypeStruct((768, 1024), jnp.float32),
            jax.ShapeDtypeStruct((768, 128), jnp.float32),
            jax.ShapeDtypeStruct((768, 128), jnp.float32),
            jax.ShapeDtypeStruct((16, 1024), jnp.float32),
            jax.ShapeDtypeStruct((NFFT, 1024), jnp.float32),
            jax.ShapeDtypeStruct((12, 8, NFFT), jnp.float32),
            jax.ShapeDtypeStruct((8, NFFT, 128), jnp.float32),
            jax.ShapeDtypeStruct((8, 128), jnp.int32),
        ),
        in_specs=[vm, vm, vm, vm, vm, vm, hbm, hbm],
        out_specs=(hbm, vm, hbm, hbm, hbm, hbm, hbm, vm, vm, vm, vm, vm),
        scratch_shapes=[
            pltpu.VMEM((4, 4, 4, 16, WIDE), bf),
            pltpu.VMEM((8, WIDE), jnp.float32),
            pltpu.VMEM((8, WIDE), jnp.float32),
            pltpu.VMEM((2, 1, 768), jnp.int32),
            pltpu.VMEM((832, 1024), bf),
            pltpu.VMEM((832, 1024), jnp.float32),
            pltpu.VMEM((832, 1024), bf),
            pltpu.VMEM((832, 1024), bf),
            pltpu.VMEM((832, 1024), jnp.float32),
            pltpu.VMEM((832, 128), jnp.float32),
            pltpu.VMEM((832, 128), jnp.float32),
            pltpu.SemaphoreType.DMA,
            pltpu.SemaphoreType.DMA((11,)),
            pltpu.SemaphoreType.DMA((2,)),
            pltpu.SemaphoreType.DMA((3, 2)),
            pltpu.SemaphoreType.DMA((3, 2)),
            pltpu.SemaphoreType.DMA((6, 3, 4)),
            pltpu.SemaphoreType.DMA((6, 3, 4)),
            pltpu.SemaphoreType.DMA((6, 4)),
            pltpu.SemaphoreType.DMA((6, 4)),
            pltpu.SemaphoreType.DMA((6, 2)),
        ],
        compiler_params=pltpu.CompilerParams(
            collective_id=0, has_side_effects=True, vmem_limit_bytes=60 << 20),
        name="gather_weights",
    )(w_in, w_out, kern, gain, seg, spread, frames, cot)


def back_kernel(
    early, ln_hbm, dpre_hbm, w_hbm, frames, cot, inv_hbm, mean_hbm, gains, w_rows, gain,
    o_in, o_out, o_kern, o_vec, out,
    acc, sibbuf, gsend, h0, f0, f1, f2, last, low, fin,
    ln, turned, dpre, w, xe, ce, inv_in, mean_in, work,
    load_sem, d_send, d_recv, a_send, a_recv, e_sem,
):
    scale = 1.0 / math.sqrt(98304.0)
    f32, bf = jnp.float32, jnp.bfloat16
    me, core = place()
    sibling = dev(me, 1 - core)
    full4 = (slice(None),) * 4

    def cp(src, dst, n):
        c = pltpu.make_async_copy(src, dst, load_sem.at[n])
        c.start()
        return c

    def early_cols(c):
        return full4 + (pl.ds(pl.multiple_of(c * 640, 128), 640),)

    def lanes(p):
        return pl.ds(*PARTS[p])

    later = pl.ds(1024, 640)

    loads = [
        cp(ln_hbm, ln, 0),
        cp(dpre_hbm, dpre, 1),
        cp(early.at[early_cols(core)], acc.at[full4 + (later,)], 2),
        cp(w_hbm.at[:, pl.ds(0, 1024)], w.at[:, pl.ds(0, 1024)], 3),
        cp(w_hbm.at[:, pl.ds(HALFW, 1024)], w.at[:, pl.ds(1024, 1024)], 4),
        cp(frames, xe, 5),
        cp(cot, ce, 6),
        cp(inv_hbm, inv_in, 7),
        cp(mean_hbm, mean_in, 8),
    ]
    targets = [dev(moved(me, a, b), core) for a in "yxz" for b in (1, -1, 2)] + [sibling]
    greet(targets)

    def give(p):
        src = early.at[early_cols(1 - core)] if p == 3 else gsend.at[full4 + (lanes(p),)]
        return pltpu.make_async_remote_copy(
            src_ref=src, dst_ref=sibbuf.at[full4 + (later if p == 3 else lanes(p),)],
            send_sem=d_send.at[p], recv_sem=d_recv.at[p], device_id=sibling, device_id_type=MESH)

    sends = []

    def go(c):
        c.start()
        sends.append(c)

    def axis_of(p, ph):
        return ORDERS[p][2 - ph]

    def block(p, ph, by):
        axis = axis_of(p, ph)
        return block_index(me, ORDERS[p][: 2 - ph], axis, (me[axis] + by + 4) % 4)

    def send_half(p, which):
        return pltpu.make_async_remote_copy(
            src_ref=acc.at[half_of(block(p, 0, 2), which) + (slice(None), lanes(p))],
            dst_ref=h0.at[pl.ds(2 * which, 2), :, :, lanes(p)],
            send_sem=a_send.at[p, 0, which], recv_sem=a_recv.at[p, 0, which],
            device_id=dev(moved(me, axis_of(p, 0), (1, -1)[which]), core), device_id_type=MESH)

    def send_full(p, ph, which):
        by = (1, -1, 2)[which]
        dst = (f0, f1, f2)[ph].at[(which,) + (slice(None),) * (3 - ph) + (lanes(p),)]
        return pltpu.make_async_remote_copy(
            src_ref=acc.at[block(p, ph, by) + (slice(None), lanes(p))], dst_ref=dst,
            send_sem=a_send.at[p, ph, 2 + which], recv_sem=a_recv.at[p, ph, 2 + which],
            device_id=dev(moved(me, axis_of(p, ph), by), core), device_id_type=MESH)

    def over(p, ph, value, body, span=(0, 4)):
        axis, full = axis_of(p, ph), ORDERS[p][: 2 - ph]
        names = [a for a in "yxz" if a in full]

        def at(k):
            by_name = {axis: value}
            if len(names) == 2:
                by_name[names[0]] = k
                by_name[names[1]] = slice(None)
            elif len(names) == 1:
                by_name[names[0]] = slice(None)
            return tuple(by_name[a] if a in by_name else me[a] for a in "yxz")

        if len(names) == 2:
            @pl.loop(*span)
            def _(k):
                body(at(k), (k, slice(None)))
        else:
            body(at(0), (slice(None),) * len(names))

    def start_halves(p):
        for which in (0, 1):
            go(send_half(p, which))

    def pass_on(p):
        axis = axis_of(p, 0)
        for which, by in ((0, 1), (1, -1)):
            send_half(p, which).wait_recv()

            def body(at, dig):
                at = at + (slice(None), lanes(p))
                acc[at] = (acc[at].astype(f32) + h0[dig + (slice(None), lanes(p))].astype(f32)).astype(bf)
            over(p, 0, (me[axis] + by + 4) % 4, body, (2 * which, 2 * which + 2))
            go(send_full(p, 0, which))

    def take(p, ph):
        count = 2 if ph == 0 else 3
        ref = (f0, f1, f2)[ph]
        for which in range(count):
            send_full(p, ph, which).wait_recv()
        sl = lanes(p)

        def body(at, dig):
            at = at + (slice(None), sl)
            total = acc[at].astype(f32)
            for which in range(count):
                total = total + ref[(which,) + dig + (slice(None), sl)].astype(f32)
            if ph < 2:
                acc[at] = total.astype(bf)
            else:
                last[:, sl] = total
        over(p, ph, me[axis_of(p, ph)], body)
        if ph < 2:
            for which in range(3):
                go(send_full(p, ph + 1, which))

    def product(p, half, store, fresh=False):
        at, width = PARTS[p]

        @pl.loop(0, 4)
        def _(y):
            some = pl.ds(pl.multiple_of(y * 256, 256), 256)
            if fresh:
                lhs = ln[:, some].T
                turned[some, :] = lhs
            else:
                lhs = turned[some, :]
            rhs = dpre[:, pl.ds(pl.multiple_of(half * 1024 + at, 128), width)]
            r = jnp.dot(lhs, rhs, preferred_element_type=f32) * scale
            store(y, r.reshape(4, 4, 16, width))

    def for_sibling(p):
        def store(y, r):
            gsend[y, :, :, :, lanes(p)] = r.astype(bf)
        product(p, 1 - core, store, fresh=p == 0)

    def for_own(p):
        give(p).wait_recv()

        def store(y, r):
            acc[y, :, :, :, lanes(p)] = (r + sibbuf[y, :, :, :, lanes(p)].astype(f32)).astype(bf)
        product(p, core, store)
        start_halves(p)

    def input_product(j):
        col = slice(j * 256, j * 256 + 256)
        work[:, col] = lax.dot_general(dpre[...], w[col, :], (((1,), (1,)), ((), ())), preferred_element_type=f32)

    def input_rows(n):
        @pl.loop(3 * n, 3 * n + 3)
        def _(i):
            ats = [pl.ds(pl.multiple_of(i * 64 + 16 * u, 16), 16) for u in range(4)]
            gain = gains[0:1, :]
            invs = [inv_in[at, 0:1] for at in ats]
            normals = [(xe[at, :].astype(f32) - mean_in[at, 0:1]) * inv for at, inv in zip(ats, invs)]
            us = [work[at, :] * gain for at in ats]
            m1 = [row_mean(u) for u in us]
            m2 = [row_mean(u * n) for u, n in zip(us, normals)]
            for at, inv, u, n, a, b in zip(ats, invs, us, normals, m1, m2):
                out[at, :] = (ce[at, :].astype(f32) + inv * (u - a - n * b)).astype(bf)

    loads[0].wait()
    loads[1].wait()
    for_sibling(0)
    greeted(targets)
    go(give(3))
    go(give(0))
    for_sibling(1)
    go(give(1))
    loads[2].wait()
    give(3).wait_recv()

    @pl.loop(0, 4)
    def _(y):
        at = (y, slice(None), slice(None), slice(None), later)
        acc[at] = (acc[at].astype(f32) + sibbuf[at].astype(f32)).astype(bf)
    for p in SECOND:
        start_halves(p)
    for_sibling(2)
    go(give(2))
    for_own(0)
    for p in SECOND:
        pass_on(p)
    for_own(1)
    for_own(2)
    pass_on(0)
    for n in (3, 4):
        loads[n].wait()
    input_product(0)
    pass_on(1)
    pass_on(2)
    for p in SECOND:
        take(p, 0)
    input_product(1)
    take(0, 0)
    input_product(2)
    for p in SECOND:
        take(p, 1)
    take(1, 0)
    take(2, 0)
    input_product(3)
    for n in (5, 6, 7, 8):
        loads[n].wait()
    take(0, 1)
    for p in SECOND:
        take(p, 2)
    input_rows(0)
    take(1, 1)
    take(2, 1)
    input_rows(1)
    take(0, 2)
    input_rows(2)
    take(1, 2)
    take(2, 2)
    top, bottom = last[0:8, :], last[8:16, :]
    low[...] = jnp.where(core == 0, bottom, top)
    swap = pltpu.make_async_remote_copy(
        src_ref=low, dst_ref=fin, send_sem=e_sem.at[0], recv_sem=e_sem.at[1], device_id=sibling, device_id_type=MESH)
    swap.start()
    input_rows(3)
    mine = jnp.where(core == 0, top, bottom)
    swap.wait()
    theirs = fin[...]
    total = jnp.zeros((8, 1), f32)
    for c in (0, 1):
        own = jnp.where(core == c, mine, theirs)
        o_in[:, c * 1024 : c * 1024 + 1024] = own[:, :1024]
        o_out[:, c * 512 : c * 512 + 512] = own[:, 1152:1664]
        rows = w_rows[:, c * 1024 : c * 1024 + 1024].astype(f32)
        total = total + jnp.sum(rows * own[:, :1024], axis=-1, keepdims=True)
        if c == 0:
            rest = own[:, 1024:1152]
    eye = lax.broadcasted_iota(jnp.int32, (8, 8), 0) == lax.broadcasted_iota(jnp.int32, (8, 8), 1)
    column = jnp.sum(jnp.where(eye, jnp.broadcast_to(gain[0:1, :], (8, 8)), 0.0), axis=1, keepdims=True)
    o_kern[...] = rest[:, 0:31]
    pair = []
    for v in (total / column, rest[:, 32:33]):
        pair.append(jnp.sum(jnp.where(eye, jnp.broadcast_to(v, (8, 8)), 0.0), axis=0, keepdims=True))
    o_vec[...] = jnp.concatenate(pair, axis=0)
    for c in sends:
        c.wait_send()


def back(early, ln, dpre, w, frames, cot, inv, mean, gains, w_rows, gain):
    bf, f32 = jnp.bfloat16, jnp.float32
    vm = pl.BlockSpec(memory_space=pltpu.VMEM)
    hbm = pl.BlockSpec(memory_space=pltpu.HBM)
    V = pltpu.VMEM
    return pl.pallas_call(
        back_kernel,
        out_shape=(
            jax.ShapeDtypeStruct((8, 2048), f32),
            jax.ShapeDtypeStruct((8, 1024), f32),
            jax.ShapeDtypeStruct((8, 31), f32),
            jax.ShapeDtypeStruct((2, 8), f32),
            jax.ShapeDtypeStruct((768, 1024), bf),
        ),
        in_specs=[hbm] * 8 + [vm] * 3,
        out_specs=(vm, vm, vm, vm, vm),
        scratch_shapes=[
            V((4, 4, 4, 16, HALFW), bf),
            V((4, 4, 4, 16, HALFW), bf),
            V((4, 4, 4, 16, 1024), bf),
            V((4, 4, 16, HALFW), bf),
            V((2, 4, 4, 16, HALFW), bf),
            V((3, 4, 16, HALFW), bf),
            V((3, 16, HALFW), bf),
            V((16, HALFW), f32),
            V((8, HALFW), f32),
            V((8, HALFW), f32),
            V((768, 1024), bf),
            V((1024, 768), bf),
            V((768, 2048), bf),
            V((1024, 2048), bf),
            V((768, 1024), bf),
            V((768, 1024), bf),
            V((768, 128), f32),
            V((768, 128), f32),
            V((768, 1024), f32),
            pltpu.SemaphoreType.DMA((10,)),
            pltpu.SemaphoreType.DMA((4,)),
            pltpu.SemaphoreType.DMA((4,)),
            pltpu.SemaphoreType.DMA((6, 3, 5)),
            pltpu.SemaphoreType.DMA((6, 3, 5)),
            pltpu.SemaphoreType.DMA((2,)),
        ],
        compiler_params=pltpu.CompilerParams(
            collective_id=1, has_side_effects=True, vmem_limit_bytes=60 << 20),
        name="back_and_scatter",
    )(early, ln, dpre, w, frames, cot, inv, mean, gains, w_rows, gain)


EPS = 1e-05
HALF = 15
ROWS = 768
D = 1024
NFFT = 256


def tables():
    omega = 2 * np.pi * (np.arange(128) + 0.5) / NFFT
    phase = omega[:, None] * np.arange(NFFT)[None]
    basis = np.concatenate([np.cos(phase), -np.sin(phase)], axis=0)
    lag = omega[:, None] * (np.arange(31) - HALF)[None]
    spread = np.zeros((NFFT, 128))
    spread[:, :31] = np.concatenate([np.cos(lag), np.sin(lag)], axis=0) * (2 / NFFT)
    back = np.zeros((128, NFFT))
    back[:31] = np.concatenate([np.cos(lag), -np.sin(lag)], axis=0).T * (2 / NFFT)
    f32 = jnp.float32
    return (jnp.asarray(basis, f32), jnp.asarray(basis.T, f32), jnp.asarray(spread, f32), jnp.asarray(back, f32))


def sigmoid(v):
    return 0.5 * jnp.tanh(0.5 * v) + 0.5


NT = (((1,), (1,)), ((), ()))
TN = (((0,), (0,)), ((), ()))
F32 = jnp.float32
BF = jnp.bfloat16


def nt(a, b):
    return lax.dot_general(a, b, NT, preferred_element_type=F32)


def mm(a, b):
    return jnp.dot(a, b, preferred_element_type=F32)


def row_mean(v):
    return jnp.sum(v, axis=-1, keepdims=True) * (1.0 / D)


FWD_AT, BWD_AT = (0, 208, 416, 592), (16, 208, 400, 592)


def colours(ids, table, across, counts):
    lane = lax.broadcasted_iota(jnp.int32, (1, 128), 1)
    wide = lax.broadcasted_iota(jnp.int32, (1, NFFT), 1)
    for n, at in enumerate(FWD_AT + BWD_AT):
        length = 240 if n < 4 else 224
        r, o = divmod(at + 96, 128)

        def piece(k, o=o):
            if o == 0:
                return ids[k : k + 1, :]
            first = pltpu.roll(ids[k : k + 1, :], 128 - o, 1)
            return jnp.where(lane < 128 - o, first, pltpu.roll(ids[min(k + 1, 7) : min(k + 1, 7) + 1, :], 128 - o, 1))

        own = jnp.concatenate([piece(r), piece(r + 1)], axis=1)
        step = jnp.where(wide < length - HALF, pltpu.roll(own, NFFT - HALF, 1) - own, 0.0)
        count = jnp.max(step, axis=1, keepdims=True) + 1.0
        own = own + 1.0
        own = own - count * jnp.floor((own + 0.5) / count)
        own = jnp.where(wide < length, own, -1.0)
        rows = jnp.broadcast_to(own, (8, NFFT))
        table[n] = rows
        across[n] = jnp.broadcast_to(rows.T[:, 0:1], (NFFT, 128))
        if n >= 4:
            table[n + 4] = jnp.where((wide >= 16) & (wide < 208), rows, -1.0)
        counts[n : n + 1, :] = jnp.broadcast_to(count, (1, 128)).astype(jnp.int32)


def mid_kernel(
    counts, gains, basis, turned, back, frames, cot, hc, w_hbm, glu_hbm, sig_hbm, spec_hbm, table_hbm, across_hbm,
    out_hbm, dpre_hbm, early_hbm,
    xe, ce, w, glu, sig, mixed, work, act, dm, dpre, g, spec, prod, extra, table, across, out, sems,
):
    scale = 1.0 / math.sqrt(98304.0)

    def cp(src, dst, n):
        c = pltpu.make_async_copy(src, dst, sems.at[n])
        c.start()
        return c

    cols = lambda lo, n: (slice(None), pl.ds(lo, n))
    loads = [
        cp(table_hbm, table, 0),
        cp(across_hbm, across, 1),
        cp(spec_hbm, spec, 2),
        cp(glu_hbm, glu.at[pl.ds(0, 832)], 3),
        cp(cot, ce.at[pl.ds(16, ROWS)], 4),
        cp(hc.at[pl.ds(0, 16)], ce.at[pl.ds(0, 16)], 5),
        cp(hc.at[pl.ds(16, 16)], ce.at[pl.ds(784, 16)], 6),
        cp(w_hbm.at[cols(1152, 512)], w.at[cols(0, 512)], 7),
        cp(w_hbm.at[cols(2816, 512)], w.at[cols(512, 512)], 8),
        cp(frames, xe, 9),
        cp(sig_hbm, sig, 10),
    ]
    glu[pl.ds(832, 16), :] = jnp.zeros((16, D), BF)
    dm[pl.ds(800, 32), :] = jnp.zeros((32, D), BF)
    prod[...] = jnp.zeros((NFFT, D), F32)
    extra[...] = jnp.zeros((128, D), F32)
    stores = []
    for n in range(4):
        loads[n].wait()

    def strips(i, n, off=0):
        return [pl.ds(pl.multiple_of(i * (16 * n) + off + 16 * u, 16), 16) for u in range(n)]

    def picked(row, first, k):
        return jnp.concatenate(
            [jnp.where(table[row, 0:1, :] == (first + c).astype(F32), basis[...], 0.0) for c in range(k)],
            axis=0).astype(BF)

    def placed(row, first, k, lo, hi):
        own = across[row, lo:hi, :]
        own = jnp.concatenate([own, own], axis=1)
        return jnp.concatenate(
            [jnp.where(own == (first + c).astype(F32), turned[lo:hi, :], 0.0) for c in range(k)], axis=1).astype(BF)

    def staged(spectrum, filtered, put):
        x = [spectrum(0)]
        y = None
        for j in range(4):
            if j < 3:
                x.append(spectrum(j + 1))
            new = filtered(j, x[j])
            if y is not None:
                put(j - 1, y)
            y = new
        put(3, y)

    def forward(wi, first, k, add):
        base = pl.multiple_of(jnp.minimum(wi * 208, 592), 16)
        to = picked(wi, first, k)
        fro = placed(wi, first, k, 16, 224)

        def spectrum(j):
            return mm(to, glu[pl.ds(base, 256), j * 256 : j * 256 + 256])

        def filtered(j, x):
            col = slice(j * 256, j * 256 + 256)
            hr, hi = spec[:128, col], spec[128:, col]
            ys = []
            for c in range(k):
                xr, xi = x[256 * c : 256 * c + 128], x[256 * c + 128 : 256 * c + 256]
                ys += [(xr * hr - xi * hi).astype(BF), (xr * hi + xi * hr).astype(BF)]
            return jnp.concatenate(ys, axis=0)

        def put(j, y):
            col = slice(j * 256, j * 256 + 256)
            y = mm(fro, y)
            if add:
                mixed[pl.ds(base, 208), col] += y
            else:
                mixed[pl.ds(base, 208), col] = y

        staged(spectrum, filtered, put)

    def backward(wi, first, k, add):
        base = pl.multiple_of(wi * 192, 16)
        to = picked(4 + wi, first, k)
        mid_to = picked(8 + wi, first, k)
        fro = placed(4 + wi, first, k, 16, 208)

        def spectrum(j):
            col = slice(j * 256, j * 256 + 256)
            return mm(to, dm[pl.ds(base, 256), col]), mm(mid_to, glu[pl.ds(base + 16, 256), col])

        def filtered(j, pair):
            d, q = pair
            col = slice(j * 256, j * 256 + 256)
            hr, hi = spec[:128, col], spec[128:, col]
            ys = []
            pr, pi = prod[:128, col], prod[128:, col]
            for c in range(k):
                lo, mi, up = 256 * c, 256 * c + 128, 256 * c + 256
                dr, di, qr, qi = d[lo:mi], d[mi:up], q[lo:mi], q[mi:up]
                ys += [(dr * hr + di * hi).astype(BF), (di * hr - dr * hi).astype(BF)]
                pr = pr + (qr * dr + qi * di)
                pi = pi + (qi * dr - qr * di)
            prod[:128, col] = pr
            prod[128:, col] = pi
            return jnp.concatenate(ys, axis=0)

        def put(j, y):
            col = slice(j * 256, j * 256 + 256)
            y = mm(fro, y)
            if add:
                mixed[pl.ds(base, 192), col] += y
            else:
                mixed[pl.ds(base, 192), col] = y

        staged(spectrum, filtered, put)

    def by_class(run, wi, count):
        zero = jnp.int32(0)

        @pl.when(count <= 2)
        def _():
            run(wi, zero, 2, False)

        @pl.when(count == 3)
        def _():
            run(wi, zero, 3, False)

        @pl.when(count > 3)
        def _():
            run(wi, zero, 4, False)

            @pl.loop(0, (count - 3) // 2)
            def _(n):
                run(wi, 4 + n * 2, 2, True)

    @pl.loop(0, 4)
    def _(wi):
        by_class(forward, wi, counts[wi, 0])

    for n in range(4, 11):
        loads[n].wait()

    @pl.loop(0, 4)
    def _(j):
        col = pl.ds(pl.multiple_of(j * 256, 256), 256)
        work[:, col] = nt(ce[...], w[col, :])

    def mid_rows(ats, central):
        gain = gains[8:9, :]
        cens = [mixed[at, :] for at in ats]
        cens = [m - row_mean(m) for m in cens]
        invs = [lax.rsqrt(row_mean(c * c) + EPS) for c in cens]
        normals = [c * inv for c, inv in zip(cens, invs)]
        us = []
        for at, normal in zip(ats, normals):
            y = normal * gain
            s = sigmoid(y)
            ys = y * s
            act[at, :] = ys.astype(BF)
            d_ln = work[at, :] * (s + ys * (1.0 - s))
            if central:
                dn = d_ln * normal
                extra[40:48, :] += dn[:8] + dn[8:]
            us.append(d_ln * gain)
        m1 = [row_mean(u) for u in us]
        m2 = [row_mean(u * n) for u, n in zip(us, normals)]
        for at, inv, u, n, a, b in zip(ats, invs, us, normals, m1, m2):
            dm[at, :] = (inv * (u - a - n * b)).astype(BF)

    mid_rows([pl.ds(0, 16), pl.ds(784, 16)], False)

    @pl.loop(0, 12)
    def _(i):
        mid_rows(strips(i, 4, 16), True)

    @pl.loop(0, 4)
    def _(j):
        col = pl.ds(pl.multiple_of(j * 256, 256), 256)
        y = mm(act[16:784, :], w[:, col])
        out[:, col] = (xe[:, col].astype(F32) + y).astype(BF)
        lhs = act[16:784, col].T
        r = (mm(lhs, ce[16:784, :]) * scale).astype(BF)
        g[col, 128:640] = r[:, :512]
        g[col, 768:1280] = r[:, 512:]

    stores.append(cp(out, out_hbm, 11))

    @pl.loop(0, 4)
    def _(wi):
        by_class(backward, wi, counts[4 + wi, 0])

    gk = jnp.dot(back[...], prod[...], precision=lax.Precision.HIGHEST, preferred_element_type=F32)
    extra[0:31, :] = gk[0:31]
    g_mid = jnp.sum(extra[40:48, :], axis=0, keepdims=True)
    extra[32:33, :] = g_mid
    g[:, 0:128] = (extra[...].T * scale).astype(BF)
    g[:, 640:768] = jnp.zeros((D, 128), BF)
    stores.append(cp(g, early_hbm, 12))

    for q in range(4):
        @pl.loop(q * 6, q * 6 + 6)
        def _(i):
            for u in range(2):
                at = pl.ds(pl.multiple_of(i * 32 + 16 * u, 16), 16)
                ext = pl.ds(pl.multiple_of(i * 32 + 16 * u + 32, 16), 16)
                d = mixed[at, :]
                s = sig[at, :]
                dpre[at, :1024] = (d * s).astype(BF)
                dpre[at, 1024:] = (d * glu[ext, :].astype(F32) * (1.0 - s)).astype(BF)

        part = pl.ds(q * 192, 192)
        stores.append(cp(dpre.at[part], dpre_hbm.at[part], 13 + q))
    for s in stores:
        s.wait()


def mid(counts, gains, consts, *rest):
    vm = pl.BlockSpec(memory_space=pltpu.VMEM)
    hbm = pl.BlockSpec(memory_space=pltpu.HBM)
    V = pltpu.VMEM
    return pl.pallas_call(
        mid_kernel,
        out_shape=(
            jax.ShapeDtypeStruct((ROWS, D), BF),
            jax.ShapeDtypeStruct((ROWS, 2 * D), BF),
            jax.ShapeDtypeStruct((D, 1280), BF),
        ),
        in_specs=[pl.BlockSpec(memory_space=pltpu.SMEM), vm, vm, vm, vm] + [hbm] * 9,
        out_specs=(hbm,) * 3,
        scratch_shapes=[
            V((768, D), BF), V((800, D), BF), V((D, D), BF),
            V((848, D), BF), V((768, D), F32),
            V((800, D), F32), V((800, D), F32), V((800, D), BF), V((832, D), BF),
            V((768, 2 * D), BF), V((D, 1280), BF), V((NFFT, D), F32), V((NFFT, D), F32),
            V((128, D), F32), V((12, 8, NFFT), F32), V((8, NFFT, 128), F32), V((ROWS, D), BF),
            pltpu.SemaphoreType.DMA((17,)),
        ],
        compiler_params=pltpu.CompilerParams(vmem_limit_bytes=60 << 20),
        name="block_pass",
    )(counts, gains, *consts, *rest)


def shards(frames, cotangent, segments, w_in, w_out, kernel, gain_in, gain_mid):
    gain = jnp.stack([gain_in, gain_mid]).astype(F32)
    x, cot = frames[0], cotangent[0]
    basis, turned, spread, back_table = tables()
    full, c_halo, ln, glu, sig, inv, mean, gains, spec, table, across, counts = gather(
        w_in, w_out, kernel, gain, segments, spread, x, cot)
    full = full.reshape(D, WIDE)
    block_out, dpre, early = mid(
        counts, gains, (basis, turned, back_table), x, cot, c_halo, full, glu, sig, spec, table, across)
    g_in, g_out, g_kern, g_vec, input_grad = back(
        early.reshape(4, 4, 4, 16, 1280), ln, dpre, full, x, cot, inv, mean, gains, w_in, gain)
    return (block_out[None], input_grad[None], g_in, g_out, g_kern, g_vec[0], g_vec[1])


def solution(mesh):
    rows = P("dp", "seq", None)
    mat = P(("dp", "seq"), None)
    vec = P(("dp", "seq"))
    return jax.shard_map(
        shards, mesh=mesh, in_specs=(rows, rows, P("dp", "seq"), mat, mat, mat, vec, vec),
        out_specs=(rows, rows, mat, mat, mat, vec, vec), check_vma=False)
```

```python
import math

import jax
import jax.numpy as jnp
import numpy as np
from jax import lax
from jax.experimental import pallas as pl
from jax.experimental.pallas import tpu as pltpu
from jax.sharding import PartitionSpec as P

MESH = pl.DeviceIdType.MESH
HALFW = 1664
WIDE = 2 * HALFW
OUT_PARTS = ((0, 384), (384, 384), (768, 384), (1152, 128), (1280, 128), (1408, 256))
PARTS = ((0, 384), (384, 384), (768, 256), (1024, 128), (1152, 256), (1408, 256))
FIRST, SECOND = (0, 1, 2), (3, 4, 5)
ORDERS = (("z", "x", "y"), ("x", "y", "z"), ("y", "z", "x")) * 2
HALO = 32


def place():
    d, s = lax.axis_index("dp"), lax.axis_index("seq")
    return {"y": d // 4, "x": d % 4, "z": s // 2}, s % 2


def dev(coords, core):
    return (coords["y"] * 4 + coords["x"], coords["z"] * 2 + core)


def moved(coords, axis, by):
    out = dict(coords)
    out[axis] = (coords[axis] + by + 4) % 4
    return out


def greet(targets):
    for t in targets:
        pl.semaphore_signal(pltpu.get_barrier_semaphore(), inc=1, device_id=t, device_id_type=MESH)


def greeted(targets):
    pl.semaphore_wait(pltpu.get_barrier_semaphore(), len(targets))


def half_of(index, which):
    at = [isinstance(i, slice) for i in index].index(True)
    return index[:at] + (pl.ds(2 * which, 2),) + index[at + 1 :]


def block_index(coords, full, axis, value):
    out = []
    for a in ("y", "x", "z"):
        if a == axis:
            out.append(value)
        elif a in full:
            out.append(slice(None))
        else:
            out.append(coords[a])
    return tuple(out)


def gather_kernel(
    w_in_ref, w_out_ref, kern_ref, gain_ref, seg_ref, spread, frames_ref, cot_ref,
    out_ref, hc_ref, ln_hbm, glu_hbm, sig_hbm, inv_hbm, mean_hbm, gains, spec, table, across, counts,
    buf, shard, sib, segs, xe, hat, ln, glu, sig, inv_in, mean_in, load_sem, store_sem, sib_sem, halo_send, halo_recv, a_send, a_recv, s_send, s_recv, out_sem,
):
    me, core = place()
    f32, bf = jnp.float32, jnp.bfloat16
    sibling = dev(me, 1 - core)
    seq = lax.axis_index("seq")
    right = (lax.axis_index("dp"), (seq + 1) % 8)
    left = (lax.axis_index("dp"), (seq + 7) % 8)
    cross = dev(moved(me, "z", 2 * core - 1), 1 - core)
    targets = [dev(moved(me, a, b), core) for a in "yxz" for b in (1, -1, 2)] + [sibling, cross]
    greet(targets)
    rows = frames_ref.shape[0]
    load = pltpu.make_async_copy(frames_ref, xe.at[pl.ds(HALO, rows)], load_sem)
    load.start()
    for c in (0, 1):
        at = c * HALFW
        shard[:, at : at + 1024] = w_in_ref[:, c * 1024 : c * 1024 + 1024].astype(f32)
        shard[:, at + 1024 : at + 1152] = jnp.zeros((8, 128), f32)
        shard[:, at + 1152 : at + HALFW] = w_out_ref[:, c * 512 : c * 512 + 512].astype(f32)
    shard[:, 1024 : 1024 + 31] = kern_ref[...].astype(f32)
    eye = lax.broadcasted_iota(jnp.int32, (8, 8), 0) == lax.broadcasted_iota(jnp.int32, (8, 8), 1)
    for n in (0, 1):
        row = jnp.broadcast_to(gain_ref[n : n + 1, :], (8, 8))
        shard[:, 1055 + n : 1056 + n] = jnp.sum(jnp.where(eye, row, 0.0), axis=1, keepdims=True)
    greeted(targets)

    first = pltpu.make_async_remote_copy(
        src_ref=shard, dst_ref=sib, send_sem=sib_sem.at[0], recv_sem=sib_sem.at[1],
        device_id=sibling, device_id_type=MESH)
    first.start()
    halos = []
    for n, (src, dst, h, end) in enumerate(((frames_ref, xe, HALO, HALO + rows), (cot_ref, hc_ref, 16, 16))):
        for m, (at, to, who) in enumerate(((rows - h, 0, right), (0, end, left))):
            halos.append(pltpu.make_async_remote_copy(
                src_ref=src.at[pl.ds(at, h)], dst_ref=dst.at[pl.ds(to, h)],
                send_sem=halo_send.at[n, m], recv_sem=halo_recv.at[n, m],
                device_id=who, device_id_type=MESH))
    for m, who in enumerate((right, left)):
        halos.append(pltpu.make_async_remote_copy(
            src_ref=seg_ref, dst_ref=segs.at[m], send_sem=halo_send.at[2, m], recv_sem=halo_recv.at[2, m],
            device_id=who, device_id_type=MESH))
    first.wait()
    mine, other = shard[...], sib[...]
    low = jnp.where(core == 0, mine[:, :HALFW], other[:, HALFW:])
    high = jnp.where(core == 0, other[:, :HALFW], mine[:, HALFW:])
    buf[me["y"], me["x"], me["z"], :, pl.ds(pl.multiple_of(core * HALFW, 128), HALFW)] = jnp.concatenate(
        [low, high], axis=0).astype(bf)

    def cols(p, c=core):
        return pl.ds(pl.multiple_of(c * HALFW + OUT_PARTS[p][0], 128), OUT_PARTS[p][1])

    def send(p, ph, which, idx, by):
        axis = ORDERS[p][ph]
        ref = buf.at[idx + (slice(None), cols(p))]
        return pltpu.make_async_remote_copy(
            src_ref=ref, dst_ref=ref, send_sem=a_send.at[p, ph, which], recv_sem=a_recv.at[p, ph, which],
            device_id=dev(moved(me, axis, by), core), device_id_type=MESH)

    def to_sibling(p, which, idx, c=core):
        ref = buf.at[idx + (slice(None), cols(p, c))]
        return pltpu.make_async_remote_copy(
            src_ref=ref, dst_ref=ref, send_sem=s_send.at[p, which], recv_sem=s_recv.at[p, which],
            device_id=sibling, device_id_type=MESH)

    def block(p, ph, by):
        axis = ORDERS[p][ph]
        return block_index(me, ORDERS[p][:ph], axis, (me[axis] + by + 4) % 4)

    sends, outs = [], []

    def go(cp):
        cp.start()
        sends.append(cp)

    def start(p, ph):
        if ph > 0:
            for which, by in ((0, -1), (1, 1), (2, 2)):
                send(p, ph - 1, which, block(p, ph - 1, by), by).wait_recv()
        own = block(p, ph, 0)
        for which, by in ((0, 1), (1, -1), (2, 2))[: 3 if ph < 2 else 2]:
            go(send(p, ph, which, own, by))
        if ph == 2:
            go(to_sibling(p, 0, own))

    def pass_on(p):
        for which, by in ((0, -1), (1, 1)):
            idx = block(p, 2, by)
            send(p, 2, which, idx, -by).wait_recv()
            go(send(p, 2, which + 2, half_of(idx, which), -by))
            go(to_sibling(p, 1 + which, idx))

    def flush(p, c, n):
        at = (slice(None),) * 4 + (cols(p, c),)
        cp = pltpu.make_async_copy(buf.at[at], out_ref.at[at], out_sem.at[p, n])
        cp.start()
        outs.append(cp)

    def finish(p):
        idx = block(p, 2, 2)
        for which in (0, 1):
            send(p, 2, 2 + which, half_of(idx, which), 1).wait_recv()
        go(to_sibling(p, 3, idx))
        flush(p, core, 0)

    def from_sibling(p):
        for which, by in ((0, 0), (1, -1), (2, 1), (3, 2)):
            to_sibling(p, which, block(p, 2, by), 1 - core).wait_recv()
        flush(p, 1 - core, 1)

    def strips(i, n):
        return [pl.ds(pl.multiple_of(i * (16 * n) + 16 * u, 16), 16) for u in range(n)]

    def normalise(lo, hi):
        @pl.loop(lo, hi)
        def _(i):
            ats = strips(i, 4)
            xs = [xe[at, :].astype(f32) for at in ats]
            means = [row_mean(x) for x in xs]
            cens = [x - m for x, m in zip(xs, means)]
            invs = [lax.rsqrt(row_mean(c * c) + EPS) for c in cens]
            for at, c, inv, m in zip(ats, cens, invs, means):
                hat[at, :] = c * inv
                inv_in[at, :] = jnp.broadcast_to(inv, (16, 128))
                mean_in[at, :] = jnp.broadcast_to(m, (16, 128))

    def keep(src, dst, n):
        cp = pltpu.make_async_copy(src, dst, store_sem.at[n])
        cp.start()
        outs.append(cp)

    for p in FIRST + SECOND:
        start(p, 0)
    for cp in halos:
        cp.start()
    load.wait()
    normalise(1, 4)
    for p in FIRST + SECOND:
        start(p, 1)
    normalise(4, 12)
    for p in FIRST:
        start(p, 2)
    for cp in halos:
        cp.wait()
    for n in (0, 12):
        normalise(n, n + 1)
    inner = pl.ds(HALO, rows)
    keep(inv_in.at[inner], inv_hbm, 0)
    keep(mean_in.at[inner], mean_hbm, 1)
    own = seg_ref[...]
    before = jnp.where(seq == 0, jnp.broadcast_to(own[:, 0:1] - 1, (1, 128)), segs[0, :, 640:768])
    after = jnp.where(seq == 7, jnp.broadcast_to(own[:, 767:768] + 1, (1, 128)), segs[1, :, 0:128])
    ids = jnp.concatenate(
        [before] + [own[:, n * 128 : n * 128 + 128] for n in range(6)] + [after], axis=0).astype(f32)
    colours(ids, table, across, counts)
    for p in FIRST:
        pass_on(p)
    for p in SECOND:
        start(p, 2)
    for p in FIRST:
        finish(p)
    for p in FIRST:
        from_sibling(p)
    taps = buf[:, :, :, :, 1024:1152].reshape(1024, 128).astype(f32).T
    gains[0:8, :] = jnp.broadcast_to(taps[31:32, :], (8, 1024))
    gains[8:16, :] = jnp.broadcast_to(taps[32:33, :], (8, 1024))

    @pl.loop(0, 13)
    def _(i):
        for at in strips(i, 4):
            ln[at, :] = (hat[at, :] * gains[0:1, :]).astype(bf)
    keep(ln.at[inner], ln_hbm, 2)

    def project(j):
        col = slice(j * 256, j * 256 + 256)
        w0 = buf[:, :, :, :, j * 256 : j * 256 + 256].reshape(1024, 256)
        w1 = buf[:, :, :, :, HALFW + j * 256 : HALFW + j * 256 + 256].reshape(1024, 256)

        pairs = []
        for r in (0, 1):
            lhs = ln[r * 416 : r * 416 + 416, :]
            pairs.append((mm(lhs, w0), mm(lhs, w1)))
        for r, (value, gate) in enumerate(pairs):
            at = slice(r * 416, r * 416 + 416)
            s = sigmoid(gate)
            glu[at, col] = (value * s).astype(bf)
            sig[at, col] = s
        keep(glu.at[:, col], glu_hbm.at[:, col], 3 + 2 * j)
        keep(sig.at[inner, col], sig_hbm.at[:, col], 4 + 2 * j)

    for p in SECOND:
        pass_on(p)
    project(0)
    project(1)
    for p in SECOND:
        finish(p)
    project(2)
    spec[...] = jnp.dot(spread[...], taps, precision=lax.Precision.HIGHEST, preferred_element_type=f32)
    for p in SECOND:
        from_sibling(p)
    project(3)
    for cp in sends:
        cp.wait_send()
    for cp in outs:
        cp.wait()


def gather(w_in, w_out, kern, gain, seg, spread, frames, cot):
    bf = jnp.bfloat16
    vm = pl.BlockSpec(memory_space=pltpu.VMEM)
    hbm = pl.BlockSpec(memory_space=pltpu.HBM)
    return pl.pallas_call(
        gather_kernel,
        out_shape=(
            jax.ShapeDtypeStruct((4, 4, 4, 16, WIDE), bf),
            jax.ShapeDtypeStruct((32, 1024), bf),
            jax.ShapeDtypeStruct((768, 1024), bf),
            jax.ShapeDtypeStruct((832, 1024), bf),
            jax.ShapeDtypeStruct((768, 1024), jnp.float32),
            jax.ShapeDtypeStruct((768, 128), jnp.float32),
            jax.ShapeDtypeStruct((768, 128), jnp.float32),
            jax.ShapeDtypeStruct((16, 1024), jnp.float32),
            jax.ShapeDtypeStruct((NFFT, 1024), jnp.float32),
            jax.ShapeDtypeStruct((12, 8, NFFT), jnp.float32),
            jax.ShapeDtypeStruct((8, NFFT, 128), jnp.float32),
            jax.ShapeDtypeStruct((8, 128), jnp.int32),
        ),
        in_specs=[vm, vm, vm, vm, vm, vm, hbm, hbm],
        out_specs=(hbm, vm, hbm, hbm, hbm, hbm, hbm, vm, vm, vm, vm, vm),
        scratch_shapes=[
            pltpu.VMEM((4, 4, 4, 16, WIDE), bf),
            pltpu.VMEM((8, WIDE), jnp.float32),
            pltpu.VMEM((8, WIDE), jnp.float32),
            pltpu.VMEM((2, 1, 768), jnp.int32),
            pltpu.VMEM((832, 1024), bf),
            pltpu.VMEM((832, 1024), jnp.float32),
            pltpu.VMEM((832, 1024), bf),
            pltpu.VMEM((832, 1024), bf),
            pltpu.VMEM((832, 1024), jnp.float32),
            pltpu.VMEM((832, 128), jnp.float32),
            pltpu.VMEM((832, 128), jnp.float32),
            pltpu.SemaphoreType.DMA,
            pltpu.SemaphoreType.DMA((11,)),
            pltpu.SemaphoreType.DMA((2,)),
            pltpu.SemaphoreType.DMA((3, 2)),
            pltpu.SemaphoreType.DMA((3, 2)),
            pltpu.SemaphoreType.DMA((6, 3, 4)),
            pltpu.SemaphoreType.DMA((6, 3, 4)),
            pltpu.SemaphoreType.DMA((6, 4)),
            pltpu.SemaphoreType.DMA((6, 4)),
            pltpu.SemaphoreType.DMA((6, 2)),
        ],
        compiler_params=pltpu.CompilerParams(
            collective_id=0, has_side_effects=True, vmem_limit_bytes=60 << 20),
        name="gather_weights",
    )(w_in, w_out, kern, gain, seg, spread, frames, cot)


def back_kernel(
    early, ln_hbm, dpre_hbm, w_hbm, frames, cot, inv_hbm, mean_hbm, gains, w_rows, gain,
    o_in, o_out, o_kern, o_vec, out,
    acc, sibbuf, gsend, h0, f0, f1, f2, last, low, fin,
    ln, turned, dpre, w, xe, ce, inv_in, mean_in, work,
    load_sem, d_send, d_recv, a_send, a_recv, e_sem,
):
    scale = 1.0 / math.sqrt(98304.0)
    f32, bf = jnp.float32, jnp.bfloat16
    me, core = place()
    sibling = dev(me, 1 - core)
    full4 = (slice(None),) * 4

    def cp(src, dst, n):
        c = pltpu.make_async_copy(src, dst, load_sem.at[n])
        c.start()
        return c

    def early_cols(c):
        return full4 + (pl.ds(pl.multiple_of(c * 640, 128), 640),)

    def lanes(p):
        return pl.ds(*PARTS[p])

    later = pl.ds(1024, 640)

    loads = [
        cp(ln_hbm, ln, 0),
        cp(dpre_hbm, dpre, 1),
        cp(early.at[early_cols(core)], acc.at[full4 + (later,)], 2),
        cp(w_hbm.at[:, pl.ds(0, 1024)], w.at[:, pl.ds(0, 1024)], 3),
        cp(w_hbm.at[:, pl.ds(HALFW, 1024)], w.at[:, pl.ds(1024, 1024)], 4),
        cp(frames, xe, 5),
        cp(cot, ce, 6),
        cp(inv_hbm, inv_in, 7),
        cp(mean_hbm, mean_in, 8),
    ]
    targets = [dev(moved(me, a, b), core) for a in "yxz" for b in (1, -1, 2)] + [sibling]
    greet(targets)

    def give(p):
        src = early.at[early_cols(1 - core)] if p == 3 else gsend.at[full4 + (lanes(p),)]
        return pltpu.make_async_remote_copy(
            src_ref=src, dst_ref=sibbuf.at[full4 + (later if p == 3 else lanes(p),)],
            send_sem=d_send.at[p], recv_sem=d_recv.at[p], device_id=sibling, device_id_type=MESH)

    sends = []

    def go(c):
        c.start()
        sends.append(c)

    def axis_of(p, ph):
        return ORDERS[p][2 - ph]

    def block(p, ph, by):
        axis = axis_of(p, ph)
        return block_index(me, ORDERS[p][: 2 - ph], axis, (me[axis] + by + 4) % 4)

    def send_half(p, which):
        return pltpu.make_async_remote_copy(
            src_ref=acc.at[half_of(block(p, 0, 2), which) + (slice(None), lanes(p))],
            dst_ref=h0.at[pl.ds(2 * which, 2), :, :, lanes(p)],
            send_sem=a_send.at[p, 0, which], recv_sem=a_recv.at[p, 0, which],
            device_id=dev(moved(me, axis_of(p, 0), (1, -1)[which]), core), device_id_type=MESH)

    def send_full(p, ph, which):
        by = (1, -1, 2)[which]
        dst = (f0, f1, f2)[ph].at[(which,) + (slice(None),) * (3 - ph) + (lanes(p),)]
        return pltpu.make_async_remote_copy(
            src_ref=acc.at[block(p, ph, by) + (slice(None), lanes(p))], dst_ref=dst,
            send_sem=a_send.at[p, ph, 2 + which], recv_sem=a_recv.at[p, ph, 2 + which],
            device_id=dev(moved(me, axis_of(p, ph), by), core), device_id_type=MESH)

    def over(p, ph, value, body, span=(0, 4)):
        axis, full = axis_of(p, ph), ORDERS[p][: 2 - ph]
        names = [a for a in "yxz" if a in full]

        def at(k):
            by_name = {axis: value}
            if len(names) == 2:
                by_name[names[0]] = k
                by_name[names[1]] = slice(None)
            elif len(names) == 1:
                by_name[names[0]] = slice(None)
            return tuple(by_name[a] if a in by_name else me[a] for a in "yxz")

        if len(names) == 2:
            @pl.loop(*span)
            def _(k):
                body(at(k), (k, slice(None)))
        else:
            body(at(0), (slice(None),) * len(names))

    def start_halves(p):
        for which in (0, 1):
            go(send_half(p, which))

    def pass_on(p):
        axis = axis_of(p, 0)
        for which, by in ((0, 1), (1, -1)):
            send_half(p, which).wait_recv()

            def body(at, dig):
                at = at + (slice(None), lanes(p))
                acc[at] = (acc[at].astype(f32) + h0[dig + (slice(None), lanes(p))].astype(f32)).astype(bf)
            over(p, 0, (me[axis] + by + 4) % 4, body, (2 * which, 2 * which + 2))
            go(send_full(p, 0, which))

    def take(p, ph):
        count = 2 if ph == 0 else 3
        ref = (f0, f1, f2)[ph]
        for which in range(count):
            send_full(p, ph, which).wait_recv()
        sl = lanes(p)

        def body(at, dig):
            at = at + (slice(None), sl)
            total = acc[at].astype(f32)
            for which in range(count):
                total = total + ref[(which,) + dig + (slice(None), sl)].astype(f32)
            if ph < 2:
                acc[at] = total.astype(bf)
            else:
                last[:, sl] = total
        over(p, ph, me[axis_of(p, ph)], body)
        if ph < 2:
            for which in range(3):
                go(send_full(p, ph + 1, which))

    def product(p, half, store, fresh=False):
        at, width = PARTS[p]

        @pl.loop(0, 4)
        def _(y):
            some = pl.ds(pl.multiple_of(y * 256, 256), 256)
            if fresh:
                lhs = ln[:, some].T
                turned[some, :] = lhs
            else:
                lhs = turned[some, :]
            rhs = dpre[:, pl.ds(pl.multiple_of(half * 1024 + at, 128), width)]
            r = jnp.dot(lhs, rhs, preferred_element_type=f32) * scale
            store(y, r.reshape(4, 4, 16, width))

    def for_sibling(p):
        def store(y, r):
            gsend[y, :, :, :, lanes(p)] = r.astype(bf)
        product(p, 1 - core, store, fresh=p == 0)

    def for_own(p):
        give(p).wait_recv()

        def store(y, r):
            acc[y, :, :, :, lanes(p)] = (r + sibbuf[y, :, :, :, lanes(p)].astype(f32)).astype(bf)
        product(p, core, store)
        start_halves(p)

    def input_product(j):
        col = slice(j * 256, j * 256 + 256)
        work[:, col] = lax.dot_general(dpre[...], w[col, :], (((1,), (1,)), ((), ())), preferred_element_type=f32)

    def input_rows(n):
        @pl.loop(3 * n, 3 * n + 3)
        def _(i):
            ats = [pl.ds(pl.multiple_of(i * 64 + 16 * u, 16), 16) for u in range(4)]
            gain = gains[0:1, :]
            invs = [inv_in[at, 0:1] for at in ats]
            normals = [(xe[at, :].astype(f32) - mean_in[at, 0:1]) * inv for at, inv in zip(ats, invs)]
            us = [work[at, :] * gain for at in ats]
            m1 = [row_mean(u) for u in us]
            m2 = [row_mean(u * n) for u, n in zip(us, normals)]
            for at, inv, u, n, a, b in zip(ats, invs, us, normals, m1, m2):
                out[at, :] = (ce[at, :].astype(f32) + inv * (u - a - n * b)).astype(bf)

    loads[0].wait()
    loads[1].wait()
    greeted(targets)
    go(give(3))
    for_sibling(0)
    go(give(0))
    for_sibling(1)
    go(give(1))
    loads[2].wait()
    give(3).wait_recv()

    @pl.loop(0, 4)
    def _(y):
        at = (y, slice(None), slice(None), slice(None), later)
        acc[at] = (acc[at].astype(f32) + sibbuf[at].astype(f32)).astype(bf)
    for p in SECOND:
        start_halves(p)
    for_sibling(2)
    go(give(2))
    for_own(0)
    for p in SECOND:
        pass_on(p)
    for_own(1)
    for_own(2)
    pass_on(0)
    for n in (3, 4):
        loads[n].wait()
    input_product(0)
    pass_on(1)
    pass_on(2)
    for p in SECOND:
        take(p, 0)
    input_product(1)
    take(0, 0)
    input_product(2)
    for p in SECOND:
        take(p, 1)
    take(1, 0)
    take(2, 0)
    input_product(3)
    for n in (5, 6, 7, 8):
        loads[n].wait()
    take(0, 1)
    for p in SECOND:
        take(p, 2)
    input_rows(0)
    take(1, 1)
    take(2, 1)
    input_rows(1)
    take(0, 2)
    input_rows(2)
    take(1, 2)
    take(2, 2)
    top, bottom = last[0:8, :], last[8:16, :]
    low[...] = jnp.where(core == 0, bottom, top)
    swap = pltpu.make_async_remote_copy(
        src_ref=low, dst_ref=fin, send_sem=e_sem.at[0], recv_sem=e_sem.at[1], device_id=sibling, device_id_type=MESH)
    swap.start()
    input_rows(3)
    mine = jnp.where(core == 0, top, bottom)
    swap.wait()
    theirs = fin[...]
    total = jnp.zeros((8, 1), f32)
    for c in (0, 1):
        own = jnp.where(core == c, mine, theirs)
        o_in[:, c * 1024 : c * 1024 + 1024] = own[:, :1024]
        o_out[:, c * 512 : c * 512 + 512] = own[:, 1152:1664]
        rows = w_rows[:, c * 1024 : c * 1024 + 1024].astype(f32)
        total = total + jnp.sum(rows * own[:, :1024], axis=-1, keepdims=True)
        if c == 0:
            rest = own[:, 1024:1152]
    eye = lax.broadcasted_iota(jnp.int32, (8, 8), 0) == lax.broadcasted_iota(jnp.int32, (8, 8), 1)
    column = jnp.sum(jnp.where(eye, jnp.broadcast_to(gain[0:1, :], (8, 8)), 0.0), axis=1, keepdims=True)
    o_kern[...] = rest[:, 0:31]
    pair = []
    for v in (total / column, rest[:, 32:33]):
        pair.append(jnp.sum(jnp.where(eye, jnp.broadcast_to(v, (8, 8)), 0.0), axis=0, keepdims=True))
    o_vec[...] = jnp.concatenate(pair, axis=0)
    for c in sends:
        c.wait_send()


def back(early, ln, dpre, w, frames, cot, inv, mean, gains, w_rows, gain):
    bf, f32 = jnp.bfloat16, jnp.float32
    vm = pl.BlockSpec(memory_space=pltpu.VMEM)
    hbm = pl.BlockSpec(memory_space=pltpu.HBM)
    V = pltpu.VMEM
    return pl.pallas_call(
        back_kernel,
        out_shape=(
            jax.ShapeDtypeStruct((8, 2048), f32),
            jax.ShapeDtypeStruct((8, 1024), f32),
            jax.ShapeDtypeStruct((8, 31), f32),
            jax.ShapeDtypeStruct((2, 8), f32),
            jax.ShapeDtypeStruct((768, 1024), bf),
        ),
        in_specs=[hbm] * 8 + [vm] * 3,
        out_specs=(vm, vm, vm, vm, vm),
        scratch_shapes=[
            V((4, 4, 4, 16, HALFW), bf),
            V((4, 4, 4, 16, HALFW), bf),
            V((4, 4, 4, 16, 1024), bf),
            V((4, 4, 16, HALFW), bf),
            V((2, 4, 4, 16, HALFW), bf),
            V((3, 4, 16, HALFW), bf),
            V((3, 16, HALFW), bf),
            V((16, HALFW), f32),
            V((8, HALFW), f32),
            V((8, HALFW), f32),
            V((768, 1024), bf),
            V((1024, 768), bf),
            V((768, 2048), bf),
            V((1024, 2048), bf),
            V((768, 1024), bf),
            V((768, 1024), bf),
            V((768, 128), f32),
            V((768, 128), f32),
            V((768, 1024), f32),
            pltpu.SemaphoreType.DMA((10,)),
            pltpu.SemaphoreType.DMA((4,)),
            pltpu.SemaphoreType.DMA((4,)),
            pltpu.SemaphoreType.DMA((6, 3, 5)),
            pltpu.SemaphoreType.DMA((6, 3, 5)),
            pltpu.SemaphoreType.DMA((2,)),
        ],
        compiler_params=pltpu.CompilerParams(
            collective_id=1, has_side_effects=True, vmem_limit_bytes=60 << 20),
        name="back_and_scatter",
    )(early, ln, dpre, w, frames, cot, inv, mean, gains, w_rows, gain)


EPS = 1e-05
HALF = 15
ROWS = 768
D = 1024
NFFT = 256


def tables():
    omega = 2 * np.pi * (np.arange(128) + 0.5) / NFFT
    phase = omega[:, None] * np.arange(NFFT)[None]
    basis = np.concatenate([np.cos(phase), -np.sin(phase)], axis=0)
    lag = omega[:, None] * (np.arange(31) - HALF)[None]
    spread = np.zeros((NFFT, 128))
    spread[:, :31] = np.concatenate([np.cos(lag), np.sin(lag)], axis=0) * (2 / NFFT)
    back = np.zeros((128, NFFT))
    back[:31] = np.concatenate([np.cos(lag), -np.sin(lag)], axis=0).T * (2 / NFFT)
    f32 = jnp.float32
    return (jnp.asarray(basis, f32), jnp.asarray(basis.T, f32), jnp.asarray(spread, f32), jnp.asarray(back, f32))


def sigmoid(v):
    return 0.5 * jnp.tanh(0.5 * v) + 0.5


NT = (((1,), (1,)), ((), ()))
TN = (((0,), (0,)), ((), ()))
F32 = jnp.float32
BF = jnp.bfloat16


def nt(a, b):
    return lax.dot_general(a, b, NT, preferred_element_type=F32)


def mm(a, b):
    return jnp.dot(a, b, preferred_element_type=F32)


def row_mean(v):
    return jnp.sum(v, axis=-1, keepdims=True) * (1.0 / D)


FWD_AT, BWD_AT = (0, 208, 416, 592), (16, 208, 400, 592)


def colours(ids, table, across, counts):
    lane = lax.broadcasted_iota(jnp.int32, (1, 128), 1)
    wide = lax.broadcasted_iota(jnp.int32, (1, NFFT), 1)
    for n, at in enumerate(FWD_AT + BWD_AT):
        length = 240 if n < 4 else 224
        r, o = divmod(at + 96, 128)

        def piece(k, o=o):
            if o == 0:
                return ids[k : k + 1, :]
            first = pltpu.roll(ids[k : k + 1, :], 128 - o, 1)
            return jnp.where(lane < 128 - o, first, pltpu.roll(ids[min(k + 1, 7) : min(k + 1, 7) + 1, :], 128 - o, 1))

        own = jnp.concatenate([piece(r), piece(r + 1)], axis=1)
        step = jnp.where(wide < length - HALF, pltpu.roll(own, NFFT - HALF, 1) - own, 0.0)
        count = jnp.max(step, axis=1, keepdims=True) + 1.0
        own = own + 1.0
        own = own - count * jnp.floor((own + 0.5) / count)
        own = jnp.where(wide < length, own, -1.0)
        rows = jnp.broadcast_to(own, (8, NFFT))
        table[n] = rows
        across[n] = jnp.broadcast_to(rows.T[:, 0:1], (NFFT, 128))
        if n >= 4:
            table[n + 4] = jnp.where((wide >= 16) & (wide < 208), rows, -1.0)
        counts[n : n + 1, :] = jnp.broadcast_to(count, (1, 128)).astype(jnp.int32)


def mid_kernel(
    counts, gains, basis, turned, back, frames, cot, hc, w_hbm, glu_hbm, sig_hbm, spec_hbm, table_hbm, across_hbm,
    out_hbm, dpre_hbm, early_hbm,
    xe, ce, w, glu, sig, mixed, work, act, dm, dpre, g, spec, prod, extra, table, across, out, sems,
):
    scale = 1.0 / math.sqrt(98304.0)

    def cp(src, dst, n):
        c = pltpu.make_async_copy(src, dst, sems.at[n])
        c.start()
        return c

    cols = lambda lo, n: (slice(None), pl.ds(lo, n))
    loads = [
        cp(table_hbm, table, 0),
        cp(across_hbm, across, 1),
        cp(spec_hbm, spec, 2),
        cp(glu_hbm, glu.at[pl.ds(0, 832)], 3),
        cp(cot, ce.at[pl.ds(16, ROWS)], 4),
        cp(hc.at[pl.ds(0, 16)], ce.at[pl.ds(0, 16)], 5),
        cp(hc.at[pl.ds(16, 16)], ce.at[pl.ds(784, 16)], 6),
        cp(w_hbm.at[cols(1152, 512)], w.at[cols(0, 512)], 7),
        cp(w_hbm.at[cols(2816, 512)], w.at[cols(512, 512)], 8),
        cp(frames, xe, 9),
        cp(sig_hbm, sig, 10),
    ]
    glu[pl.ds(832, 16), :] = jnp.zeros((16, D), BF)
    dm[pl.ds(800, 32), :] = jnp.zeros((32, D), BF)
    prod[...] = jnp.zeros((NFFT, D), F32)
    extra[...] = jnp.zeros((128, D), F32)
    stores = []
    for n in range(4):
        loads[n].wait()

    def strips(i, n, off=0):
        return [pl.ds(pl.multiple_of(i * (16 * n) + off + 16 * u, 16), 16) for u in range(n)]

    def picked(row, first, k):
        return jnp.concatenate(
            [jnp.where(table[row, 0:1, :] == (first + c).astype(F32), basis[...], 0.0) for c in range(k)],
            axis=0).astype(BF)

    def placed(row, first, k, lo, hi):
        own = across[row, lo:hi, :]
        own = jnp.concatenate([own, own], axis=1)
        return jnp.concatenate(
            [jnp.where(own == (first + c).astype(F32), turned[lo:hi, :], 0.0) for c in range(k)], axis=1).astype(BF)

    def staged(spectrum, filtered, put):
        x = [spectrum(0)]
        y = None
        for j in range(4):
            if j < 3:
                x.append(spectrum(j + 1))
            new = filtered(j, x[j])
            if y is not None:
                put(j - 1, y)
            y = new
        put(3, y)

    def forward(wi, first, k, add):
        base = pl.multiple_of(jnp.minimum(wi * 208, 592), 16)
        to = picked(wi, first, k)
        fro = placed(wi, first, k, 16, 224)

        def spectrum(j):
            return mm(to, glu[pl.ds(base, 256), j * 256 : j * 256 + 256])

        def filtered(j, x):
            col = slice(j * 256, j * 256 + 256)
            hr, hi = spec[:128, col], spec[128:, col]
            ys = []
            for c in range(k):
                xr, xi = x[256 * c : 256 * c + 128], x[256 * c + 128 : 256 * c + 256]
                ys += [(xr * hr - xi * hi).astype(BF), (xr * hi + xi * hr).astype(BF)]
            return jnp.concatenate(ys, axis=0)

        def put(j, y):
            col = slice(j * 256, j * 256 + 256)
            y = mm(fro, y)
            if add:
                mixed[pl.ds(base, 208), col] += y
            else:
                mixed[pl.ds(base, 208), col] = y

        staged(spectrum, filtered, put)

    def backward(wi, first, k, add):
        base = pl.multiple_of(wi * 192, 16)
        to = picked(4 + wi, first, k)
        mid_to = picked(8 + wi, first, k)
        fro = placed(4 + wi, first, k, 16, 208)

        def spectrum(j):
            col = slice(j * 256, j * 256 + 256)
            return mm(to, dm[pl.ds(base, 256), col]), mm(mid_to, glu[pl.ds(base + 16, 256), col])

        def filtered(j, pair):
            d, q = pair
            col = slice(j * 256, j * 256 + 256)
            hr, hi = spec[:128, col], spec[128:, col]
            ys = []
            pr, pi = prod[:128, col], prod[128:, col]
            for c in range(k):
                lo, mi, up = 256 * c, 256 * c + 128, 256 * c + 256
                dr, di, qr, qi = d[lo:mi], d[mi:up], q[lo:mi], q[mi:up]
                ys += [(dr * hr + di * hi).astype(BF), (di * hr - dr * hi).astype(BF)]
                pr = pr + (qr * dr + qi * di)
                pi = pi + (qi * dr - qr * di)
            prod[:128, col] = pr
            prod[128:, col] = pi
            return jnp.concatenate(ys, axis=0)

        def put(j, y):
            col = slice(j * 256, j * 256 + 256)
            y = mm(fro, y)
            if add:
                mixed[pl.ds(base, 192), col] += y
            else:
                mixed[pl.ds(base, 192), col] = y

        staged(spectrum, filtered, put)

    def by_class(run, wi, count):
        zero = jnp.int32(0)

        @pl.when(count <= 2)
        def _():
            run(wi, zero, 2, False)

        @pl.when(count == 3)
        def _():
            run(wi, zero, 3, False)

        @pl.when(count > 3)
        def _():
            run(wi, zero, 4, False)

            @pl.loop(0, (count - 3) // 2)
            def _(n):
                run(wi, 4 + n * 2, 2, True)

    @pl.loop(0, 4)
    def _(wi):
        by_class(forward, wi, counts[wi, 0])

    for n in range(4, 11):
        loads[n].wait()

    @pl.loop(0, 4)
    def _(j):
        col = pl.ds(pl.multiple_of(j * 256, 256), 256)
        work[:, col] = nt(ce[...], w[col, :])

    def mid_rows(ats, central):
        gain = gains[8:9, :]
        cens = [mixed[at, :] for at in ats]
        cens = [m - row_mean(m) for m in cens]
        invs = [lax.rsqrt(row_mean(c * c) + EPS) for c in cens]
        normals = [c * inv for c, inv in zip(cens, invs)]
        us = []
        for at, normal in zip(ats, normals):
            y = normal * gain
            s = sigmoid(y)
            ys = y * s
            act[at, :] = ys.astype(BF)
            d_ln = work[at, :] * (s + ys * (1.0 - s))
            if central:
                dn = d_ln * normal
                extra[40:48, :] += dn[:8] + dn[8:]
            us.append(d_ln * gain)
        m1 = [row_mean(u) for u in us]
        m2 = [row_mean(u * n) for u, n in zip(us, normals)]
        for at, inv, u, n, a, b in zip(ats, invs, us, normals, m1, m2):
            dm[at, :] = (inv * (u - a - n * b)).astype(BF)

    mid_rows([pl.ds(0, 16), pl.ds(784, 16)], False)

    @pl.loop(0, 12)
    def _(i):
        mid_rows(strips(i, 4, 16), True)

    @pl.loop(0, 4)
    def _(j):
        col = pl.ds(pl.multiple_of(j * 256, 256), 256)
        y = mm(act[16:784, :], w[:, col])
        out[:, col] = (xe[:, col].astype(F32) + y).astype(BF)
        lhs = act[16:784, col].T
        r = (mm(lhs, ce[16:784, :]) * scale).astype(BF)
        g[col, 128:640] = r[:, :512]
        g[col, 768:1280] = r[:, 512:]

    stores.append(cp(out, out_hbm, 11))

    @pl.loop(0, 4)
    def _(wi):
        by_class(backward, wi, counts[4 + wi, 0])

    gk = jnp.dot(back[...], prod[...], precision=lax.Precision.HIGHEST, preferred_element_type=F32)
    extra[0:31, :] = gk[0:31]
    g_mid = jnp.sum(extra[40:48, :], axis=0, keepdims=True)
    extra[32:33, :] = g_mid
    g[:, 0:128] = (extra[...].T * scale).astype(BF)
    g[:, 640:768] = jnp.zeros((D, 128), BF)
    stores.append(cp(g, early_hbm, 12))

    for q in range(4):
        @pl.loop(q * 6, q * 6 + 6)
        def _(i):
            for u in range(2):
                at = pl.ds(pl.multiple_of(i * 32 + 16 * u, 16), 16)
                ext = pl.ds(pl.multiple_of(i * 32 + 16 * u + 32, 16), 16)
                d = mixed[at, :]
                s = sig[at, :]
                dpre[at, :1024] = (d * s).astype(BF)
                dpre[at, 1024:] = (d * glu[ext, :].astype(F32) * (1.0 - s)).astype(BF)

        part = pl.ds(q * 192, 192)
        stores.append(cp(dpre.at[part], dpre_hbm.at[part], 13 + q))
    for s in stores:
        s.wait()


def mid(counts, gains, consts, *rest):
    vm = pl.BlockSpec(memory_space=pltpu.VMEM)
    hbm = pl.BlockSpec(memory_space=pltpu.HBM)
    V = pltpu.VMEM
    return pl.pallas_call(
        mid_kernel,
        out_shape=(
            jax.ShapeDtypeStruct((ROWS, D), BF),
            jax.ShapeDtypeStruct((ROWS, 2 * D), BF),
            jax.ShapeDtypeStruct((D, 1280), BF),
        ),
        in_specs=[pl.BlockSpec(memory_space=pltpu.SMEM), vm, vm, vm, vm] + [hbm] * 9,
        out_specs=(hbm,) * 3,
        scratch_shapes=[
            V((768, D), BF), V((800, D), BF), V((D, D), BF),
            V((848, D), BF), V((768, D), F32),
            V((800, D), F32), V((800, D), F32), V((800, D), BF), V((832, D), BF),
            V((768, 2 * D), BF), V((D, 1280), BF), V((NFFT, D), F32), V((NFFT, D), F32),
            V((128, D), F32), V((12, 8, NFFT), F32), V((8, NFFT, 128), F32), V((ROWS, D), BF),
            pltpu.SemaphoreType.DMA((17,)),
        ],
        compiler_params=pltpu.CompilerParams(vmem_limit_bytes=60 << 20),
        name="block_pass",
    )(counts, gains, *consts, *rest)


def shards(frames, cotangent, segments, w_in, w_out, kernel, gain_in, gain_mid):
    gain = jnp.stack([gain_in, gain_mid]).astype(F32)
    x, cot = frames[0], cotangent[0]
    basis, turned, spread, back_table = tables()
    full, c_halo, ln, glu, sig, inv, mean, gains, spec, table, across, counts = gather(
        w_in, w_out, kernel, gain, segments, spread, x, cot)
    full = full.reshape(D, WIDE)
    block_out, dpre, early = mid(
        counts, gains, (basis, turned, back_table), x, cot, c_halo, full, glu, sig, spec, table, across)
    g_in, g_out, g_kern, g_vec, input_grad = back(
        early.reshape(4, 4, 4, 16, 1280), ln, dpre, full, x, cot, inv, mean, gains, w_in, gain)
    return (block_out[None], input_grad[None], g_in, g_out, g_kern, g_vec[0], g_vec[1])


def solution(mesh):
    rows = P("dp", "seq", None)
    mat = P(("dp", "seq"), None)
    vec = P(("dp", "seq"))
    return jax.shard_map(
        shards, mesh=mesh, in_specs=(rows, rows, P("dp", "seq"), mat, mat, mat, vec, vec),
        out_specs=(rows, rows, mat, mat, mat, vec, vec), check_vma=False)
```
